512 devices in a mesh: img: 128 (over x, z, core), sub: 4 (over y).
Axes of the slice: x: 4, y: 4, z: 16, core: 2. Of those that a mesh axis runs over, the one named last changes fastest.
Arguments:
- descriptors: bfloat16 [1024, 256, 256], P('img', 'sub'), may hold values from -6 to 6
- counts: int32 [1024], P('img'), may hold values from 128 to 256, as said below
- visible: int32 [1024, 256], P('img', 'sub'), may hold values 0 or 1
- pair_list: int32 [4096, 2], P('img'), may hold values from 0 to 1023, as said below
- pair_count: int32 [128], P('img'), may hold values from 16 to 32, as said below
- w_attend: bfloat16 [256, 256], replicated, may hold values from -0.375 to 0.375
- w_value: bfloat16 [256, 256], replicated, may hold values from -0.375 to 0.375
- w_output: bfloat16 [256, 256], replicated, may hold values from -0.375 to 0.375
- w_hidden: bfloat16 [512, 512], replicated, may hold values from -0.25 to 0.25
- norm_gain: float32 [512], replicated, may hold values from 0.1 to 1.9
- w_down: bfloat16 [512, 256], replicated, may hold values from -0.25 to 0.25
- w_match: bfloat16 [256, 256], replicated, may hold values from -0.375 to 0.375
- unassigned_bucket: float32 [1], replicated, may hold values from 0.5 to 2
Outputs:
- updates: bfloat16 [1024, 256, 256], P('img', 'sub')
- masses: float32 [1024, 256], P('img', 'sub')
The draws below stay inside these ranges and needn't reach their ends.
Inputs may be any that keep to these rules, and one draw needn't show every extreme that they name: `counts`: multiples of 128; some image has all 256. `pair_list`: rows o * 32 to (o + 1) * 32 - 1 are owner o's slots; in every row image i is held by img index o and image j by img index (o + d) mod 128 for some d in -3 to 3 other than 0; no unordered pair of images appears twice among live rows; among one owner's live rows at most 6 have image j on one img index, reached in every draw. `pair_count`: some owner has all 32 slots live.
All inputs are finite; a program needn't handle non-finite values. No bound on the sum of `visible` on one device may be relied on, other than what follows from the above.
Results may differ from the reference program's by a relative error of at most 0.01.
Values may be sent and summed in bfloat16 or wider, within the bound.
A program may use at most 64 MiB of HBM per device.

```python
import math
import jax
import jax.numpy as jnp
from jax import lax

D = 256
HEADS = 4
KEYS = 256
PAD = 128
IMG_DEV = 8
PAIR_DEV = 32
WIN = 3
ITERS = 10
IMAGES = 1024
N_IMG = 128


def pair_tables(key):
    owners = N_IMG
    reach = 2 * WIN
    half_codes = IMG_DEV * IMG_DEV // 2
    halfway = IMG_DEV // 2
    subkeys = jax.random.split(key, 4)
    lowest = PAIR_DEV // 2
    highest = PAIR_DEV // 2 + PAIR_DEV // 8 + 1
    workload = jax.random.randint(subkeys[0], (owners,), lowest, highest)
    fullest = jax.random.randint(subkeys[1], (), 0, owners)
    workload = jnp.where(jnp.arange(owners) == fullest, PAIR_DEV, workload).astype(jnp.int32)
    column_ids = jnp.arange(reach)
    offsets = (column_ids // 2 + 1) * (1 - 2 * (column_ids % 2))
    affinity_matrix = jax.random.randint(subkeys[2], (owners, reach), 0, 2 ** 20) * reach + column_ids[None, :]
    ordering = jnp.argsort(affinity_matrix, axis=1, stable=True)
    slot_ids = jnp.arange(PAIR_DEV)
    owner_ids = jnp.arange(owners)[:, None]
    source = (owner_ids + owners + offsets[ordering[:, slot_ids % reach]]) % owners
    rank_ids = (slot_ids // reach)[None, :]
    base_codes = jax.random.randint(subkeys[3], (owners, owners), 0, half_codes)
    pair_code = (base_codes[owner_ids, source] + rank_ids) % half_codes
    first_local = pair_code // halfway
    parity = (owner_ids > source).astype(jnp.int32)
    second_local = 2 * (pair_code % halfway) + (first_local + parity) % 2
    first_img = owner_ids * IMG_DEV + first_local
    second_img = source * IMG_DEV + second_local
    listed = jnp.stack([first_img, second_img], axis=-1).reshape(owners * PAIR_DEV, 2)
    return (listed.astype(jnp.int32), workload)


def draw_pair_list(key, part):
    tables = pair_tables(key)
    return tables[0]


def draw_pair_count(key, part):
    tables = pair_tables(key)
    return tables[1]


def draw_counts(key, part):
    key = jax.random.fold_in(key, 5)
    subkeys = jax.random.split(key, 2)
    blocks = jax.random.randint(subkeys[0], (IMAGES,), 1, KEYS // PAD + 1) * PAD
    fullest = jax.random.randint(subkeys[1], (), 0, IMAGES)
    return jnp.where(jnp.arange(IMAGES) == fullest, KEYS, blocks).astype(jnp.int32)


def draw_descriptors(key, part):
    key = jax.random.fold_in(key, 3)
    subkeys = jax.random.split(key, 1)
    values = jnp.clip(jax.random.normal(subkeys[0], (IMAGES, KEYS, D), jnp.float32), -6.0, 6.0)
    return values.astype(jnp.bfloat16)


def with_ends(values, rng, smallest, high):
    dims = values.shape
    index_at = [jax.random.randint(jax.random.fold_in(rng, axis), (), 0, dims[axis]) for axis in range(len(dims))]
    values = values.at[tuple(index_at)].set(smallest)
    longest = dims.index(max(dims))
    index_at[longest] = (index_at[longest] + 1) % dims[longest]
    return values.at[tuple(index_at)].set(high)


def scatter_about(key, shape, scale, most, held_as=jnp.bfloat16):
    result = scale * jax.random.normal(key, shape, jnp.float32)
    return jnp.clip(result, min=-most, max=most).astype(held_as)


def setup_inputs(seed: int = 0) -> dict:
    splits = jax.random.split(jax.random.key(seed), 14)
    return {
        "descriptors": draw_descriptors(jax.random.fold_in(splits[13], 71), 0),
        "counts": draw_counts(jax.random.fold_in(splits[13], 71), 0),
        "visible": with_ends((jax.random.randint(splits[2], (IMAGES, KEYS), 0, 4) < 3).astype(jnp.int32), jax.random.fold_in(splits[2], 1), 0, 1),
        "pair_list": draw_pair_list(jax.random.fold_in(splits[13], 71), 0),
        "pair_count": draw_pair_count(jax.random.fold_in(splits[13], 71), 0),
        "w_attend": scatter_about(splits[5], (D, D), D ** -0.5, 0.375),
        "w_value": scatter_about(splits[6], (D, D), D ** -0.5, 0.375),
        "w_output": scatter_about(splits[7], (D, D), D ** -0.5, 0.375),
        "w_hidden": scatter_about(splits[8], (2 * D, 2 * D), (2 * D) ** -0.5, 0.25),
        "norm_gain": jnp.clip(1.0 + 0.18 * jax.random.normal(splits[9], (2 * D,), jnp.float32), 0.1, 1.9),
        "w_down": scatter_about(splits[10], (2 * D, D), (2 * D) ** -0.5, 0.25),
        "w_match": scatter_about(splits[11], (D, D), D ** -0.5, 0.375),
        "unassigned_bucket": jnp.clip(jax.random.uniform(splits[12], (1,), jnp.float32, 0.5, 2.0), 0.5, 2.0),
    }


MASKED = -1e+30
FORGET = 30.0

def project(features, weight):
    return jnp.dot(features, weight, preferred_element_type=jnp.float32).astype(jnp.bfloat16)

def split_heads(values):
    return values.reshape(values.shape[0], HEADS, -1).astype(jnp.float32)

def softmax_weights(similarity, kept, axis):
    masked = jnp.where(kept, similarity, MASKED)
    top_value = lax.optimization_barrier(jnp.max(masked, axis=axis, keepdims=True))
    raised = jnp.exp(masked - top_value)
    return (raised / lax.optimization_barrier(jnp.sum(raised, axis=axis, keepdims=True))).astype(jnp.bfloat16)

def refine(features, message, w_output, w_hidden, norm_gain, w_down):
    sent = project(message, w_output)
    joined = jnp.concatenate([features, sent], axis=-1)
    hidden = jnp.dot(joined, w_hidden, preferred_element_type=jnp.float32)
    average = lax.optimization_barrier(jnp.mean(hidden, axis=-1, keepdims=True))
    centred = hidden - average
    variance = lax.optimization_barrier(jnp.mean(centred * centred, axis=-1, keepdims=True))
    normed = centred * lax.rsqrt(variance + 1e-05) * norm_gain
    activated = jax.nn.gelu(normed, approximate=False).astype(jnp.bfloat16)
    return project(activated, w_down)

def entropic_transport_iterate(affinity_matrix, source_valid_indicator, target_valid_indicator, unassigned_bucket):
    count_rows = jnp.sum(source_valid_indicator)
    count_cols = jnp.sum(target_valid_indicator)
    total = count_rows + count_cols
    offset = -jnp.log(jnp.maximum(total, 1.0))
    bin_value = unassigned_bucket[0]
    side_column = jnp.zeros((affinity_matrix.shape[0], 1), jnp.float32) + bin_value
    bottom_row = jnp.zeros((1, affinity_matrix.shape[1] + 1), jnp.float32) + bin_value
    coupling = jnp.concatenate([jnp.concatenate([affinity_matrix, side_column], axis=1), bottom_row], axis=0)
    log_rows = jnp.concatenate([jnp.where(source_valid_indicator > 0, offset, offset - FORGET), jnp.reshape(jnp.log(jnp.maximum(count_cols, 1.0)) + offset, (1,))])
    log_cols = jnp.concatenate([jnp.where(target_valid_indicator > 0, offset, offset - FORGET), jnp.reshape(jnp.log(jnp.maximum(count_rows, 1.0)) + offset, (1,))])
    row_pot = jnp.zeros((coupling.shape[0],), jnp.float32)
    col_pot = jnp.zeros((coupling.shape[1],), jnp.float32)
    for sweep in range(ITERS):
        row_pot = log_rows - jax.nn.logsumexp(coupling + col_pot[None, :], axis=1)
        col_pot = log_cols - jax.nn.logsumexp(coupling + row_pot[:, None], axis=0)
    plan = jnp.exp(coupling[:-1, :-1] + row_pot[:-1, None] + col_pot[None, :-1])
    mass_rows = (lax.optimization_barrier(jnp.sum(plan, axis=1)) * total * source_valid_indicator).astype(jnp.bfloat16)
    mass_cols = (lax.optimization_barrier(jnp.sum(plan, axis=0)) * total * target_valid_indicator).astype(jnp.bfloat16)
    return (mass_rows, mass_cols)

def pair_work(own_feat, source_valid_entries, own_attend, own_value, other_feat, target_valid_entries, w_attend, w_value, w_output, w_hidden, norm_gain, w_down, w_match, unassigned_bucket):
    key_count, width = own_feat.shape
    head_size = width // HEADS
    other_attend = project(other_feat, w_attend)
    other_value = project(other_feat, w_value)
    similarity = jnp.einsum('khd,lhd->hkl', split_heads(own_attend), split_heads(other_attend)) / math.sqrt(head_size)
    to_other = softmax_weights(similarity, target_valid_entries[None, None, :] > 0, 2)
    to_own = softmax_weights(similarity, source_valid_entries[None, :, None] > 0, 1)
    own_message = jnp.einsum('hkl,lhd->khd', to_other.astype(jnp.float32), split_heads(other_value))
    own_message = own_message.reshape(key_count, width).astype(jnp.bfloat16)
    other_message = jnp.einsum('hkl,khd->lhd', to_own.astype(jnp.float32), split_heads(own_value))
    other_message = other_message.reshape(key_count, width).astype(jnp.bfloat16)
    own_delta = refine(own_feat, own_message, w_output, w_hidden, norm_gain, w_down)
    other_delta = refine(other_feat, other_message, w_output, w_hidden, norm_gain, w_down)
    own_new = (own_feat.astype(jnp.float32) + own_delta.astype(jnp.float32)).astype(jnp.bfloat16)
    other_new = (other_feat.astype(jnp.float32) + other_delta.astype(jnp.float32)).astype(jnp.bfloat16)
    own_match = project(own_new, w_match)
    other_match = project(other_new, w_match)
    affinity_matrix = jnp.dot(own_match, other_match.T, preferred_element_type=jnp.float32) / math.sqrt(width)
    source_marginal_weight, target_marginal_weight = entropic_transport_iterate(affinity_matrix, source_valid_entries, target_valid_entries, unassigned_bucket)
    return (own_delta, other_delta, source_marginal_weight, target_marginal_weight)

def reference(descriptors, counts, visible, pair_list, pair_count, w_attend, w_value, w_output, w_hidden, norm_gain, w_down, w_match, unassigned_bucket):
    positions = jnp.arange(KEYS, dtype=jnp.int32)
    keep_all = ((positions[None, :] < counts[:, None]) & (visible > 0)).astype(jnp.float32)

    def visit(carry, index):
        summed, massed = carry
        owner_id = index // PAIR_DEV
        alive = index - owner_id * PAIR_DEV < pair_count[owner_id]
        first_img = pair_list[index, 0]
        second_img = pair_list[index, 1]

        def compute(unused):
            own_feat = descriptors[first_img]
            other_feat = descriptors[second_img]
            outputs = pair_work(own_feat, keep_all[first_img], project(own_feat, w_attend), project(own_feat, w_value), other_feat, keep_all[second_img], w_attend, w_value, w_output, w_hidden, norm_gain, w_down, w_match, unassigned_bucket)
            return tuple((item.astype(jnp.float32) for item in outputs))

        def skip(unused):
            zero_rows = jnp.zeros((KEYS, D), jnp.float32)
            zero_mass = jnp.zeros((KEYS,), jnp.float32)
            return (zero_rows, zero_rows, zero_mass, zero_mass)
        own_delta, other_delta, source_marginal_weight, target_marginal_weight = lax.cond(alive, compute, skip, 0)
        summed = summed.at[first_img].add(own_delta).at[second_img].add(other_delta)
        massed = massed.at[first_img].add(source_marginal_weight).at[second_img].add(target_marginal_weight)
        return ((summed, massed), None)
    start = (jnp.zeros((IMAGES, KEYS, D), jnp.float32), jnp.zeros((IMAGES, KEYS), jnp.float32))
    (summed, massed), unused = lax.scan(visit, start, jnp.arange(N_IMG * PAIR_DEV, dtype=jnp.int32))
    return (summed.astype(jnp.bfloat16), massed)
```

```python
import math

import jax, jax.numpy as jnp
from jax import lax
from jax.experimental import pallas as pl
from jax.experimental.pallas import tpu as pltpu
from jax.sharding import PartitionSpec as P

BF=jnp.bfloat16; F32=jnp.float32
LOG2E=1.4426950408889634
HEADS=4; ITERS=10; K=256; D=256; SLAB=272; KEYS=256

def nn(a,b): return lax.dot_general(a,b,(((1,),(0,)),((),())),preferred_element_type=F32)
def nt(a,b): return lax.dot_general(a,b,(((1,),(1,)),((),())),preferred_element_type=F32)

def eye(n,dt=BF):
    return (lax.broadcasted_iota(jnp.int32,(n,n),0)==lax.broadcasted_iota(jnp.int32,(n,n),1)).astype(dt)

def to_col(row, id_ref):
    return nt(id_ref[...], jnp.broadcast_to(row,(128,row.shape[1])))

def prologue(wa,wv,wo,wh,gain,wd,wm, wvT,woT,whT,wdT,wmT,gcol,ident):
    ident[...]=eye(256)
    I=ident[...]
    wvT[...]=nt(I,wv[...]).astype(BF)
    woT[...]=nt(I,wo[...]).astype(BF)
    wmT[...]=nt(I,wm[...]).astype(BF)
    for a in range(2):
        for b in range(2):
            whT[a*256:a*256+256,b*256:b*256+256]=nt(I,wh[b*256:b*256+256,a*256:a*256+256]).astype(BF)
    for b in range(2):
        wdT[:,b*256:b*256+256]=nt(I,wd[b*256:b*256+256,:]).astype(BF)
    e=lax.broadcasted_iota(jnp.int32,(128,128),0)==lax.broadcasted_iota(jnp.int32,(128,128),1)
    for q in range(4):
        g=jnp.sum(jnp.where(e,jnp.broadcast_to(gain[:,q*128:q*128+128],(128,128)),0.0),axis=1,keepdims=True)
        gcol[q*128:q*128+128,:]=jnp.broadcast_to(g,(128,128))

def gelu(y):
    return 0.5*y*(1.0+lax.erf(y*math.sqrt(0.5)))

def attention(a_other, a_self, vT_other, bias):
    outs=[]
    ones=jnp.ones((16,K),BF)
    for h in range(HEADS):
        sl=slice(h*64,h*64+64)
        s=nt(a_other[:,sl],a_self[:,sl])*(LOG2E/8.0)+bias
        m=jnp.max(s,axis=0,keepdims=True)
        e=jnp.exp2(s-m).astype(BF)
        r=nn(jnp.concatenate([vT_other[sl,:],ones],axis=0),e)
        outs.append((r[:64]*(1.0/r[64:65])).astype(BF))
    return jnp.concatenate(outs,axis=0)

def refine(x, msgT, W):
    sentT=nn(W['woT'][...],msgT).astype(BF)
    hid=nt(W['whT'][:,:256],x)+nn(W['whT'][:,256:],sentT)
    mean=jnp.sum(hid,axis=0,keepdims=True)*(1.0/512)
    cen=hid-mean
    var=jnp.sum(cen*cen,axis=0,keepdims=True)*(1.0/512)
    g=W['gcol'][...]
    normed=cen*lax.rsqrt(var+1e-5)*jnp.concatenate([g,g],axis=1)
    act=gelu(normed).astype(BF)
    return nn(W['wdT'][...],act).astype(BF)

def phase_a(xi,ki,xj,kj,W):
    big=1e30
    bi=(to_col(ki,W['ident'])-1.0)*big; bi=jnp.concatenate([bi,bi],axis=1)
    bj=(to_col(kj,W['ident'])-1.0)*big; bj=jnp.concatenate([bj,bj],axis=1)
    ai=nn(xi,W['wa'][...]).astype(BF); aj=nn(xj,W['wa'][...]).astype(BF)
    viT=nt(W['wvT'][...],xi).astype(BF); vjT=nt(W['wvT'][...],xj).astype(BF)
    miT=attention(aj,ai,vjT,bj)
    mjT=attention(ai,aj,viT,bi)
    diT=refine(xi,miT,W); djT=refine(xj,mjT,W)
    I=W['ident'][...]
    riT=(nt(I,xi)+diT.astype(F32)).astype(BF)
    rjT=(nt(I,xj)+djT.astype(F32)).astype(BF)
    mi=nn(W['wmT'][...],riT).astype(BF); mj=nn(W['wmT'][...],rjT).astype(BF)
    mi=nt(I,mi).astype(BF)
    sc=nn(mi,mj)*(LOG2E/16.0)
    return diT,djT,sc

def marginals(ki,kj,W):
    ki32=ki.astype(F32); kj32=kj.astype(F32)
    m=jnp.sum(ki32,axis=1,keepdims=True); n=jnp.sum(kj32,axis=1,keepdims=True)
    tot=m+n
    off=-jnp.log2(jnp.maximum(tot,1.0))
    fg=30.0*LOG2E
    kic=to_col(ki,W['ident'])[:,:1]
    lr=off-fg*(1.0-kic)
    lc=off-fg*(1.0-kj32)
    lrb=jnp.log2(jnp.maximum(n,1.0))+off
    lcb=jnp.log2(jnp.maximum(m,1.0))+off
    return tot,kic,lr,lc,lrb,lcb

def sink_init(c_ref,p,binv,lr,lc,lrb,lcb):
    c=c_ref[p]
    mx=jnp.maximum(jnp.max(c,axis=1,keepdims=True),binv)
    s=jnp.sum(jnp.exp2(c-mx),axis=1,keepdims=True)+jnp.exp2(binv-mx)
    f=lr-mx-jnp.log2(s)
    fb=lrb-binv-math.log2(257.0)
    t=jnp.sum(jnp.exp2(c+f),axis=0,keepdims=True)+jnp.exp2(binv+fb)
    g=lc-jnp.log2(t)
    tb=jnp.sum(jnp.exp2(binv+f),axis=0,keepdims=True)+jnp.exp2(binv+fb)
    gb=lcb-jnp.log2(tb)
    return f,fb,g,gb

CH=256
def sink_iter(c_ref,p,binv,lr,lc,lrb,lcb,r,rb,st):
    f,fb,g,gb=st
    eb=jnp.exp2(binv+fb+g); ebb=jnp.exp2(binv+fb+gb)
    ub=rb/(jnp.sum(eb,axis=1,keepdims=True)+ebb)
    t=eb*ub
    tb=ebb*ub
    nf=[]
    for q in range(0,K,CH):
        fq=f[q:q+CH]
        pq=jnp.exp2(c_ref[p,q:q+CH,:]+g+fq)
        bq=jnp.exp2((binv+gb)+fq)
        s=jnp.sum(pq,axis=1,keepdims=True)+bq
        u=r[q:q+CH]/s
        nf.append(fq+jnp.log2(u))
        t=t+jnp.sum(pq*u,axis=0,keepdims=True)
        tb=tb+jnp.sum(bq*u,axis=0,keepdims=True)
    f=jnp.concatenate(nf,axis=0) if len(nf)>1 else nf[0]
    return f,fb+jnp.log2(ub),g+lc-jnp.log2(t),gb+lcb-jnp.log2(tb)

def sink_out(c_ref,p,tot,kic,kj32,st,W):
    f,fb,g,gb=st
    plan=jnp.exp2(c_ref[p]+f+g)
    mi=(jnp.sum(plan,axis=1,keepdims=True)*tot*kic).astype(BF)
    mj=(jnp.sum(plan,axis=0,keepdims=True)*tot*kj32).astype(BF)
    e0=(lax.broadcasted_iota(jnp.int32,(16,128),1)==0).astype(BF)
    mirow=nt(e0,jnp.broadcast_to(mi,(256,128)))[:1]
    return mirow, mj.astype(F32)

WIN = 3
REACH = 2 * WIN
PER = 2
SLOTS = REACH * PER
OWN = 8
ROWS = 64
SUBS = 4
MESH = pl.DeviceIdType.MESH


def step_of(turn):
    return (turn // 2 + 1) * (1 - 2 * (turn % 2))


def places():
    n = lax.axis_size("img")
    me = lax.axis_index("img")
    sub = lax.axis_index("sub")
    others = [lax.rem(me + step_of(t) + n, n) for t in range(REACH)]
    peers = [lax.rem(sub + d, SUBS) for d in range(1, SUBS)]
    return me, sub, others, peers


def greet(others, peers):
    barrier = pltpu.get_barrier_semaphore()
    for h in others:
        pl.semaphore_signal(barrier, inc=1, device_id={"img": h}, device_id_type=MESH)
    for s in peers:
        pl.semaphore_signal(barrier, inc=1, device_id={"sub": s}, device_id_type=MESH)
    pl.semaphore_wait(barrier, len(others) + len(peers))


def job_table(pairs, live_count, me, img_count):
    first = pairs[:, 0:1]
    second = pairs[:, 1:2]
    slots = pairs.shape[0]
    row_ids = lax.broadcasted_iota(jnp.int32, (slots, 1), 0)
    holder = second >> 3
    ahead = holder - me
    ahead = jnp.where(ahead < 0, ahead + img_count, ahead)
    turn = jnp.where(ahead <= WIN, 2 * (ahead - 1), 2 * (img_count - ahead - 1) + 1)
    live = row_ids < live_count
    key = jnp.where(live, turn, REACH)
    code = 1 + (first & 7) * 8 + (second & 7)
    up = lax.broadcasted_iota(jnp.int32, (slots, slots), 0)
    across = lax.broadcasted_iota(jnp.int32, (slots, slots), 1)
    key_row = jnp.sum(jnp.where(up == across, key, 0), axis=0, keepdims=True)
    below = (key_row < key).astype(jnp.int32)
    base = jnp.sum(below, axis=1, keepdims=True)
    rank = jnp.sum(((key_row == key) & (across < up)).astype(jnp.int32), axis=1, keepdims=True)
    place = base + rank
    lane_of = jnp.where(live, key * 8 + (place & 3) * 2 + (rank >> 2), -1)
    lanes = lax.broadcasted_iota(jnp.int32, (slots, 128), 1)
    row = jnp.sum(jnp.where(lanes == lane_of, code, 0), axis=0, keepdims=True)
    return jnp.broadcast_to(row, (8, 128))


def gather_kernel(
    desc, counts, visible, pairs, pair_count, full, tables, masks, table, send_sem, recv_sem, tsend, trecv
):
    me, sub, others, peers = places()
    rows = pl.ds(pl.multiple_of(sub * ROWS, ROWS), ROWS)
    full[:, rows, :] = desc[...]
    image = lax.broadcasted_iota(jnp.int32, (OWN, ROWS), 0)
    found = jnp.zeros((OWN, ROWS), jnp.int32)
    for a in range(OWN):
        found = jnp.where(image == a, counts[a], found)
    spot = lax.broadcasted_iota(jnp.int32, (OWN, ROWS), 1) + sub * ROWS
    kept = jnp.where((spot < found) & (visible[...] > 0), 1.0, 0.0)
    wide = jnp.concatenate([kept] * SUBS, axis=1)
    lane = lax.broadcasted_iota(jnp.int32, (OWN, KEYS), 1)
    wide = jnp.where((lane >= sub * ROWS) & (lane < sub * ROWS + ROWS), wide, 0.0)
    masks[0] = jnp.concatenate([wide, jnp.zeros_like(wide)], axis=0).astype(BF)
    greet(others, peers)
    copies = []
    for d in range(1, SUBS):
        to = {"sub": peers[d - 1]}
        copies.append(
            pltpu.make_async_remote_copy(
                src_ref=full.at[:, rows, :],
                dst_ref=full.at[:, rows, :],
                send_sem=send_sem.at[0, d - 1],
                recv_sem=recv_sem.at[0, d - 1],
                device_id=to,
                device_id_type=MESH,
            )
        )
        copies.append(
            pltpu.make_async_remote_copy(
                src_ref=masks.at[0],
                dst_ref=masks.at[d],
                send_sem=send_sem.at[1, d - 1],
                recv_sem=recv_sem.at[1, d - 1],
                device_id=to,
                device_id_type=MESH,
            )
        )
    for copy in copies:
        copy.start()
    mine = job_table(pairs[...], pair_count[0], me, lax.axis_size("img"))
    table[...] = mine
    tables[REACH] = mine
    tells = []
    for t in range(REACH):
        tells.append(
            pltpu.make_async_remote_copy(
                src_ref=table,
                dst_ref=tables.at[t ^ 1],
                send_sem=tsend.at[t],
                recv_sem=trecv.at[t ^ 1],
                device_id={"img": others[t]},
                device_id_type=MESH,
            )
        )
    for copy in tells:
        copy.start()
    for copy in tells:
        copy.wait_send()
    for t in range(REACH):
        tells[t].wait_recv()
    for copy in copies:
        copy.wait()
    whole = masks[0].astype(F32)
    for d in range(1, SUBS):
        whole = whole + masks[d].astype(F32)
    for a in range(OWN):
        full[a, KEYS:, :] = jnp.broadcast_to(whole[a : a + 1], (SLAB - KEYS, KEYS)).astype(BF)


def asked(tables, t, c, sub):
    return tables[t, 0, (t ^ 1) * 8 + sub * 2 + c]


def fetch_kernel(tables, full, landed, stage, send_sem, recv_sem):
    me, sub, others, peers = places()
    greet(others, [])
    copies = []
    for t in (4, 5, 2, 3, 0, 1):
        for c in range(PER):
            which = jnp.maximum(asked(tables, t, c, sub) - 1, 0) & 7
            stage[t, c] = full[which]
        copy = pltpu.make_async_remote_copy(
            src_ref=stage.at[t],
            dst_ref=landed.at[t ^ 1],
            send_sem=send_sem.at[t],
            recv_sem=recv_sem.at[t ^ 1],
            device_id={"img": others[t]},
            device_id_type=MESH,
        )
        copy.start()
        copies.append(copy)
    for copy in copies:
        copy.wait()


def give_kernel(tables, own, slots, upd, mass, back, total, parts, got, mparts, mgot, zsend, zrecv, ysend, yrecv):
    me, sub, others, peers = places()
    greet(others, peers)
    copies = []
    for t in (4, 5, 2, 3, 0, 1):
        copy = pltpu.make_async_remote_copy(
            src_ref=slots.at[t],
            dst_ref=back.at[t ^ 1],
            send_sem=zsend.at[t],
            recv_sem=zrecv.at[t ^ 1],
            device_id={"img": others[t]},
            device_id_type=MESH,
        )
        copy.start()
        copies.append(copy)
    for copy in copies:
        copy.wait()
    wants = []
    for t in range(REACH):
        for c in range(PER):
            code = asked(tables, t, c, sub)
            wants.append((t, c, jnp.where(code > 0, (code - 1) & 7, -1)))
    ident = eye(KEYS)
    for a in range(OWN):
        def add(r, _):
            at = pl.ds(pl.multiple_of(r * 64, 64), 64)
            value = own[a, at, :]
            for t, c, which in wants:
                value = value + back[t, c, at, :].astype(F32) * jnp.where(which == a, 1.0, 0.0)
            total[at, :] = value.astype(BF)
            return 0
        lax.fori_loop(0, 4, add, 0)
        turned = nt(ident, total[...]).astype(BF)
        for s in range(SUBS):
            parts[s, a] = turned[s * ROWS : s * ROWS + ROWS]
        value = own[a, KEYS : KEYS + 16, :]
        for t, c, which in wants:
            value = value + back[t, c, KEYS:, :].astype(F32) * jnp.where(which == a, 1.0, 0.0)
        mparts[a : a + 1, :] = value[:1]
    sends = []
    for d in range(1, SUBS):
        to = {"sub": peers[d - 1]}
        sends.append(
            pltpu.make_async_remote_copy(
                src_ref=parts.at[peers[d - 1]],
                dst_ref=got.at[d - 1],
                send_sem=ysend.at[0, d - 1],
                recv_sem=yrecv.at[0, d - 1],
                device_id=to,
                device_id_type=MESH,
            )
        )
        sends.append(
            pltpu.make_async_remote_copy(
                src_ref=mparts,
                dst_ref=mgot.at[d - 1],
                send_sem=ysend.at[1, d - 1],
                recv_sem=yrecv.at[1, d - 1],
                device_id=to,
                device_id_type=MESH,
            )
        )
    for copy in sends:
        copy.start()
    for copy in sends:
        copy.wait()
    for a in range(OWN):
        value = parts[sub, a].astype(F32)
        for d in range(SUBS - 1):
            value = value + got[d, a].astype(F32)
        upd[a] = value.astype(BF)
    value = mparts[...]
    for d in range(SUBS - 1):
        value = value + mgot[d]
    out = jnp.zeros((OWN, ROWS), F32)
    for s in range(SUBS):
        out = jnp.where(sub == s, value[:, s * ROWS : s * ROWS + ROWS], out)
    mass[...] = out


def work_kernel(tables, full, landed, binr, wa, wv, wo, wh, gain, wd, wm, own, slots, wvT, woT, whT, wdT, wmT, gcol, ident, sc, jobs):
    sub = lax.axis_index("sub")
    prologue(wa, wv, wo, wh, gain, wd, wm, wvT, woT, whT, wdT, wmT, gcol, ident)
    W = dict(wa=wa, wvT=wvT, woT=woT, whT=whT, wdT=wdT, wmT=wmT, gcol=gcol, ident=ident)
    binv = binr[...] * LOG2E
    own[...] = jnp.zeros_like(own)
    n = jnp.int32(0)
    for t in range(REACH):
        for c in range(PER):
            code = tables[REACH, 0, t * 8 + sub * 2 + c]
            jobs[0, n] = (code - 1) >> 3
            jobs[1, n] = t * PER + c
            n = n + jnp.where(code > 0, 1, 0)

            @pl.when(code == 0)
            def _():
                slots[t, c] = jnp.zeros((SLAB, KEYS), BF)
    jobs[0, n] = jobs[0, jnp.maximum(n - 1, 0)]
    jobs[1, n] = jobs[1, jnp.maximum(n - 1, 0)]
    @pl.loop(0, n)
    def _(p):
        a = jobs[0, p]
        z = jobs[1, p]
        tz, cz = z >> 1, z & 1
        di, dj, s = phase_a(full[a, :KEYS], full[a, KEYS : KEYS + 1], landed[tz, cz, :KEYS], landed[tz, cz, KEYS : KEYS + 1], W)
        own[a, :KEYS] = own[a, :KEYS] + di.astype(F32)
        slots[tz, cz, :KEYS] = dj
        sc[p] = s

    @pl.loop(0, (n + 1) >> 1)
    def _(q):
        P = [q * 2 + i for i in range(2)]
        A = [jobs[0, p] for p in P]
        Z = [(jobs[1, p] >> 1, jobs[1, p] & 1) for p in P]
        KI = [full[a, KEYS : KEYS + 1] for a in A]
        KJ = [landed[z[0], z[1], KEYS : KEYS + 1] for z in Z]
        M = [marginals(ki, kj, W) for ki, kj in zip(KI, KJ)]
        RR = [(jnp.exp2(m[2]), jnp.exp2(m[4])) for m in M]
        S = [jnp.minimum(p, n - 1) for p in P]
        st = [sink_init(sc, p, binv, *m[2:]) for p, m in zip(S, M)]
        def body(_, st):
            return [sink_iter(sc, p, binv, *m[2:], *r, s) for p, m, r, s in zip(S, M, RR, st)]
        st = lax.fori_loop(0, ITERS - 1, body, st)
        for i, (p, m, s) in enumerate(zip(S, M, st)):
            x, y = sink_out(sc, p, m[0], m[1], KJ[i].astype(F32), s, W)
            fresh = jnp.where(P[i] < n, 1.0, 0.0)
            own[A[i], KEYS:] = own[A[i], KEYS:] + jnp.broadcast_to(x * fresh, (SLAB - KEYS, KEYS))
            slots[Z[i][0], Z[i][1], KEYS:] = jnp.broadcast_to(y, (SLAB - KEYS, KEYS)).astype(BF)


VM = pl.BlockSpec(memory_space=pltpu.VMEM)
SM = pl.BlockSpec(memory_space=pltpu.SMEM)
DMA = pltpu.SemaphoreType.DMA
LIMIT = 56 * 2**20


def local(descriptors, counts, visible, pair_list, pair_count, w_attend, w_value, w_output, w_hidden, norm_gain, w_down, w_match, unassigned_bucket):
    V = pltpu.VMEM
    full, tables = pl.pallas_call(
        gather_kernel,
        out_shape=(jax.ShapeDtypeStruct((OWN, SLAB, D), BF), jax.ShapeDtypeStruct((REACH + 1, 8, 128), jnp.int32)),
        in_specs=[VM, SM, VM, VM, SM],
        out_specs=(VM, VM),
        scratch_shapes=[V((SUBS, 16, KEYS), BF), V((8, 128), jnp.int32), DMA((2, SUBS - 1)), DMA((2, SUBS - 1)), DMA((REACH,)), DMA((REACH,))],
        compiler_params=pltpu.CompilerParams(collective_id=0, has_side_effects=True, vmem_limit_bytes=LIMIT),
    )(descriptors, counts, visible, pair_list, pair_count)
    landed = pl.pallas_call(
        fetch_kernel,
        out_shape=jax.ShapeDtypeStruct((REACH, PER, SLAB, D), BF),
        in_specs=[SM, VM],
        out_specs=VM,
        scratch_shapes=[V((REACH, PER, SLAB, D), BF), DMA((REACH,)), DMA((REACH,))],
        compiler_params=pltpu.CompilerParams(collective_id=1, has_side_effects=True, vmem_limit_bytes=LIMIT),
    )(tables, full)
    own, slots = pl.pallas_call(
        work_kernel,
        out_shape=(jax.ShapeDtypeStruct((OWN, SLAB, D), F32), jax.ShapeDtypeStruct((REACH, PER, SLAB, D), BF)),
        in_specs=[SM] + [VM] * 10,
        out_specs=(VM, VM),
        scratch_shapes=[V((256, 256), BF), V((256, 256), BF), V((512, 512), BF), V((256, 512), BF), V((256, 256), BF), V((512, 128), F32), V((256, 256), BF), V((8, 256, 256), F32), pltpu.SMEM((2, 16), jnp.int32)],
        compiler_params=pltpu.CompilerParams(vmem_limit_bytes=LIMIT),
    )(tables, full, landed, unassigned_bucket.reshape(1, 1), w_attend, w_value, w_output, w_hidden, norm_gain.reshape(1, -1), w_down, w_match)
    return pl.pallas_call(
        give_kernel,
        out_shape=(jax.ShapeDtypeStruct((OWN, ROWS, D), BF), jax.ShapeDtypeStruct((OWN, ROWS), F32)),
        in_specs=[SM, VM, VM],
        out_specs=(VM, VM),
        scratch_shapes=[
            V((REACH, PER, SLAB, D), BF), V((KEYS, D), BF), V((SUBS, OWN, ROWS, D), BF), V((SUBS - 1, OWN, ROWS, D), BF),
            V((OWN, KEYS), F32), V((SUBS - 1, OWN, KEYS), F32),
            DMA((REACH,)), DMA((REACH,)), DMA((2, SUBS - 1)), DMA((2, SUBS - 1)),
        ],
        compiler_params=pltpu.CompilerParams(collective_id=2, has_side_effects=True, vmem_limit_bytes=LIMIT),
    )(tables, own, slots)


def solution(mesh):
    placed = (P("img", "sub", None), P("img"), P("img", "sub"), P("img", None), P("img")) + (P(),) * 8
    return jax.shard_map(local, mesh=mesh, in_specs=placed, out_specs=(P("img", "sub", None), P("img", "sub")), check_vma=False)
```

```python
import math

import jax
import jax.numpy as jnp
from jax import lax
from jax.experimental import pallas as pl
from jax.experimental.pallas import tpu as pltpu
from jax.sharding import PartitionSpec as P

BF = jnp.bfloat16
F32 = jnp.float32
I32 = jnp.int32
LOG2E = 1.4426950408889634
FORGET = 30.0 * LOG2E
HEADS = 4
ITERS = 10
KEYS = 256
D = 256
WIN = 3
REACH = 2 * WIN
MOST = 6
OWN = 8
ROWS = 64
SUBS = 4
JOBS = 8
MESH = pl.DeviceIdType.MESH
LIMIT = 56 * 2**20


def nn(a, b):
    return lax.dot_general(a, b, (((1,), (0,)), ((), ())), preferred_element_type=F32)


def nt(a, b):
    return lax.dot_general(a, b, (((1,), (1,)), ((), ())), preferred_element_type=F32)


def eye(n):
    up = lax.broadcasted_iota(I32, (n, n), 0)
    return (up == lax.broadcasted_iota(I32, (n, n), 1)).astype(BF)


def to_col(row, ident):
    return nt(ident, jnp.broadcast_to(row, (128, row.shape[1])))


def prepare(wv, wo, wh, gain, wd, wm, wvT, woT, whT, wdT, wmT, gcol):
    ident = eye(256)
    wvT[...] = nt(ident, wv[...]).astype(BF)
    woT[...] = nt(ident, wo[...]).astype(BF)
    wmT[...] = nt(ident, wm[...]).astype(BF)
    for a in range(0, 512, 256):
        for b in range(0, 512, 256):
            whT[a : a + 256, b : b + 256] = nt(ident, wh[b : b + 256, a : a + 256]).astype(BF)
    for b in range(0, 512, 256):
        wdT[:, b : b + 256] = nt(ident, wd[b : b + 256, :]).astype(BF)
    same = lax.broadcasted_iota(I32, (128, 128), 0) == lax.broadcasted_iota(I32, (128, 128), 1)
    for q in range(0, 512, 128):
        spread = jnp.broadcast_to(gain[:, q : q + 128], (128, 128))
        column = jnp.sum(jnp.where(same, spread, 0.0), axis=1, keepdims=True)
        gcol[q : q + 128, :] = jnp.broadcast_to(column, (128, 128))


def attention(a_other, a_self, vT_other, bias, ident):
    outs = []
    ones = jnp.ones((16, KEYS), BF)
    aT = nt(ident, a_self).astype(BF)
    for h in range(HEADS):
        sl = slice(h * 64, h * 64 + 64)
        s = nn(a_other[:, sl], aT[sl]) * (LOG2E / 8.0) + bias
        top = jnp.max(s, axis=0, keepdims=True)
        e = jnp.exp2(s - top).astype(BF)
        r = nn(jnp.concatenate([vT_other[sl, :], ones], axis=0), e)
        outs.append((r[:64] * (1.0 / r[64:65])).astype(BF))
    return jnp.concatenate(outs, axis=0)


def refine(x, msgT, w):
    outs = []
    gain = w["gcol"][...]
    sentT = nn(w["woT"][...], msgT).astype(BF)
    for c in range(0, KEYS, 128):
        hid = nt(w["whT"][:, :256], x[c : c + 128]) + nn(w["whT"][:, 256:], sentT[:, c : c + 128])
        mean = jnp.sum(hid, axis=0, keepdims=True) * (1.0 / 512)
        cen = hid - mean
        var = jnp.sum(cen * cen, axis=0, keepdims=True) * (1.0 / 512)
        normed = cen * lax.rsqrt(var + 1e-5) * gain
        outs.append((0.5 * normed * (1.0 + lax.erf(normed * math.sqrt(0.5)))).astype(BF))
    return nn(w["wdT"][...], jnp.concatenate(outs, axis=1)).astype(BF)


def pair_scores(xi, ki, xj, kj, w):
    ident = w["ident"][...]
    bi = (to_col(ki, ident) - 1.0) * 1e30
    bj = (to_col(kj, ident) - 1.0) * 1e30
    bi = jnp.concatenate([bi, bi], axis=1)
    bj = jnp.concatenate([bj, bj], axis=1)
    ai = nn(xi, w["wa"][...]).astype(BF)
    aj = nn(xj, w["wa"][...]).astype(BF)
    viT = nt(w["wvT"][...], xi).astype(BF)
    vjT = nt(w["wvT"][...], xj).astype(BF)
    diT = refine(xi, attention(aj, ai, vjT, bj, ident), w)
    djT = refine(xj, attention(ai, aj, viT, bi, ident), w)
    riT = (nt(ident, xi) + diT.astype(F32)).astype(BF)
    rjT = (nt(ident, xj) + djT.astype(F32)).astype(BF)
    mi = nn(w["wmT"][...], riT).astype(BF)
    mj = nn(w["wmT"][...], rjT).astype(BF)
    scores = nn(nt(ident, mi).astype(BF), mj) * (LOG2E / 16.0)
    return nt(ident, diT).astype(BF), nt(ident, djT).astype(BF), scores


def marginals(ki, kj, ident):
    m = jnp.sum(ki, axis=1, keepdims=True)
    n = jnp.sum(kj, axis=1, keepdims=True)
    total = m + n
    off = -jnp.log2(jnp.maximum(total, 1.0))
    kic = to_col(ki.astype(BF), ident)[:, :1]
    lr = off - FORGET * (1.0 - kic)
    lc = off - FORGET * (1.0 - kj)
    lrb = jnp.log2(jnp.maximum(n, 1.0)) + off
    lcb = jnp.log2(jnp.maximum(m, 1.0)) + off
    return total, kic, lr, lc, lrb, lcb


def sink_first(c, bucket, lr, lc, lrb, lcb):
    top = jnp.maximum(jnp.max(c, axis=1, keepdims=True), bucket)
    s = jnp.sum(jnp.exp2(c - top), axis=1, keepdims=True) + jnp.exp2(bucket - top)
    f = lr - top - jnp.log2(s)
    fb = lrb - bucket - math.log2(257.0)
    t = jnp.sum(jnp.exp2(c + f), axis=0, keepdims=True) + jnp.exp2(bucket + fb)
    tb = jnp.sum(jnp.exp2(bucket + f), axis=0, keepdims=True) + jnp.exp2(bucket + fb)
    return f, fb, lc - jnp.log2(t), lcb - jnp.log2(tb)


def sink_next(c, bucket, lr, lc, lrb, lcb, r, rb, state):
    f, fb, g, gb = state
    eb = jnp.exp2(bucket + fb + g)
    ebb = jnp.exp2(bucket + fb + gb)
    ub = rb / (jnp.sum(eb, axis=1, keepdims=True) + ebb)
    p = jnp.exp2(c + g + f)
    b = jnp.exp2((bucket + gb) + f)
    u = r / (jnp.sum(p, axis=1, keepdims=True) + b)
    t = eb * ub + jnp.sum(p * u, axis=0, keepdims=True)
    tb = ebb * ub + jnp.sum(b * u, axis=0, keepdims=True)
    return f + jnp.log2(u), fb + jnp.log2(ub), g + lc - jnp.log2(t), gb + lcb - jnp.log2(tb)


def sink_out(c, total, kic, kj, state):
    f, fb, g, gb = state
    plan = jnp.exp2(c + f + g)
    mi = (jnp.sum(plan, axis=1, keepdims=True) * total * kic).astype(BF)
    mj = (jnp.sum(plan, axis=0, keepdims=True) * total * kj).astype(BF)
    first = (lax.broadcasted_iota(I32, (16, 128), 1) == 0).astype(BF)
    return nt(first, jnp.broadcast_to(mi, (KEYS, 128)))[:1], mj.astype(F32)


def row_of(block, index):
    at = lax.broadcasted_iota(I32, block.shape, 0)
    return jnp.sum(jnp.where(at == index, block, 0.0), axis=0, keepdims=True)


def job_of(tab, q, sub):
    code = tab[0, q * SUBS + sub]
    return (code >> 8) & 7, (code >> 12) & 1


def do_scores(q, tab, sub, allx, okeep, jkeep, w, dmine, dother, sc):
    mine, swap = job_of(tab, q, sub)
    first = jnp.where(swap == 1, OWN + q, mine)
    second = jnp.where(swap == 1, mine, OWN + q)
    km = row_of(okeep[...], mine)
    ko = row_of(jkeep[...], q)
    ki = jnp.where(swap == 1, ko, km).astype(BF)
    kj = jnp.where(swap == 1, km, ko).astype(BF)
    di, dj, s = pair_scores(allx[first], ki, allx[second], kj, w)
    dmine[q] = jnp.where(swap == 1, dj, di)
    dother[q] = jnp.where(swap == 1, di, dj)
    sc[q] = s


def do_masses(jobs, tab, sub, okeep, jkeep, bucket, w, mm, mo, sc):
    ident = w["ident"][...]
    swaps, margs, states, kjs = [], [], [], []
    for q in jobs:
        mine, swap = job_of(tab, q, sub)
        km = row_of(okeep[...], mine)
        ko = row_of(jkeep[...], q)
        ki = jnp.where(swap == 1, ko, km)
        kj = jnp.where(swap == 1, km, ko)
        marg = marginals(ki, kj, ident)
        swaps.append(swap)
        kjs.append(kj)
        margs.append(marg)
        states.append(sink_first(sc[q], bucket, *marg[2:]))
    sums = [(jnp.exp2(m[2]), jnp.exp2(m[4])) for m in margs]

    def sweep(_, states):
        return [sink_next(sc[q], bucket, *m[2:], *r, s) for q, m, r, s in zip(jobs, margs, sums, states)]

    states = lax.fori_loop(0, ITERS - 1, sweep, states)
    for q, m, s, kj, swap in zip(jobs, margs, states, kjs, swaps):
        a, b = sink_out(sc[q], m[0], m[1], kj, s)
        mm[q] = jnp.broadcast_to(jnp.where(swap == 1, b, a), (8, KEYS))
        mo[q] = jnp.broadcast_to(jnp.where(swap == 1, a, b), (8, KEYS))


def step_of(turn):
    return (turn // 2 + 1) * (1 - 2 * (turn % 2))


def places():
    n = lax.axis_size("img")
    me = lax.axis_index("img")
    sub = lax.axis_index("sub")
    others = [lax.rem(me + step_of(t) + n, n) for t in range(REACH)]
    peers = [lax.rem(sub + d, SUBS) for d in range(1, SUBS)]
    return me, sub, others, peers


def greet(others, peers):
    barrier = pltpu.get_barrier_semaphore()
    for h in others:
        pl.semaphore_signal(barrier, inc=1, device_id={"img": h}, device_id_type=MESH)
    for s in peers:
        pl.semaphore_signal(barrier, inc=1, device_id={"sub": s}, device_id_type=MESH)
    pl.semaphore_wait(barrier, len(others) + len(peers))


def send(src, dst, ssem, rsem, to):
    return pltpu.make_async_remote_copy(
        src_ref=src, dst_ref=dst, send_sem=ssem, recv_sem=rsem, device_id=to, device_id_type=MESH
    )


def own_rows(pairs, live_count, me, img_count):
    first = pairs[:, 0:1]
    second = pairs[:, 1:2]
    slots = pairs.shape[0]
    row_ids = lax.broadcasted_iota(I32, (slots, 1), 0)
    ahead = (second >> 3) - me
    ahead = jnp.where(ahead < 0, ahead + img_count, ahead)
    turn = jnp.where(ahead <= WIN, 2 * (ahead - 1), 2 * (img_count - ahead - 1) + 1)
    live = row_ids < live_count
    key = jnp.where(live, turn, 15)
    code = 1 + (first & 7) * 8 + (second & 7)
    up = lax.broadcasted_iota(I32, (slots, slots), 0)
    across = lax.broadcasted_iota(I32, (slots, slots), 1)
    key_row = jnp.sum(jnp.where(up == across, key, 0), axis=0, keepdims=True)
    rank = jnp.sum(jnp.where((key_row == key) & (across < up), 1, 0), axis=1, keepdims=True)
    lanes = lax.broadcasted_iota(I32, (slots, 128), 1)
    lane = lax.broadcasted_iota(I32, (1, 128), 1)
    rows = []
    for k in (key, key ^ 1):
        at = jnp.where(live, k * 8 + rank, -1)
        codes = jnp.sum(jnp.where(lanes == at, code, 0), axis=0, keepdims=True)
        counts = jnp.sum(jnp.where((lanes == 64 + k) & live, 1, 0), axis=0, keepdims=True)
        row = codes + counts
        rows.append(jnp.where((lane >= 80) & (lane < 88), live_count, row))
    return rows


def plan_rows(own, near, live_count):
    r8 = lax.broadcasted_iota(I32, (8, 128), 0)
    l8 = lax.broadcasted_iota(I32, (8, 128), 1)
    mine = jnp.where(l8 < 64, l8 >> 3, l8 & 7)
    from_near = jnp.sum(jnp.where((mine == r8) & (r8 < REACH), near, 0), axis=0, keepdims=True)
    slots = 64
    lanes = lax.broadcasted_iota(I32, (slots, 128), 1)
    slot = lax.broadcasted_iota(I32, (slots, 1), 0)
    turn = slot >> 3
    u = slot & 7
    own_all = jnp.broadcast_to(own, (slots, 128))
    near_all = jnp.broadcast_to(from_near, (slots, 128))

    def pick(table, lane):
        return jnp.sum(jnp.where(lanes == lane, table, 0), axis=1, keepdims=True)

    n_own = pick(own_all, 64 + turn)
    n_near = pick(near_all, 64 + turn)
    l_near = pick(near_all, 80 + turn)

    def sixth(value):
        return (jnp.maximum(value, 0) * 43) >> 8

    give = jnp.maximum(jnp.minimum(jnp.minimum(sixth(live_count - l_near), n_own), MOST - n_near), 0)
    take = jnp.maximum(jnp.minimum(jnp.minimum(sixth(l_near - live_count), n_near), MOST - n_own), 0)
    kept = n_own - give
    near_kept = n_near - take
    own_code = pick(own_all, turn * 8 + u) - 1
    near_code = pick(near_all, turn * 8 + u) - 1
    taken_code = pick(near_all, turn * 8 + near_kept + u - kept) - 1
    given_code = pick(own_all, turn * 8 + kept + u - near_kept) - 1
    live = (u < kept + take) & (turn < REACH)
    image = jnp.where(u < kept, own_code >> 3, taken_code & 7)
    swap = jnp.where(u < kept, 0, 1)
    asked = (u < near_kept + give) & (turn < REACH)
    sends = jnp.where(u < near_kept, near_code & 7, given_code >> 3)
    eye64 = lax.broadcasted_iota(I32, (slots, slots), 0) == lax.broadcasted_iota(I32, (slots, slots), 1)
    live_row = jnp.sum(jnp.where(eye64, jnp.where(live, 1, 0), 0), axis=0, keepdims=True)
    short = lax.broadcasted_iota(I32, (slots, slots), 1)
    place = jnp.sum(jnp.where(short < slot, live_row, 0), axis=1, keepdims=True)
    count = jnp.sum(live_row, axis=1, keepdims=True)

    def put(lane, value):
        return jnp.sum(jnp.where(lanes == lane, value, 0), axis=0, keepdims=True)

    by_place = put(jnp.where(live, place, -1), 1 + slot + image * 256 + swap * 4096)
    by_slot = put(slot, jnp.where(asked, 1 + sends, 0))
    places_row = put(slot, jnp.where(live, place, 0))
    row = lax.broadcasted_iota(I32, (8, 128), 0)
    out = jnp.where(row == 0, by_place, jnp.where(row == 1, by_slot, jnp.where(row == 2, places_row, count)))
    return out


def meet_kernel(pairs, pair_count, wv, wo, wh, gain, wd, wm, tab, wvT, woT, whT, wdT, wmT, gcol, told, near, ssem, rsem):
    me, sub, others, peers = places()
    own, out = own_rows(pairs[...], pair_count[0], me, lax.axis_size("img"))
    told[...] = jnp.broadcast_to(out, (8, 128))
    greet(others, [])
    copies = [send(told, near.at[t ^ 1], ssem.at[t], rsem.at[t ^ 1], {"img": others[t]}) for t in range(REACH)]
    for copy in copies:
        copy.start()
    prepare(wv, wo, wh, gain, wd, wm, wvT, woT, whT, wdT, wmT, gcol)
    for copy in copies:
        copy.wait()
    row = lax.broadcasted_iota(I32, (8, 128), 0)
    table = jnp.zeros((8, 128), I32)
    for t in range(REACH):
        table = jnp.where(row == t, near[t], table)
    tab[...] = plan_rows(own, table, pair_count[0])


def sent_image(tab, t, u):
    return tab[1, t * 8 + u]


def fetch_kernel(tab, desc, counts, visible, allx, okeep, jkeep, zst, zland, zms, zml, yst, yms, yml, omask, zsem, zrem, ysem, yrem, osem, orem):
    me, sub, others, peers = places()
    rows = pl.ds(pl.multiple_of(sub * ROWS, ROWS), ROWS)
    for a in range(OWN):
        allx[a, rows, :] = desc[a]
    image = lax.broadcasted_iota(I32, (OWN, ROWS), 0)
    found = jnp.zeros((OWN, ROWS), I32)
    for a in range(OWN):
        found = jnp.where(image == a, counts[a], found)
    spot = lax.broadcasted_iota(I32, (OWN, ROWS), 1) + sub * ROWS
    kept = jnp.where((spot < found) & (visible[...] > 0), 1.0, 0.0)
    wide = jnp.concatenate([kept] * SUBS, axis=1)
    lane = lax.broadcasted_iota(I32, (OWN, KEYS), 1)
    wide = jnp.where((lane >= sub * ROWS) & (lane < sub * ROWS + ROWS), wide, 0.0)
    omask[0] = wide
    greet(others, peers)
    zcopies = []
    for t in (4, 5, 2, 3, 0, 1):
        line = lax.broadcasted_iota(I32, (8, KEYS), 0)
        masks = jnp.zeros((8, KEYS), F32)
        for u in range(MOST):
            which = jnp.maximum(sent_image(tab, t, u) - 1, 0)
            zst[t, u] = desc[which]
            masks = jnp.where(line == u, row_of(wide, which), masks)
        zms[t] = masks
        to = {"img": others[t]}
        zcopies.append(send(zst.at[t], zland.at[t ^ 1], zsem.at[0, t], zrem.at[0, t ^ 1], to))
        zcopies.append(send(zms.at[t], zml.at[t ^ 1], zsem.at[1, t], zrem.at[1, t ^ 1], to))
        zcopies[-2].start()
        zcopies[-1].start()
    ocopies = []
    for d in range(1, SUBS):
        to = {"sub": peers[d - 1]}
        mine = allx.at[0:OWN, rows, :]
        ocopies.append(send(mine, mine, osem.at[0, d - 1], orem.at[0, d - 1], to))
        ocopies.append(send(omask.at[0], omask.at[d], osem.at[1, d - 1], orem.at[1, d - 1], to))
    for copy in ocopies:
        copy.start()
    for copy in zcopies:
        copy.wait()
    ycopies = []
    line = lax.broadcasted_iota(I32, (JOBS, KEYS), 0)
    zmasks = jnp.concatenate([zml[t] for t in range(REACH)], axis=0)
    for q in range(JOBS):
        for d in range(SUBS):
            worker = sub if d == 0 else peers[d - 1]
            slot = jnp.maximum((tab[0, q * SUBS + worker] & 255) - 1, 0)
            t, u = slot >> 3, slot & 7
            masks = jnp.where(line == q, row_of(zmasks, slot), 0.0 if q == 0 else yms[d])
            yms[d] = masks
            if d == 0:
                allx[OWN + q, rows, :] = zland[t, u]
            else:
                yst[d - 1, q] = zland[t, u]
                copy = send(
                    yst.at[d - 1, q],
                    allx.at[OWN + q, rows, :],
                    ysem.at[q, d - 1],
                    yrem.at[q, d - 1],
                    {"sub": worker},
                )
                copy.start()
                ycopies.append(copy)
    for d in range(1, SUBS):
        copy = send(yms.at[d], yml.at[d - 1], ysem.at[JOBS, d - 1], yrem.at[JOBS, d - 1], {"sub": peers[d - 1]})
        copy.start()
        ycopies.append(copy)
    for copy in ocopies:
        copy.wait()
    okeep[...] = omask[0] + omask[1] + omask[2] + omask[3]
    for copy in ycopies:
        copy.wait()
    jkeep[...] = yms[0] + yml[0] + yml[1] + yml[2]


def work_kernel(tab, allx, okeep, jkeep, bucket, wa, wvT, woT, whT, wdT, wmT, gcol, dmine, dother, mm, mo, ident, sc):
    sub = lax.axis_index("sub")
    ident[...] = eye(256)
    w = dict(wa=wa, wvT=wvT, woT=woT, whT=whT, wdT=wdT, wmT=wmT, gcol=gcol, ident=ident)
    n = (tab[3, 0] + (SUBS - 1) - sub) >> 2
    binv = bucket[...] * LOG2E

    @pl.loop(0, n)
    def _(q):
        do_scores(q, tab, sub, allx, okeep, jkeep, w, dmine, dother, sc)

    @pl.loop(0, n >> 1)
    def _(p):
        do_masses([2 * p, 2 * p + 1], tab, sub, okeep, jkeep, binv, w, mm, mo, sc)

    @pl.when((n & 1) == 1)
    def _():
        do_masses([n - 1], tab, sub, okeep, jkeep, binv, w, mm, mo, sc)


def give_kernel(tab, dmine, dother, mm, mo, upd, mass, yb, ymst, yml, zst, zms, zret, zmr, parts, got, mparts, mgot, ysem, yrem, zsem, zrem, osem, orem):
    me, sub, others, peers = places()
    rows = pl.ds(pl.multiple_of(sub * ROWS, ROWS), ROWS)
    mline = lax.broadcasted_iota(I32, (JOBS, KEYS), 0)
    masks = jnp.zeros((JOBS, KEYS), F32)
    for q in range(JOBS):
        masks = jnp.where(mline == q, mo[q], masks)
    ymst[...] = masks
    greet(others, peers)
    ycopies = []
    for q in range(JOBS):
        for d in range(1, SUBS):
            p = peers[d - 1]
            part = dother.at[q, pl.ds(pl.multiple_of(p * ROWS, ROWS), ROWS), :]
            ycopies.append(send(part, yb.at[q, sub], ysem.at[q, d - 1], yrem.at[q, d - 1], {"sub": p}))
    for d in range(1, SUBS):
        ycopies.append(send(ymst, yml.at[sub], ysem.at[JOBS, d - 1], yrem.at[JOBS, d - 1], {"sub": peers[d - 1]}))
    for copy in ycopies:
        copy.start()
    for q in range(JOBS):
        yb[q, sub] = dother[q, rows, :]
    yml[sub] = masks
    for copy in ycopies:
        copy.wait()
    ymasses = jnp.concatenate([yml[s] for s in range(SUBS)], axis=0)
    zcopies = [None] * REACH
    for t in (4, 5, 2, 3, 0, 1):
        line = lax.broadcasted_iota(I32, (8, KEYS), 0)
        back = jnp.zeros((8, KEYS), F32)
        for u in range(MOST):
            place = tab[2, t * 8 + u]
            zst[t, u] = yb[place >> 2, place & 3]
            back = jnp.where(line == u, row_of(ymasses, (place & 3) * JOBS + (place >> 2)), back)
        zms[t] = back
        to = {"img": others[t]}
        zcopies[t] = [
            send(zst.at[t], zret.at[t ^ 1], zsem.at[0, t], zrem.at[0, t ^ 1], to),
            send(zms.at[t], zmr.at[t ^ 1], zsem.at[1, t], zrem.at[1, t ^ 1], to),
        ]
        for copy in zcopies[t]:
            copy.start()
    n = (tab[3, 0] + (SUBS - 1) - sub) >> 2
    owners = [jnp.where(q < n, job_of(tab, q, sub)[0], -1) for q in range(JOBS)]
    for a in range(OWN):
        for s in range(SUBS):
            value = jnp.zeros((ROWS, D), F32)
            for q in range(JOBS):
                value = value + jnp.where(owners[q] == a, dmine[q, s * ROWS : s * ROWS + ROWS, :].astype(F32), 0.0)
            parts[s, a] = value.astype(BF)
        value = jnp.zeros((1, KEYS), F32)
        for q in range(JOBS):
            value = value + jnp.where(owners[q] == a, mm[q, 0:1, :], 0.0)
        mparts[a : a + 1, :] = value
    ocopies = []
    for d in range(1, SUBS):
        to = {"sub": peers[d - 1]}
        ocopies.append(send(parts.at[peers[d - 1]], got.at[d - 1], osem.at[0, d - 1], orem.at[0, d - 1], to))
        ocopies.append(send(mparts, mgot.at[d - 1], osem.at[1, d - 1], orem.at[1, d - 1], to))
    for copy in ocopies:
        copy.start()
    for copy in ocopies:
        copy.wait()
    for t in range(REACH):
        for copy in zcopies[t]:
            copy.wait()
    masses = mparts[...] + mgot[0] + mgot[1] + mgot[2]
    wants = [(t, u, sent_image(tab, t, u) - 1) for t in range(REACH) for u in range(MOST)]
    for a in range(OWN):
        value = parts[sub, a].astype(F32)
        for d in range(SUBS - 1):
            value = value + got[d, a].astype(F32)
        extra = jnp.zeros((1, KEYS), F32)
        for t, u, which in wants:
            value = value + jnp.where(which == a, zret[t, u].astype(F32), 0.0)
            extra = extra + jnp.where(which == a, zmr[t, u : u + 1, :], 0.0)
        upd[a] = value.astype(BF)
        masses = masses + jnp.where(mline == a, extra, 0.0)
    out = jnp.zeros((OWN, ROWS), F32)
    for s in range(SUBS):
        out = jnp.where(sub == s, masses[:, s * ROWS : s * ROWS + ROWS], out)
    mass[...] = out


VM = pl.BlockSpec(memory_space=pltpu.VMEM)
SM = pl.BlockSpec(memory_space=pltpu.SMEM)
DMA = pltpu.SemaphoreType.DMA


def shape(dims, kind=BF):
    return jax.ShapeDtypeStruct(dims, kind)


def talk(number):
    return pltpu.CompilerParams(collective_id=number, has_side_effects=True, vmem_limit_bytes=LIMIT)


def local(descriptors, counts, visible, pair_list, pair_count, w_attend, w_value, w_output, w_hidden, norm_gain, w_down, w_match, unassigned_bucket):
    V = pltpu.VMEM
    tab, *ready = pl.pallas_call(
        meet_kernel,
        out_shape=(shape((8, 128), I32), shape((256, 256)), shape((256, 256)), shape((512, 512)), shape((256, 512)), shape((256, 256)), shape((512, 128), F32)),
        in_specs=[VM, SM] + [VM] * 6,
        out_specs=(VM,) * 7,
        scratch_shapes=[V((8, 128), I32), V((REACH, 8, 128), I32), DMA((REACH,)), DMA((REACH,))],
        compiler_params=talk(0),
    )(pair_list, pair_count, w_value, w_output, w_hidden, norm_gain.reshape(1, -1), w_down, w_match)
    allx, okeep, jkeep = pl.pallas_call(
        fetch_kernel,
        out_shape=(shape((OWN + JOBS, KEYS, D)), shape((OWN, KEYS), F32), shape((JOBS, KEYS), F32)),
        in_specs=[SM, VM, SM, VM],
        out_specs=(VM,) * 3,
        scratch_shapes=[
            V((REACH, MOST, ROWS, D), BF), V((REACH, MOST, ROWS, D), BF), V((REACH, 8, KEYS), F32), V((REACH, 8, KEYS), F32),
            V((SUBS - 1, JOBS, ROWS, D), BF), V((SUBS, JOBS, KEYS), F32), V((SUBS - 1, JOBS, KEYS), F32), V((SUBS, OWN, KEYS), F32),
            DMA((2, REACH)), DMA((2, REACH)), DMA((JOBS + 1, SUBS - 1)), DMA((JOBS + 1, SUBS - 1)), DMA((2, SUBS - 1)), DMA((2, SUBS - 1)),
        ],
        compiler_params=talk(1),
    )(tab, descriptors, counts, visible)
    done = pl.pallas_call(
        work_kernel,
        out_shape=(shape((JOBS, KEYS, D)), shape((JOBS, KEYS, D)), shape((JOBS, 8, KEYS), F32), shape((JOBS, 8, KEYS), F32)),
        in_specs=[SM] + [VM] * 11,
        out_specs=(VM,) * 4,
        scratch_shapes=[V((256, 256), BF), V((JOBS, KEYS, KEYS), F32)],
        compiler_params=pltpu.CompilerParams(vmem_limit_bytes=LIMIT),
    )(tab, allx, okeep, jkeep, unassigned_bucket.reshape(1, 1), w_attend, *ready)
    return pl.pallas_call(
        give_kernel,
        out_shape=(shape((OWN, ROWS, D)), shape((OWN, ROWS), F32)),
        in_specs=[SM] + [VM] * 4,
        out_specs=(VM, VM),
        scratch_shapes=[
            V((JOBS, SUBS, ROWS, D), BF), V((JOBS, KEYS), F32), V((SUBS, JOBS, KEYS), F32),
            V((REACH, MOST, ROWS, D), BF), V((REACH, 8, KEYS), F32), V((REACH, MOST, ROWS, D), BF), V((REACH, 8, KEYS), F32),
            V((SUBS, OWN, ROWS, D), BF), V((SUBS - 1, OWN, ROWS, D), BF), V((OWN, KEYS), F32), V((SUBS - 1, OWN, KEYS), F32),
            DMA((JOBS + 1, SUBS - 1)), DMA((JOBS + 1, SUBS - 1)), DMA((2, REACH)), DMA((2, REACH)), DMA((2, SUBS - 1)), DMA((2, SUBS - 1)),
        ],
        compiler_params=talk(2),
    )(tab, *done)


def solution(mesh):
    placed = (P("img", "sub", None), P("img"), P("img", "sub"), P("img", None), P("img")) + (P(),) * 8
    return jax.shard_map(
        local, mesh=mesh, in_specs=placed, out_specs=(P("img", "sub", None), P("img", "sub")), check_vma=False
    )
```

```python
import math

import jax
import jax.numpy as jnp
from jax import lax
from jax.experimental import pallas as pl
from jax.experimental.pallas import tpu as pltpu
from jax.sharding import PartitionSpec as P

BF = jnp.bfloat16
F32 = jnp.float32
I32 = jnp.int32
LOG2E = 1.4426950408889634
FORGET = 30.0 * LOG2E
HEADS = 4
ITERS = 10
KEYS = 256
D = 256
WIN = 3
REACH = 2 * WIN
MOST = 6
OWN = 8
ROWS = 64
SUBS = 4
JOBS = 8
FIXED = 4
EARLY = 2
MESH = pl.DeviceIdType.MESH
LIMIT = 56 * 2**20


def nn(a, b):
    return lax.dot_general(a, b, (((1,), (0,)), ((), ())), preferred_element_type=F32)


def nt(a, b):
    return lax.dot_general(a, b, (((1,), (1,)), ((), ())), preferred_element_type=F32)


def eye(n):
    up = lax.broadcasted_iota(I32, (n, n), 0)
    return (up == lax.broadcasted_iota(I32, (n, n), 1)).astype(BF)


def to_col(row, ident):
    return nt(ident, jnp.broadcast_to(row, (128, row.shape[1])))


def prepare(wv, wo, wh, gain, wd, wm, wvT, woT, whT, wdT, wmT, gcol):
    ident = eye(256)
    wvT[...] = nt(ident, wv[...]).astype(BF)
    woT[...] = nt(ident, wo[...]).astype(BF)
    wmT[...] = nt(ident, wm[...]).astype(BF)
    for a in range(0, 512, 256):
        for b in range(0, 512, 256):
            whT[a : a + 256, b : b + 256] = nt(ident, wh[b : b + 256, a : a + 256]).astype(BF)
    for b in range(0, 512, 256):
        wdT[:, b : b + 256] = nt(ident, wd[b : b + 256, :]).astype(BF)
    same = lax.broadcasted_iota(I32, (128, 128), 0) == lax.broadcasted_iota(I32, (128, 128), 1)
    for q in range(0, 512, 128):
        spread = jnp.broadcast_to(gain[:, q : q + 128], (128, 128))
        column = jnp.sum(jnp.where(same, spread, 0.0), axis=1, keepdims=True)
        gcol[q : q + 128, :] = jnp.broadcast_to(column, (128, 128))


def attention(a_other, a_self, vT_other, bias, ident):
    outs = []
    ones = jnp.ones((16, KEYS), BF)
    aT = nt(ident, a_self).astype(BF)
    for h in range(HEADS):
        sl = slice(h * 64, h * 64 + 64)
        s = nn(a_other[:, sl], aT[sl]) * (LOG2E / 8.0) + bias
        top = jnp.max(s, axis=0, keepdims=True)
        e = jnp.exp2(s - top).astype(BF)
        r = nn(jnp.concatenate([vT_other[sl, :], ones], axis=0), e)
        outs.append((r[:64] * (1.0 / r[64:65])).astype(BF))
    return jnp.concatenate(outs, axis=0)


def refine(x, msgT, w):
    outs = []
    gain = w["gcol"][...]
    sentT = nn(w["woT"][...], msgT).astype(BF)
    for c in range(0, KEYS, 128):
        hid = nt(w["whT"][:, :256], x[c : c + 128]) + nn(w["whT"][:, 256:], sentT[:, c : c + 128])
        mean = jnp.sum(hid, axis=0, keepdims=True) * (1.0 / 512)
        cen = hid - mean
        var = jnp.sum(cen * cen, axis=0, keepdims=True) * (1.0 / 512)
        normed = cen * lax.rsqrt(var + 1e-5) * gain
        outs.append((0.5 * normed * (1.0 + lax.erf(normed * math.sqrt(0.5)))).astype(BF))
    return nn(w["wdT"][...], jnp.concatenate(outs, axis=1)).astype(BF)


def pair_scores(xi, ki, xj, kj, w):
    ident = w["ident"][...]
    bi = (to_col(ki, ident) - 1.0) * 1e30
    bj = (to_col(kj, ident) - 1.0) * 1e30
    bi = jnp.concatenate([bi, bi], axis=1)
    bj = jnp.concatenate([bj, bj], axis=1)
    ai = nn(xi, w["wa"][...]).astype(BF)
    aj = nn(xj, w["wa"][...]).astype(BF)
    viT = nt(w["wvT"][...], xi).astype(BF)
    vjT = nt(w["wvT"][...], xj).astype(BF)
    diT = refine(xi, attention(aj, ai, vjT, bj, ident), w)
    djT = refine(xj, attention(ai, aj, viT, bi, ident), w)
    riT = (nt(ident, xi) + diT.astype(F32)).astype(BF)
    rjT = (nt(ident, xj) + djT.astype(F32)).astype(BF)
    mi = nn(w["wmT"][...], riT).astype(BF)
    mj = nn(w["wmT"][...], rjT).astype(BF)
    scores = nn(nt(ident, mi).astype(BF), mj) * (LOG2E / 16.0)
    return nt(ident, diT).astype(BF), nt(ident, djT).astype(BF), scores


def marginals(ki, kj, ident):
    m = jnp.sum(ki, axis=1, keepdims=True)
    n = jnp.sum(kj, axis=1, keepdims=True)
    total = m + n
    off = -jnp.log2(jnp.maximum(total, 1.0))
    kic = to_col(ki.astype(BF), ident)[:, :1]
    lr = off - FORGET * (1.0 - kic)
    lc = off - FORGET * (1.0 - kj)
    lrb = jnp.log2(jnp.maximum(n, 1.0)) + off
    lcb = jnp.log2(jnp.maximum(m, 1.0)) + off
    return total, kic, lr, lc, lrb, lcb


def sink_first(c, bucket, lr, lc, lrb, lcb):
    top = jnp.maximum(jnp.max(c, axis=1, keepdims=True), bucket)
    s = jnp.sum(jnp.exp2(c - top), axis=1, keepdims=True) + jnp.exp2(bucket - top)
    f = lr - top - jnp.log2(s)
    fb = lrb - bucket - math.log2(257.0)
    t = jnp.sum(jnp.exp2(c + f), axis=0, keepdims=True) + jnp.exp2(bucket + fb)
    tb = jnp.sum(jnp.exp2(bucket + f), axis=0, keepdims=True) + jnp.exp2(bucket + fb)
    return f, fb, lc - jnp.log2(t), lcb - jnp.log2(tb)


def sink_next(c, bucket, lr, lc, lrb, lcb, r, rb, state):
    f, fb, g, gb = state
    eb = jnp.exp2(bucket + fb + g)
    ebb = jnp.exp2(bucket + fb + gb)
    ub = rb / (jnp.sum(eb, axis=1, keepdims=True) + ebb)
    p = jnp.exp2(c + g + f)
    b = jnp.exp2((bucket + gb) + f)
    u = r / (jnp.sum(p, axis=1, keepdims=True) + b)
    t = eb * ub + jnp.sum(p * u, axis=0, keepdims=True)
    tb = ebb * ub + jnp.sum(b * u, axis=0, keepdims=True)
    return f + jnp.log2(u), fb + jnp.log2(ub), g + lc - jnp.log2(t), gb + lcb - jnp.log2(tb)


def sink_out(c, total, kic, kj, state):
    f, fb, g, gb = state
    plan = jnp.exp2(c + f + g)
    mi = (jnp.sum(plan, axis=1, keepdims=True) * total * kic).astype(BF)
    mj = (jnp.sum(plan, axis=0, keepdims=True) * total * kj).astype(BF)
    first = (lax.broadcasted_iota(I32, (16, 128), 1) == 0).astype(BF)
    return nt(first, jnp.broadcast_to(mi, (KEYS, 128)))[:1], mj.astype(F32)


def row_of(block, index):
    at = lax.broadcasted_iota(I32, block.shape, 0)
    return jnp.sum(jnp.where(at == index, block, 0.0), axis=0, keepdims=True)


def job_of(tab, q, sub):
    code = tab[0, q * SUBS + sub]
    return (code >> 8) & 7, (code >> 12) & 1


def do_scores(q, tab, sub, own, xo, okeep, jkeep, w):
    mine, swap = job_of(tab, q, sub)
    xm = own[mine]
    km = row_of(okeep[...], mine)
    ko = row_of(jkeep[...], q)
    ki = jnp.where(swap == 1, ko, km).astype(BF)
    kj = jnp.where(swap == 1, km, ko).astype(BF)
    di, dj, scores = pair_scores(jnp.where(swap == 1, xo, xm), ki, jnp.where(swap == 1, xm, xo), kj, w)
    return jnp.where(swap == 1, dj, di), jnp.where(swap == 1, di, dj), scores


def do_masses(jobs, sc, tab, sub, okeep, jkeep, bucket, ident):
    swaps, margs, states, kjs = [], [], [], []
    for q, (ref, at) in zip(jobs, sc):
        mine, swap = job_of(tab, q, sub)
        km = row_of(okeep[...], mine)
        ko = row_of(jkeep[...], q)
        ki = jnp.where(swap == 1, ko, km)
        kj = jnp.where(swap == 1, km, ko)
        marg = marginals(ki, kj, ident)
        swaps.append(swap)
        kjs.append(kj)
        margs.append(marg)
        states.append(sink_first(ref[at], bucket, *marg[2:]))
    sums = [(jnp.exp2(m[2]), jnp.exp2(m[4])) for m in margs]

    def sweep(_, states):
        return [sink_next(ref[at], bucket, *m[2:], *r, s) for (ref, at), m, r, s in zip(sc, margs, sums, states)]

    states = lax.fori_loop(0, ITERS - 1, sweep, states)
    outs = []
    for (ref, at), m, s, kj, swap in zip(sc, margs, states, kjs, swaps):
        a, b = sink_out(ref[at], m[0], m[1], kj, s)
        outs.append((jnp.where(swap == 1, b, a), jnp.where(swap == 1, a, b)))
    return outs


def step_of(turn):
    return (turn // 2 + 1) * (1 - 2 * (turn % 2))


def places():
    n = lax.axis_size("img")
    me = lax.axis_index("img")
    sub = lax.axis_index("sub")
    others = [lax.rem(me + step_of(t) + n, n) for t in range(REACH)]
    peers = [lax.rem(sub + d, SUBS) for d in range(1, SUBS)]
    return me, sub, others, peers


def greet(others, peers):
    barrier = pltpu.get_barrier_semaphore()
    for h in others:
        pl.semaphore_signal(barrier, inc=1, device_id={"img": h}, device_id_type=MESH)
    for s in peers:
        pl.semaphore_signal(barrier, inc=1, device_id={"sub": s}, device_id_type=MESH)
    pl.semaphore_wait(barrier, len(others) + len(peers))


def send(src, dst, ssem, rsem, to):
    return pltpu.make_async_remote_copy(
        src_ref=src, dst_ref=dst, send_sem=ssem, recv_sem=rsem, device_id=to, device_id_type=MESH
    )


def own_rows(pairs, live_count, me, img_count):
    first = pairs[:, 0:1]
    second = pairs[:, 1:2]
    slots = pairs.shape[0]
    row_ids = lax.broadcasted_iota(I32, (slots, 1), 0)
    ahead = (second >> 3) - me
    ahead = jnp.where(ahead < 0, ahead + img_count, ahead)
    turn = jnp.where(ahead <= WIN, 2 * (ahead - 1), 2 * (img_count - ahead - 1) + 1)
    live = row_ids < live_count
    key = jnp.where(live, turn, 15)
    code = 1 + (first & 7) * 8 + (second & 7)
    up = lax.broadcasted_iota(I32, (slots, slots), 0)
    across = lax.broadcasted_iota(I32, (slots, slots), 1)
    key_row = jnp.sum(jnp.where(up == across, key, 0), axis=0, keepdims=True)
    rank = jnp.sum(jnp.where((key_row == key) & (across < up), 1, 0), axis=1, keepdims=True)
    lanes = lax.broadcasted_iota(I32, (slots, 128), 1)
    lane = lax.broadcasted_iota(I32, (1, 128), 1)
    rows = []
    for k in (key, key ^ 1):
        at = jnp.where(live, k * 8 + rank, -1)
        codes = jnp.sum(jnp.where(lanes == at, code, 0), axis=0, keepdims=True)
        counts = jnp.sum(jnp.where((lanes == 64 + k) & live, 1, 0), axis=0, keepdims=True)
        row = codes + counts
        rows.append(jnp.where((lane >= 80) & (lane < 88), live_count, row))
    return rows


def plan_rows(own, near, live_count):
    r8 = lax.broadcasted_iota(I32, (8, 128), 0)
    l8 = lax.broadcasted_iota(I32, (8, 128), 1)
    mine = jnp.where(l8 < 64, l8 >> 3, l8 & 7)
    from_near = jnp.sum(jnp.where((mine == r8) & (r8 < REACH), near, 0), axis=0, keepdims=True)
    slots = 64
    lanes = lax.broadcasted_iota(I32, (slots, 128), 1)
    slot = lax.broadcasted_iota(I32, (slots, 1), 0)
    turn = slot >> 3
    u = slot & 7
    own_all = jnp.broadcast_to(own, (slots, 128))
    near_all = jnp.broadcast_to(from_near, (slots, 128))

    def pick(table, lane):
        return jnp.sum(jnp.where(lanes == lane, table, 0), axis=1, keepdims=True)

    n_own = pick(own_all, 64 + turn)
    n_near = pick(near_all, 64 + turn)
    l_near = pick(near_all, 80 + turn)

    def sixth(value):
        return (jnp.maximum(value, 0) * 43) >> 8

    give = jnp.maximum(jnp.minimum(jnp.minimum(sixth(live_count - l_near), n_own), MOST - n_near), 0)
    take = jnp.maximum(jnp.minimum(jnp.minimum(sixth(l_near - live_count), n_near), MOST - n_own), 0)
    kept = n_own - give
    near_kept = n_near - take
    own_code = pick(own_all, turn * 8 + u) - 1
    near_code = pick(near_all, turn * 8 + u) - 1
    taken_code = pick(near_all, turn * 8 + near_kept + u - kept) - 1
    given_code = pick(own_all, turn * 8 + kept + u - near_kept) - 1
    live = (u < kept + take) & (turn < REACH)
    image = jnp.where(u < kept, own_code >> 3, taken_code & 7)
    swap = jnp.where(u < kept, 0, 1)
    asked = (u < near_kept + give) & (turn < REACH)
    sends = jnp.where(u < near_kept, near_code & 7, given_code >> 3)
    eye64 = lax.broadcasted_iota(I32, (slots, slots), 0) == lax.broadcasted_iota(I32, (slots, slots), 1)
    live_row = jnp.sum(jnp.where(eye64, jnp.where(live, 1, 0), 0), axis=0, keepdims=True)
    short = lax.broadcasted_iota(I32, (slots, slots), 1)
    place = jnp.sum(jnp.where(short < slot, live_row, 0), axis=1, keepdims=True)
    count = jnp.sum(live_row, axis=1, keepdims=True)

    def put(lane, value):
        return jnp.sum(jnp.where(lanes == lane, value, 0), axis=0, keepdims=True)

    by_place = put(jnp.where(live, place, -1), 1 + slot + image * 256 + swap * 4096)
    by_slot = put(slot, jnp.where(asked, 1 + sends, 0))
    places_row = put(slot, jnp.where(live, place, 0))
    row = lax.broadcasted_iota(I32, (8, 128), 0)
    out = jnp.where(row == 0, by_place, jnp.where(row == 1, by_slot, jnp.where(row == 2, places_row, count)))
    return out


def meet_kernel(pairs, pair_count, wv, wo, wh, gain, wd, wm, tab, wvT, woT, whT, wdT, wmT, gcol, told, near, ssem, rsem):
    me, sub, others, peers = places()
    own, out = own_rows(pairs[...], pair_count[0], me, lax.axis_size("img"))
    told[...] = jnp.broadcast_to(out, (8, 128))
    greet(others, [])
    copies = [send(told, near.at[t ^ 1], ssem.at[t], rsem.at[t ^ 1], {"img": others[t]}) for t in range(REACH)]
    for copy in copies:
        copy.start()
    prepare(wv, wo, wh, gain, wd, wm, wvT, woT, whT, wdT, wmT, gcol)
    for copy in copies:
        copy.wait()
    row = lax.broadcasted_iota(I32, (8, 128), 0)
    table = jnp.zeros((8, 128), I32)
    for t in range(REACH):
        table = jnp.where(row == t, near[t], table)
    tab[...] = plan_rows(own, table, pair_count[0])


def sent_image(tab, t, u):
    return tab[1, t * 8 + u]


def fetch_kernel(tab, desc, counts, visible, wa, wvT, woT, whT, wdT, wmT, gcol, own, xj, okeep, jkeep, dmine, dother, sc, ident, zst, zland, zms, zml, yst, yms, yml, omask, zsem, zrem, ysem, yrem, osem, orem):
    me, sub, others, peers = places()
    rows = pl.ds(pl.multiple_of(sub * ROWS, ROWS), ROWS)
    ident[...] = eye(256)
    w = dict(wa=wa, wvT=wvT, woT=woT, whT=whT, wdT=wdT, wmT=wmT, gcol=gcol, ident=ident)
    for a in range(OWN):
        own[a, rows, :] = desc[a]
    image = lax.broadcasted_iota(I32, (OWN, ROWS), 0)
    found = jnp.zeros((OWN, ROWS), I32)
    for a in range(OWN):
        found = jnp.where(image == a, counts[a], found)
    spot = lax.broadcasted_iota(I32, (OWN, ROWS), 1) + sub * ROWS
    kept = jnp.where((spot < found) & (visible[...] > 0), 1.0, 0.0)
    wide = jnp.concatenate([kept] * SUBS, axis=1)
    lane = lax.broadcasted_iota(I32, (OWN, KEYS), 1)
    wide = jnp.where((lane >= sub * ROWS) & (lane < sub * ROWS + ROWS), wide, 0.0)
    omask[0] = wide
    greet(others, peers)
    zcopies = []
    for t in (4, 5, 2, 3, 0, 1):
        line = lax.broadcasted_iota(I32, (8, KEYS), 0)
        masks = jnp.zeros((8, KEYS), F32)
        for u in range(MOST):
            which = jnp.maximum(sent_image(tab, t, u) - 1, 0)
            zst[t, u] = desc[which]
            masks = jnp.where(line == u, row_of(wide, which), masks)
        zms[t] = masks
        to = {"img": others[t]}
        zcopies.append(send(zst.at[t], zland.at[t ^ 1], zsem.at[0, t], zrem.at[0, t ^ 1], to))
        zcopies.append(send(zms.at[t], zml.at[t ^ 1], zsem.at[1, t], zrem.at[1, t ^ 1], to))
        zcopies[-2].start()
        zcopies[-1].start()
    ocopies = []
    for d in range(1, SUBS):
        to = {"sub": peers[d - 1]}
        mine = own.at[:, rows, :]
        ocopies.append(send(mine, mine, osem.at[0, d - 1], orem.at[0, d - 1], to))
        ocopies.append(send(omask.at[0], omask.at[d], osem.at[1, d - 1], orem.at[1, d - 1], to))
    for copy in ocopies:
        copy.start()
    for copy in zcopies:
        copy.wait()
    ycopies = []
    line = lax.broadcasted_iota(I32, (JOBS, KEYS), 0)
    zmasks = jnp.concatenate([zml[t] for t in range(REACH)], axis=0)
    slots = [[None] * SUBS for _ in range(JOBS)]
    for d in range(SUBS):
        worker = sub if d == 0 else peers[d - 1]
        masks = jnp.zeros((JOBS, KEYS), F32)
        for q in range(JOBS):
            slots[q][d] = jnp.maximum((tab[0, q * SUBS + worker] & 255) - 1, 0)
            masks = jnp.where(line == q, row_of(zmasks, slots[q][d]), masks)
        yms[d] = masks
    mcopies = []
    for d in range(1, SUBS):
        mcopies.append(send(yms.at[d], yml.at[d - 1], ysem.at[JOBS, d - 1], yrem.at[JOBS, d - 1], {"sub": peers[d - 1]}))
        mcopies[-1].start()
    for q in range(JOBS):
        for d in range(1, SUBS):
            yst[d - 1, q] = zland[slots[q][d] >> 3, slots[q][d] & 7]
            copy = send(yst.at[d - 1, q], xj.at[q, rows, :], ysem.at[q, d - 1], yrem.at[q, d - 1], {"sub": peers[d - 1]})
            copy.start()
            ycopies.append(copy)
        xj[q, rows, :] = zland[slots[q][0] >> 3, slots[q][0] & 7]
    for copy in ocopies:
        copy.wait()
    okeep[...] = omask[0] + omask[1] + omask[2] + omask[3]
    for copy in mcopies:
        copy.wait()
    jkeep[...] = yms[0] + yml[0] + yml[1] + yml[2]
    for q in range(EARLY):
        for copy in ycopies[3 * q : 3 * q + 3]:
            copy.wait()
        dmine[q], dother[q], sc[q] = do_scores(q, tab, sub, own, xj[q], okeep, jkeep, w)
    for copy in ycopies[3 * EARLY :]:
        copy.wait()


def work_kernel(tab, own, xj, okeep, jkeep, bucket, wa, wvT, woT, whT, wdT, wmT, gcol, dmine, dother, mm, mo, ident, sc):
    sub = lax.axis_index("sub")
    ident[...] = eye(256)
    w = dict(wa=wa, wvT=wvT, woT=woT, whT=whT, wdT=wdT, wmT=wmT, gcol=gcol, ident=ident)
    n = ((tab[3, 0] + (SUBS - 1) - sub) >> 2) - FIXED
    binv = bucket[...] * LOG2E

    @pl.loop(0, n)
    def _(p):
        q = FIXED + p
        dmine[p], dother[p], sc[p] = do_scores(q, tab, sub, own, xj[q], okeep, jkeep, w)

    def masses(ps):
        outs = do_masses([FIXED + p for p in ps], [(sc, p) for p in ps], tab, sub, okeep, jkeep, binv, ident[...])
        for p, (a, b) in zip(ps, outs):
            mm[p] = jnp.broadcast_to(a, (8, KEYS))
            mo[p] = jnp.broadcast_to(b, (8, KEYS))

    @pl.loop(0, n >> 1)
    def _(p):
        masses([2 * p, 2 * p + 1])

    @pl.when((n & 1) == 1)
    def _():
        masses([n - 1])


def give_kernel(
    tab, own, xj, okeep, jkeep, bucket, wa, wvT, woT, whT, wdT, wmT, gcol, dmine0, dother0, sc0, dmine2, dother2, mm2, mo2,
    upd, mass, ident, dmine1, dother1, sc1, yb, ymst, yml, zst, zms, zret, zmr, parts, got, mparts, mgot,
    ysem, yrem, zsem, zrem, osem, orem,
):
    me, sub, others, peers = places()
    rows = pl.ds(pl.multiple_of(sub * ROWS, ROWS), ROWS)
    ident[...] = eye(256)
    w = dict(wa=wa, wvT=wvT, woT=woT, whT=whT, wdT=wdT, wmT=wmT, gcol=gcol, ident=ident)
    binv = bucket[...] * LOG2E
    mline = lax.broadcasted_iota(I32, (JOBS, KEYS), 0)

    def held(q, parts):
        if q < EARLY:
            return parts[0], q
        if q < FIXED:
            return parts[1], q - EARLY
        return parts[2], q - FIXED

    greet(others, peers)
    ycopies = []

    def hand_back(q):
        ref, at = held(q, (dother0, dother1, dother2))
        for d in range(1, SUBS):
            p = peers[d - 1]
            part = ref.at[at, pl.ds(pl.multiple_of(p * ROWS, ROWS), ROWS), :]
            ycopies.append(send(part, yb.at[q, sub], ysem.at[q, d - 1], yrem.at[q, d - 1], {"sub": p}))
            ycopies[-1].start()
        yb[q, sub] = ref[at, rows, :]

    for q in list(range(EARLY)) + list(range(FIXED, JOBS)):
        hand_back(q)
    for q in range(EARLY, FIXED):
        dmine1[q - EARLY], dother1[q - EARLY], sc1[q - EARLY] = do_scores(q, tab, sub, own, xj[q], okeep, jkeep, w)
        hand_back(q)
    masses = [None] * FIXED
    halves = (list(range(FIXED // 2)), list(range(FIXED // 2, FIXED)))
    outs = do_masses(halves[0], [held(q, (sc0, sc1)) for q in halves[0]], tab, sub, okeep, jkeep, binv, ident[...])
    for q, out in zip(halves[0], outs):
        masses[q] = out
    for copy in ycopies:
        copy.wait()
    zcopies = [None] * REACH
    for t in (4, 5, 2, 3, 0, 1):
        for u in range(MOST):
            place = tab[2, t * 8 + u]
            zst[t, u] = yb[place >> 2, place & 3]
        zcopies[t] = send(zst.at[t], zret.at[t ^ 1], zsem.at[0, t], zrem.at[0, t ^ 1], {"img": others[t]})
        zcopies[t].start()
    n = (tab[3, 0] + (SUBS - 1) - sub) >> 2
    owners = [jnp.where(q < n, job_of(tab, q, sub)[0], -1) for q in range(JOBS)]
    for a in range(OWN):
        for s in range(SUBS):
            value = jnp.zeros((ROWS, D), F32)
            for q in range(JOBS):
                ref, at = held(q, (dmine0, dmine1, dmine2))
                value = value + jnp.where(owners[q] == a, ref[at, s * ROWS : s * ROWS + ROWS, :].astype(F32), 0.0)
            parts[s, a] = value.astype(BF)
    ocopies = []
    for d in range(1, SUBS):
        to = {"sub": peers[d - 1]}
        ocopies.append(send(parts.at[peers[d - 1]], got.at[d - 1], osem.at[0, d - 1], orem.at[0, d - 1], to))
        ocopies[-1].start()
    outs = do_masses(halves[1], [held(q, (sc0, sc1)) for q in halves[1]], tab, sub, okeep, jkeep, binv, ident[...])
    for q, out in zip(halves[1], outs):
        masses[q] = out
    mine = [masses[q][0] if q < FIXED else mm2[q - FIXED, 0:1, :] for q in range(JOBS)]
    away = [masses[q][1] if q < FIXED else mo2[q - FIXED, 0:1, :] for q in range(JOBS)]
    table = jnp.zeros((JOBS, KEYS), F32)
    for q in range(JOBS):
        table = jnp.where(mline == q, away[q], table)
    ymst[...] = table
    yml[sub] = table
    ymcopies = []
    for d in range(1, SUBS):
        ymcopies.append(send(ymst, yml.at[sub], ysem.at[JOBS, d - 1], yrem.at[JOBS, d - 1], {"sub": peers[d - 1]}))
        ymcopies[-1].start()
    table = jnp.zeros((OWN, KEYS), F32)
    for a in range(OWN):
        for q in range(JOBS):
            table = table + jnp.where((mline == a) & (owners[q] == a), mine[q], 0.0)
    mparts[...] = table
    for d in range(1, SUBS):
        copy = send(mparts, mgot.at[d - 1], osem.at[1, d - 1], orem.at[1, d - 1], {"sub": peers[d - 1]})
        copy.start()
        ocopies.append(copy)
    for copy in ymcopies:
        copy.wait()
    ymasses = jnp.concatenate([yml[s] for s in range(SUBS)], axis=0)
    zmcopies = []
    for t in (4, 5, 2, 3, 0, 1):
        back = jnp.zeros((8, KEYS), F32)
        for u in range(MOST):
            place = tab[2, t * 8 + u]
            back = jnp.where(mline == u, row_of(ymasses, (place & 3) * JOBS + (place >> 2)), back)
        zms[t] = back
        zmcopies.append(send(zms.at[t], zmr.at[t ^ 1], zsem.at[1, t], zrem.at[1, t ^ 1], {"img": others[t]}))
        zmcopies[-1].start()
    for copy in ocopies:
        copy.wait()
    for t in range(REACH):
        zcopies[t].wait()
    wants = [(t, u, sent_image(tab, t, u) - 1) for t in range(REACH) for u in range(MOST)]
    for a in range(OWN):
        value = parts[sub, a].astype(F32)
        for d in range(SUBS - 1):
            value = value + got[d, a].astype(F32)
        for t, u, which in wants:
            value = value + jnp.where(which == a, zret[t, u].astype(F32), 0.0)
        upd[a] = value.astype(BF)
    for copy in zmcopies:
        copy.wait()
    total = mparts[...] + mgot[0] + mgot[1] + mgot[2]
    for a in range(OWN):
        extra = jnp.zeros((1, KEYS), F32)
        for t, u, which in wants:
            extra = extra + jnp.where(which == a, zmr[t, u : u + 1, :], 0.0)
        total = total + jnp.where(mline == a, extra, 0.0)
    out = jnp.zeros((OWN, ROWS), F32)
    for s in range(SUBS):
        out = jnp.where(sub == s, total[:, s * ROWS : s * ROWS + ROWS], out)
    mass[...] = out


VM = pl.BlockSpec(memory_space=pltpu.VMEM)
SM = pl.BlockSpec(memory_space=pltpu.SMEM)
DMA = pltpu.SemaphoreType.DMA


def shape(dims, kind=BF):
    return jax.ShapeDtypeStruct(dims, kind)


def talk(number):
    return pltpu.CompilerParams(collective_id=number, has_side_effects=True, vmem_limit_bytes=LIMIT)


def local(descriptors, counts, visible, pair_list, pair_count, w_attend, w_value, w_output, w_hidden, norm_gain, w_down, w_match, unassigned_bucket):
    V = pltpu.VMEM
    tab, *ready = pl.pallas_call(
        meet_kernel,
        out_shape=(shape((8, 128), I32), shape((256, 256)), shape((256, 256)), shape((512, 512)), shape((256, 512)), shape((256, 256)), shape((512, 128), F32)),
        in_specs=[VM, SM] + [VM] * 6,
        out_specs=(VM,) * 7,
        scratch_shapes=[V((8, 128), I32), V((REACH, 8, 128), I32), DMA((REACH,)), DMA((REACH,))],
        compiler_params=talk(0),
    )(pair_list, pair_count, w_value, w_output, w_hidden, norm_gain.reshape(1, -1), w_down, w_match)
    own, xj, okeep, jkeep, *early = pl.pallas_call(
        fetch_kernel,
        out_shape=(
            shape((OWN, KEYS, D)), shape((JOBS, KEYS, D)), shape((OWN, KEYS), F32), shape((JOBS, KEYS), F32),
            shape((EARLY, KEYS, D)), shape((EARLY, KEYS, D)), shape((EARLY, KEYS, KEYS), F32),
        ),
        in_specs=[SM, VM, SM, VM] + [VM] * 7,
        out_specs=(VM,) * 7,
        scratch_shapes=[
            V((256, 256), BF),
            V((REACH, MOST, ROWS, D), BF), V((REACH, MOST, ROWS, D), BF), V((REACH, 8, KEYS), F32), V((REACH, 8, KEYS), F32),
            V((SUBS - 1, JOBS, ROWS, D), BF), V((SUBS, JOBS, KEYS), F32), V((SUBS - 1, JOBS, KEYS), F32), V((SUBS, OWN, KEYS), F32),
            DMA((2, REACH)), DMA((2, REACH)), DMA((JOBS + 1, SUBS - 1)), DMA((JOBS + 1, SUBS - 1)), DMA((2, SUBS - 1)), DMA((2, SUBS - 1)),
        ],
        compiler_params=talk(1),
    )(tab, descriptors, counts, visible, w_attend, *ready)
    common = (tab, own, xj, okeep, jkeep, unassigned_bucket.reshape(1, 1), w_attend, *ready)
    late = JOBS - FIXED
    rest = pl.pallas_call(
        work_kernel,
        out_shape=(shape((late, KEYS, D)), shape((late, KEYS, D)), shape((late, 8, KEYS), F32), shape((late, 8, KEYS), F32)),
        in_specs=[SM] + [VM] * 12,
        out_specs=(VM,) * 4,
        scratch_shapes=[V((256, 256), BF), V((late, KEYS, KEYS), F32)],
        compiler_params=pltpu.CompilerParams(vmem_limit_bytes=LIMIT),
    )(*common)
    mid = FIXED - EARLY
    return pl.pallas_call(
        give_kernel,
        out_shape=(shape((OWN, ROWS, D)), shape((OWN, ROWS), F32)),
        in_specs=[SM] + [VM] * 19,
        out_specs=(VM, VM),
        scratch_shapes=[
            V((256, 256), BF), V((mid, KEYS, D), BF), V((mid, KEYS, D), BF), V((mid, KEYS, KEYS), F32),
            V((JOBS, SUBS, ROWS, D), BF), V((JOBS, KEYS), F32), V((SUBS, JOBS, KEYS), F32),
            V((REACH, MOST, ROWS, D), BF), V((REACH, 8, KEYS), F32), V((REACH, MOST, ROWS, D), BF), V((REACH, 8, KEYS), F32),
            V((SUBS, OWN, ROWS, D), BF), V((SUBS - 1, OWN, ROWS, D), BF), V((OWN, KEYS), F32), V((SUBS - 1, OWN, KEYS), F32),
            DMA((JOBS + 1, SUBS - 1)), DMA((JOBS + 1, SUBS - 1)), DMA((2, REACH)), DMA((2, REACH)), DMA((2, SUBS - 1)), DMA((2, SUBS - 1)),
        ],
        compiler_params=talk(2),
    )(*common, *early, *rest)


def solution(mesh):
    placed = (P("img", "sub", None), P("img"), P("img", "sub"), P("img", None), P("img")) + (P(),) * 8
    return jax.shard_map(
        local, mesh=mesh, in_specs=placed, out_specs=(P("img", "sub", None), P("img", "sub")), check_vma=False
    )
```

```python
import math

import jax
import jax.numpy as jnp
from jax import lax
from jax.experimental import pallas as pl
from jax.experimental.pallas import tpu as pltpu
from jax.sharding import PartitionSpec as P

BF = jnp.bfloat16
F32 = jnp.float32
I32 = jnp.int32
LOG2E = 1.4426950408889634
FORGET = 30.0 * LOG2E
HEADS = 4
ITERS = 10
KEYS = 256
D = 256
WIN = 3
REACH = 2 * WIN
MOST = 6
OWN = 8
ROWS = 64
SUBS = 4
JOBS = 8
FIXED = 4
EARLY = 2
MESH = pl.DeviceIdType.MESH
LIMIT = 56 * 2**20


def nn(a, b):
    return lax.dot_general(a, b, (((1,), (0,)), ((), ())), preferred_element_type=F32)


def nt(a, b):
    return lax.dot_general(a, b, (((1,), (1,)), ((), ())), preferred_element_type=F32)


def eye(n):
    up = lax.broadcasted_iota(I32, (n, n), 0)
    return (up == lax.broadcasted_iota(I32, (n, n), 1)).astype(BF)


def to_col(row, ident):
    return nt(ident, jnp.broadcast_to(row, (128, row.shape[1])))


def prepare(wa, wv, wo, wh, gain, wd, waT, wvT, woT, whT, wdT, gcol):
    ident = eye(256)
    waT[...] = nt(ident, wa[...]).astype(BF)
    wvT[...] = nt(ident, wv[...]).astype(BF)
    woT[...] = nt(ident, wo[...]).astype(BF)
    for a in range(0, 512, 256):
        for b in range(0, 512, 256):
            whT[a : a + 256, b : b + 256] = nt(ident, wh[b : b + 256, a : a + 256]).astype(BF)
    for b in range(0, 512, 256):
        wdT[:, b : b + 256] = nt(ident, wd[b : b + 256, :]).astype(BF)
    same = lax.broadcasted_iota(I32, (128, 128), 0) == lax.broadcasted_iota(I32, (128, 128), 1)
    for q in range(0, 512, 128):
        spread = jnp.broadcast_to(gain[:, q : q + 128], (128, 128))
        column = jnp.sum(jnp.where(same, spread, 0.0), axis=1, keepdims=True)
        gcol[q : q + 128, :] = jnp.broadcast_to(column, (128, 128))


def attention(sides, ahead=4, behind=2):
    ones = jnp.ones((16, KEYS), BF)
    steps = [(h, s) for h in range(HEADS) for s in range(len(sides))]

    def similarity(h, s):
        a_other, aT_self, _, bias = sides[s]
        sl = slice(h * 64, h * 64 + 64)
        value = nn(a_other[:, sl], aT_self[sl]) * (LOG2E / 8.0) + bias
        return value, jnp.max(value, axis=0, keepdims=True)

    def finish(r):
        return (r[:64] * (1.0 / r[64:65])).astype(BF)

    waiting = [similarity(*step) for step in steps[:ahead]]
    late = []
    outs = {}
    for i, (h, s) in enumerate(steps):
        if i + ahead < len(steps):
            waiting.append(similarity(*steps[i + ahead]))
        value, top = waiting.pop(0)
        e = jnp.exp2(value - top).astype(BF)
        late.append(((h, s), nn(jnp.concatenate([sides[s][2][h * 64 : h * 64 + 64], ones], axis=0), e)))
        if len(late) > behind:
            step, r = late.pop(0)
            outs[step] = finish(r)
    for step, r in late:
        outs[step] = finish(r)
    return [jnp.concatenate([outs[h, s] for h in range(HEADS)], axis=0) for s in range(len(sides))]


def refine(xs, msgs, w):
    half = math.sqrt(0.5)
    gain = jnp.concatenate([w["gcol"][...]] * 2, axis=1) * half

    def hidden(i):
        sentT = nn(w["woT"][...], msgs[i]).astype(BF)
        return nt(w["whT"][:, :256], xs[i]) + nn(w["whT"][:, 256:], sentT)

    outs = []
    later = hidden(0)
    for i in range(len(xs)):
        hid = later
        if i + 1 < len(xs):
            later = hidden(i + 1)
        mean = jnp.sum(hid, axis=0, keepdims=True) * (1.0 / 512)
        cen = hid - mean
        var = jnp.sum(cen * cen, axis=0, keepdims=True) * (1.0 / 512)
        z = cen * lax.rsqrt(var + 1e-5) * gain
        outs.append(nn(w["wdT"][...], ((half * z) * (1.0 + lax.erf(z))).astype(BF)).astype(BF))
    return outs


def pair_scores(pairs, w):
    ident = w["ident"][...]
    xs, biases = [], []
    for xi, ki, xj, kj in pairs:
        xs += [xi, xj]
        for keep in (ki, kj):
            bias = (to_col(keep, ident) - 1.0) * 1e30
            biases.append(jnp.concatenate([bias, bias], axis=1))
    attend = [nn(x, w["wa"][...]).astype(BF) for x in xs]
    attendT = [nt(w["waT"][...], x).astype(BF) for x in xs]
    valueT = [nt(w["wvT"][...], x).astype(BF) for x in xs]
    msgs = attention([(attend[i ^ 1], attendT[i], valueT[i ^ 1], biases[i ^ 1]) for i in range(len(xs))])
    deltas = [nt(ident, d).astype(BF) for d in refine(xs, msgs, w)]
    match = [
        nn((x.astype(F32) + d.astype(F32)).astype(BF), w["wm"][...]).astype(BF) for x, d in zip(xs, deltas)
    ]
    return [
        (deltas[i], deltas[i + 1], nt(match[i], match[i + 1]) * (LOG2E / 16.0)) for i in range(0, len(xs), 2)
    ]


def marginals(ki, kj, ident):
    m = jnp.sum(ki, axis=1, keepdims=True)
    n = jnp.sum(kj, axis=1, keepdims=True)
    total = m + n
    off = -jnp.log2(jnp.maximum(total, 1.0))
    kic = to_col(ki.astype(BF), ident)
    lr = off - FORGET * (1.0 - kic)
    lc = off - FORGET * (1.0 - kj)
    lrb = jnp.log2(jnp.maximum(n, 1.0)) + off
    lcb = jnp.log2(jnp.maximum(m, 1.0)) + off
    return total, kic, lr, lc, lrb, lcb


def sink_first(c, bucket, lr, lc, lrb, lcb):
    top = jnp.maximum(jnp.max(c, axis=1, keepdims=True), bucket)
    s = jnp.sum(jnp.exp2(c - top), axis=1, keepdims=True) + jnp.exp2(bucket - top)
    f = lr - top - jnp.log2(s)
    fb = lrb - bucket - math.log2(257.0)
    halves = [jnp.sum(jnp.exp2(c[:, at : at + 128] + f), axis=0, keepdims=True) for at in (0, 128)]
    t = jnp.concatenate(halves, axis=1) + jnp.exp2(bucket + fb)
    tb = jnp.sum(jnp.exp2(bucket + f), axis=0, keepdims=True)[:, :1] + jnp.exp2(bucket + fb)
    return f, fb, lc - jnp.log2(t), lcb - jnp.log2(tb)


def sink_next(c, at, bucket, lr, lc, lrb, lcb, state):
    f, fb, g, gb = state
    eb = jnp.exp2(bucket + fb + g)
    ebb = jnp.exp2(bucket + fb + gb)
    dub = lrb - jnp.log2(jnp.sum(eb, axis=1, keepdims=True) + ebb)
    ub = jnp.exp2(dub)
    p0 = jnp.exp2(c[at, :, :128] + g[:, :128] + f)
    p1 = jnp.exp2(c[at, :, 128:] + g[:, 128:] + f)
    b = jnp.exp2((bucket + gb) + f)
    du = lr - jnp.log2(jnp.sum(p0 + p1, axis=1, keepdims=True) + b)
    u = jnp.exp2(du)
    t = [jnp.sum(p * u, axis=0, keepdims=True) for p in (p0, p1)]
    t = eb * ub + jnp.concatenate(t, axis=1)
    tb = ebb * ub + jnp.sum(b * u, axis=0, keepdims=True)[:, :1]
    return f + du, fb + dub, g + lc - jnp.log2(t), gb + lcb - jnp.log2(tb)


def sink_out(c, total, kic, kj, state):
    f, fb, g, gb = state
    p0 = jnp.exp2(c[:, :128] + g[:, :128] + f)
    p1 = jnp.exp2(c[:, 128:] + g[:, 128:] + f)
    mi = (jnp.sum(p0 + p1, axis=1, keepdims=True) * total * kic).astype(BF)
    halves = [jnp.sum(p, axis=0, keepdims=True) for p in (p0, p1)]
    mj = (jnp.concatenate(halves, axis=1) * total * kj).astype(BF)
    first = (lax.broadcasted_iota(I32, (16, 128), 1) == 0).astype(BF)
    return nt(first, mi)[:1], mj.astype(F32)


def row_of(block, index):
    at = lax.broadcasted_iota(I32, block.shape, 0)
    return jnp.sum(jnp.where(at == index, block, 0.0), axis=0, keepdims=True)


def job_of(tab, q, sub):
    code = tab[0, q * SUBS + sub]
    return (code >> 8) & 7, (code >> 12) & 1


def do_scores(jobs, tab, sub, own, xj, okeep, jkeep, w):
    pairs, swaps = [], []
    for q in jobs:
        mine, swap = job_of(tab, q, sub)
        xm, xo = own[mine], xj[q]
        km = row_of(okeep[...], mine)
        ko = row_of(jkeep[...], q)
        ki = jnp.where(swap == 1, ko, km).astype(BF)
        kj = jnp.where(swap == 1, km, ko).astype(BF)
        pairs.append((jnp.where(swap == 1, xo, xm), ki, jnp.where(swap == 1, xm, xo), kj))
        swaps.append(swap)
    return [
        (jnp.where(swap == 1, dj, di), jnp.where(swap == 1, di, dj), scores)
        for swap, (di, dj, scores) in zip(swaps, pair_scores(pairs, w))
    ]


def do_masses(jobs, sc, tab, sub, okeep, jkeep, bucket, ident):
    swaps, margs, states, kjs = [], [], [], []
    for q, (ref, at) in zip(jobs, sc):
        mine, swap = job_of(tab, q, sub)
        km = row_of(okeep[...], mine)
        ko = row_of(jkeep[...], q)
        ki = jnp.where(swap == 1, ko, km)
        kj = jnp.where(swap == 1, km, ko)
        marg = marginals(ki, kj, ident)
        swaps.append(swap)
        kjs.append(kj)
        margs.append(marg)
        states.append(sink_first(ref[at], bucket, *marg[2:]))

    def sweep(_, states):
        return [sink_next(ref, at, bucket, *m[2:], s) for (ref, at), m, s in zip(sc, margs, states)]

    states = lax.fori_loop(0, ITERS - 1, sweep, states)
    outs = []
    for (ref, at), m, s, kj, swap in zip(sc, margs, states, kjs, swaps):
        a, b = sink_out(ref[at], m[0], m[1], kj, s)
        outs.append((jnp.where(swap == 1, b, a), jnp.where(swap == 1, a, b)))
    return outs


def step_of(turn):
    return (turn // 2 + 1) * (1 - 2 * (turn % 2))


def places():
    n = lax.axis_size("img")
    me = lax.axis_index("img")
    sub = lax.axis_index("sub")
    others = [lax.rem(me + step_of(t) + n, n) for t in range(REACH)]
    peers = [lax.rem(sub + d, SUBS) for d in range(1, SUBS)]
    return me, sub, others, peers


def greet(others, peers):
    barrier = pltpu.get_barrier_semaphore()
    for h in others:
        pl.semaphore_signal(barrier, inc=1, device_id={"img": h}, device_id_type=MESH)
    for s in peers:
        pl.semaphore_signal(barrier, inc=1, device_id={"sub": s}, device_id_type=MESH)
    pl.semaphore_wait(barrier, len(others) + len(peers))


def send(src, dst, ssem, rsem, to):
    return pltpu.make_async_remote_copy(
        src_ref=src, dst_ref=dst, send_sem=ssem, recv_sem=rsem, device_id=to, device_id_type=MESH
    )


def own_rows(pairs, live_count, me, img_count):
    first = pairs[:, 0:1]
    second = pairs[:, 1:2]
    slots = pairs.shape[0]
    row_ids = lax.broadcasted_iota(I32, (slots, 1), 0)
    ahead = (second >> 3) - me
    ahead = jnp.where(ahead < 0, ahead + img_count, ahead)
    turn = jnp.where(ahead <= WIN, 2 * (ahead - 1), 2 * (img_count - ahead - 1) + 1)
    live = row_ids < live_count
    key = jnp.where(live, turn, 15)
    code = 1 + (first & 7) * 8 + (second & 7)
    up = lax.broadcasted_iota(I32, (slots, slots), 0)
    across = lax.broadcasted_iota(I32, (slots, slots), 1)
    key_row = jnp.sum(jnp.where(up == across, key, 0), axis=0, keepdims=True)
    rank = jnp.sum(jnp.where((key_row == key) & (across < up), 1, 0), axis=1, keepdims=True)
    lanes = lax.broadcasted_iota(I32, (slots, 128), 1)
    lane = lax.broadcasted_iota(I32, (1, 128), 1)
    rows = []
    for k in (key, key ^ 1):
        at = jnp.where(live, k * 8 + rank, -1)
        codes = jnp.sum(jnp.where(lanes == at, code, 0), axis=0, keepdims=True)
        counts = jnp.sum(jnp.where((lanes == 64 + k) & live, 1, 0), axis=0, keepdims=True)
        row = codes + counts
        rows.append(jnp.where((lane >= 80) & (lane < 88), live_count, row))
    return rows


def plan_rows(own, near, live_count):
    r8 = lax.broadcasted_iota(I32, (8, 128), 0)
    l8 = lax.broadcasted_iota(I32, (8, 128), 1)
    mine = jnp.where(l8 < 64, l8 >> 3, l8 & 7)
    from_near = jnp.sum(jnp.where((mine == r8) & (r8 < REACH), near, 0), axis=0, keepdims=True)
    slots = 64
    lanes = lax.broadcasted_iota(I32, (slots, 128), 1)
    slot = lax.broadcasted_iota(I32, (slots, 1), 0)
    turn = slot >> 3
    u = slot & 7
    own_all = jnp.broadcast_to(own, (slots, 128))
    near_all = jnp.broadcast_to(from_near, (slots, 128))

    def pick(table, lane):
        return jnp.sum(jnp.where(lanes == lane, table, 0), axis=1, keepdims=True)

    n_own = pick(own_all, 64 + turn)
    n_near = pick(near_all, 64 + turn)
    l_near = pick(near_all, 80 + turn)

    def sixth(value):
        return (jnp.maximum(value, 0) * 43) >> 8

    give = jnp.maximum(jnp.minimum(jnp.minimum(sixth(live_count - l_near), n_own), MOST - n_near), 0)
    take = jnp.maximum(jnp.minimum(jnp.minimum(sixth(l_near - live_count), n_near), MOST - n_own), 0)
    kept = n_own - give
    near_kept = n_near - take
    own_code = pick(own_all, turn * 8 + u) - 1
    near_code = pick(near_all, turn * 8 + u) - 1
    taken_code = pick(near_all, turn * 8 + near_kept + u - kept) - 1
    given_code = pick(own_all, turn * 8 + kept + u - near_kept) - 1
    live = (u < kept + take) & (turn < REACH)
    image = jnp.where(u < kept, own_code >> 3, taken_code & 7)
    swap = jnp.where(u < kept, 0, 1)
    asked = (u < near_kept + give) & (turn < REACH)
    sends = jnp.where(u < near_kept, near_code & 7, given_code >> 3)
    eye64 = lax.broadcasted_iota(I32, (slots, slots), 0) == lax.broadcasted_iota(I32, (slots, slots), 1)
    live_row = jnp.sum(jnp.where(eye64, jnp.where(live, 1, 0), 0), axis=0, keepdims=True)
    short = lax.broadcasted_iota(I32, (slots, slots), 1)
    place = jnp.sum(jnp.where(short < slot, live_row, 0), axis=1, keepdims=True)
    count = jnp.sum(live_row, axis=1, keepdims=True)

    def put(lane, value):
        return jnp.sum(jnp.where(lanes == lane, value, 0), axis=0, keepdims=True)

    by_place = put(jnp.where(live, place, -1), 1 + slot + image * 256 + swap * 4096)
    by_slot = put(slot, jnp.where(asked, 1 + sends, 0))
    places_row = put(slot, jnp.where(live, place, 0))
    row = lax.broadcasted_iota(I32, (8, 128), 0)
    out = jnp.where(row == 0, by_place, jnp.where(row == 1, by_slot, jnp.where(row == 2, places_row, count)))
    return out


def meet_kernel(pairs, pair_count, wa, wv, wo, wh, gain, wd, tab, waT, wvT, woT, whT, wdT, gcol, told, near, ssem, rsem):
    me, sub, others, peers = places()
    own, out = own_rows(pairs[...], pair_count[0], me, lax.axis_size("img"))
    told[...] = jnp.broadcast_to(out, (8, 128))
    greet(others, [])
    copies = [send(told, near.at[t ^ 1], ssem.at[t], rsem.at[t ^ 1], {"img": others[t]}) for t in range(REACH)]
    for copy in copies:
        copy.start()
    prepare(wa, wv, wo, wh, gain, wd, waT, wvT, woT, whT, wdT, gcol)
    for copy in copies:
        copy.wait()
    row = lax.broadcasted_iota(I32, (8, 128), 0)
    table = jnp.zeros((8, 128), I32)
    for t in range(REACH):
        table = jnp.where(row == t, near[t], table)
    tab[...] = plan_rows(own, table, pair_count[0])


def sent_image(tab, t, u):
    return tab[1, t * 8 + u]


def fetch_kernel(tab, desc, counts, visible, wa, wm, waT, wvT, woT, whT, wdT, gcol, own, xj, okeep, jkeep, dmine, dother, sc, ident, zst, zland, zms, zml, yst, yms, yml, omask, zsem, zrem, ysem, yrem, osem, orem):
    me, sub, others, peers = places()
    rows = pl.ds(pl.multiple_of(sub * ROWS, ROWS), ROWS)
    ident[...] = eye(256)
    w = dict(wa=wa, wm=wm, waT=waT, wvT=wvT, woT=woT, whT=whT, wdT=wdT, gcol=gcol, ident=ident)
    for a in range(OWN):
        own[a, rows, :] = desc[a]
    image = lax.broadcasted_iota(I32, (OWN, ROWS), 0)
    found = jnp.zeros((OWN, ROWS), I32)
    for a in range(OWN):
        found = jnp.where(image == a, counts[a], found)
    spot = lax.broadcasted_iota(I32, (OWN, ROWS), 1) + sub * ROWS
    kept = jnp.where((spot < found) & (visible[...] > 0), 1.0, 0.0)
    wide = jnp.concatenate([kept] * SUBS, axis=1)
    lane = lax.broadcasted_iota(I32, (OWN, KEYS), 1)
    wide = jnp.where((lane >= sub * ROWS) & (lane < sub * ROWS + ROWS), wide, 0.0)
    omask[0] = wide
    greet(others, peers)
    zcopies = []
    for t in (4, 5, 2, 3, 0, 1):
        line = lax.broadcasted_iota(I32, (8, KEYS), 0)
        masks = jnp.zeros((8, KEYS), F32)
        for u in range(MOST):
            which = jnp.maximum(sent_image(tab, t, u) - 1, 0)
            zst[t, u] = desc[which]
            masks = jnp.where(line == u, row_of(wide, which), masks)
        zms[t] = masks
        to = {"img": others[t]}
        zcopies.append(send(zst.at[t], zland.at[t ^ 1], zsem.at[0, t], zrem.at[0, t ^ 1], to))
        zcopies.append(send(zms.at[t], zml.at[t ^ 1], zsem.at[1, t], zrem.at[1, t ^ 1], to))
        zcopies[-2].start()
        zcopies[-1].start()
    ocopies = []
    for d in range(1, SUBS):
        to = {"sub": peers[d - 1]}
        mine = own.at[:, rows, :]
        ocopies.append(send(mine, mine, osem.at[0, d - 1], orem.at[0, d - 1], to))
        ocopies.append(send(omask.at[0], omask.at[d], osem.at[1, d - 1], orem.at[1, d - 1], to))
    for copy in ocopies:
        copy.start()
    for copy in zcopies:
        copy.wait()
    ycopies = []
    line = lax.broadcasted_iota(I32, (JOBS, KEYS), 0)
    zmasks = jnp.concatenate([zml[t] for t in range(REACH)], axis=0)
    slots = [[None] * SUBS for _ in range(JOBS)]
    for d in range(SUBS):
        worker = sub if d == 0 else peers[d - 1]
        masks = jnp.zeros((JOBS, KEYS), F32)
        for q in range(JOBS):
            slots[q][d] = jnp.maximum((tab[0, q * SUBS + worker] & 255) - 1, 0)
            masks = jnp.where(line == q, row_of(zmasks, slots[q][d]), masks)
        yms[d] = masks
    mcopies = []
    for d in range(1, SUBS):
        mcopies.append(send(yms.at[d], yml.at[d - 1], ysem.at[JOBS, d - 1], yrem.at[JOBS, d - 1], {"sub": peers[d - 1]}))
        mcopies[-1].start()
    def hand_out(q):
        for d in range(1, SUBS):
            yst[d - 1, q] = zland[slots[q][d] >> 3, slots[q][d] & 7]
            copy = send(yst.at[d - 1, q], xj.at[q, rows, :], ysem.at[q, d - 1], yrem.at[q, d - 1], {"sub": peers[d - 1]})
            copy.start()
            ycopies.append(copy)
        xj[q, rows, :] = zland[slots[q][0] >> 3, slots[q][0] & 7]

    for q in range(EARLY):
        hand_out(q)
    for copy in ocopies:
        copy.wait()
    okeep[...] = omask[0] + omask[1] + omask[2] + omask[3]
    for copy in mcopies:
        copy.wait()
    jkeep[...] = yms[0] + yml[0] + yml[1] + yml[2]
    for copy in ycopies:
        copy.wait()
    for q in range(EARLY, JOBS):
        hand_out(q)
    outs = do_scores(list(range(EARLY)), tab, sub, own, xj, okeep, jkeep, w)
    for q, out in enumerate(outs):
        dmine[q], dother[q], sc[q] = out
    for copy in ycopies[3 * EARLY :]:
        copy.wait()


def work_kernel(tab, own, xj, okeep, jkeep, bucket, wa, wm, waT, wvT, woT, whT, wdT, gcol, dmine, dother, mm, mo, ident, sc):
    sub = lax.axis_index("sub")
    ident[...] = eye(256)
    w = dict(wa=wa, wm=wm, waT=waT, wvT=wvT, woT=woT, whT=whT, wdT=wdT, gcol=gcol, ident=ident)
    n = ((tab[3, 0] + (SUBS - 1) - sub) >> 2) - FIXED
    binv = bucket[...] * LOG2E

    def scores(ps):
        outs = do_scores([FIXED + p for p in ps], tab, sub, own, xj, okeep, jkeep, w)
        for p, out in zip(ps, outs):
            dmine[p], dother[p], sc[p] = out

    def masses(ps):
        outs = do_masses([FIXED + p for p in ps], [(sc, p) for p in ps], tab, sub, okeep, jkeep, binv, ident[...])
        for p, (a, b) in zip(ps, outs):
            mm[p] = jnp.broadcast_to(a, (8, KEYS))
            mo[p] = jnp.broadcast_to(b, (8, KEYS))

    @pl.loop(0, n >> 1)
    def _(p):
        scores([2 * p, 2 * p + 1])
        masses([2 * p, 2 * p + 1])

    @pl.when((n & 1) == 1)
    def _():
        scores([n - 1])
        masses([n - 1])


def give_kernel(
    tab, own, xj, okeep, jkeep, bucket, wa, wm, waT, wvT, woT, whT, wdT, gcol, dmine0, dother0, sc0, dmine2, dother2, mm2, mo2,
    upd, mass, ident, dmine1, dother1, sc1, yb, ymst, yml, zst, zms, zret, zmr, parts, got, mparts, mgot,
    ysem, yrem, zsem, zrem, osem, orem,
):
    me, sub, others, peers = places()
    rows = pl.ds(pl.multiple_of(sub * ROWS, ROWS), ROWS)
    ident[...] = eye(256)
    w = dict(wa=wa, wm=wm, waT=waT, wvT=wvT, woT=woT, whT=whT, wdT=wdT, gcol=gcol, ident=ident)
    binv = bucket[...] * LOG2E
    mline = lax.broadcasted_iota(I32, (JOBS, KEYS), 0)

    def held(q, parts):
        if q < EARLY:
            return parts[0], q
        if q < FIXED:
            return parts[1], q - EARLY
        return parts[2], q - FIXED

    greet(others, peers)
    ycopies = []

    def hand_back(q):
        ref, at = held(q, (dother0, dother1, dother2))
        for d in range(1, SUBS):
            p = peers[d - 1]
            part = ref.at[at, pl.ds(pl.multiple_of(p * ROWS, ROWS), ROWS), :]
            ycopies.append(send(part, yb.at[q, sub], ysem.at[q, d - 1], yrem.at[q, d - 1], {"sub": p}))
            ycopies[-1].start()
        yb[q, sub] = ref[at, rows, :]

    for q in list(range(EARLY)) + list(range(FIXED, JOBS)):
        hand_back(q)
    outs = do_scores(list(range(EARLY, FIXED)), tab, sub, own, xj, okeep, jkeep, w)
    for at, out in enumerate(outs):
        dmine1[at], dother1[at], sc1[at] = out
        hand_back(EARLY + at)
    n = (tab[3, 0] + (SUBS - 1) - sub) >> 2
    owners = [jnp.where(q < n, job_of(tab, q, sub)[0], -1) for q in range(JOBS)]
    for a in range(OWN):
        for s in range(SUBS):
            value = jnp.zeros((ROWS, D), F32)
            for q in range(JOBS):
                ref, at = held(q, (dmine0, dmine1, dmine2))
                value = value + jnp.where(owners[q] == a, ref[at, s * ROWS : s * ROWS + ROWS, :].astype(F32), 0.0)
            parts[s, a] = value.astype(BF)
    for copy in ycopies:
        copy.wait()
    zcopies = [None] * REACH
    for t in (4, 5, 2, 3, 0, 1):
        for u in range(MOST):
            place = tab[2, t * 8 + u]
            zst[t, u] = yb[place >> 2, place & 3]
        zcopies[t] = send(zst.at[t], zret.at[t ^ 1], zsem.at[0, t], zrem.at[0, t ^ 1], {"img": others[t]})
        zcopies[t].start()
    ocopies = []
    for d in range(1, SUBS):
        to = {"sub": peers[d - 1]}
        ocopies.append(send(parts.at[peers[d - 1]], got.at[d - 1], osem.at[0, d - 1], orem.at[0, d - 1], to))
        ocopies[-1].start()
    fixed = list(range(FIXED))
    masses = do_masses(fixed, [held(q, (sc0, sc1)) for q in fixed], tab, sub, okeep, jkeep, binv, ident[...])
    mine = [masses[q][0] if q < FIXED else mm2[q - FIXED, 0:1, :] for q in range(JOBS)]
    away = [masses[q][1] if q < FIXED else mo2[q - FIXED, 0:1, :] for q in range(JOBS)]
    table = jnp.zeros((JOBS, KEYS), F32)
    for q in range(JOBS):
        table = jnp.where(mline == q, away[q], table)
    ymst[...] = table
    yml[sub] = table
    ymcopies = []
    for d in range(1, SUBS):
        ymcopies.append(send(ymst, yml.at[sub], ysem.at[JOBS, d - 1], yrem.at[JOBS, d - 1], {"sub": peers[d - 1]}))
        ymcopies[-1].start()
    table = jnp.zeros((OWN, KEYS), F32)
    for a in range(OWN):
        for q in range(JOBS):
            table = table + jnp.where((mline == a) & (owners[q] == a), mine[q], 0.0)
    mparts[...] = table
    for d in range(1, SUBS):
        copy = send(mparts, mgot.at[d - 1], osem.at[1, d - 1], orem.at[1, d - 1], {"sub": peers[d - 1]})
        copy.start()
        ocopies.append(copy)
    for copy in ocopies[: SUBS - 1]:
        copy.wait()
    for t in range(REACH):
        zcopies[t].wait()
    wants = [(t, u, sent_image(tab, t, u) - 1) for t in range(REACH) for u in range(MOST)]
    for a in range(OWN):
        value = parts[sub, a].astype(F32)
        for d in range(SUBS - 1):
            value = value + got[d, a].astype(F32)
        for t, u, which in wants:
            value = value + jnp.where(which == a, zret[t, u].astype(F32), 0.0)
        upd[a] = value.astype(BF)
    for copy in ymcopies:
        copy.wait()
    ymasses = jnp.concatenate([yml[s] for s in range(SUBS)], axis=0)
    zmcopies = []
    for t in (4, 5, 2, 3, 0, 1):
        back = jnp.zeros((8, KEYS), F32)
        for u in range(MOST):
            place = tab[2, t * 8 + u]
            back = jnp.where(mline == u, row_of(ymasses, (place & 3) * JOBS + (place >> 2)), back)
        zms[t] = back
        zmcopies.append(send(zms.at[t], zmr.at[t ^ 1], zsem.at[1, t], zrem.at[1, t ^ 1], {"img": others[t]}))
        zmcopies[-1].start()
    for copy in ocopies[SUBS - 1 :]:
        copy.wait()
    for copy in zmcopies:
        copy.wait()
    total = mparts[...] + mgot[0] + mgot[1] + mgot[2]
    for a in range(OWN):
        extra = jnp.zeros((1, KEYS), F32)
        for t, u, which in wants:
            extra = extra + jnp.where(which == a, zmr[t, u : u + 1, :], 0.0)
        total = total + jnp.where(mline == a, extra, 0.0)
    out = jnp.zeros((OWN, ROWS), F32)
    for s in range(SUBS):
        out = jnp.where(sub == s, total[:, s * ROWS : s * ROWS + ROWS], out)
    mass[...] = out


VM = pl.BlockSpec(memory_space=pltpu.VMEM)
SM = pl.BlockSpec(memory_space=pltpu.SMEM)
DMA = pltpu.SemaphoreType.DMA


def shape(dims, kind=BF):
    return jax.ShapeDtypeStruct(dims, kind)


def talk(number):
    return pltpu.CompilerParams(collective_id=number, has_side_effects=True, vmem_limit_bytes=LIMIT)


def local(descriptors, counts, visible, pair_list, pair_count, w_attend, w_value, w_output, w_hidden, norm_gain, w_down, w_match, unassigned_bucket):
    V = pltpu.VMEM
    tab, *ready = pl.pallas_call(
        meet_kernel,
        out_shape=(shape((8, 128), I32), *[shape((256, 256))] * 3, shape((512, 512)), shape((256, 512)), shape((512, 128), F32)),
        in_specs=[VM, SM] + [VM] * 6,
        out_specs=(VM,) * 7,
        scratch_shapes=[V((8, 128), I32), V((REACH, 8, 128), I32), DMA((REACH,)), DMA((REACH,))],
        compiler_params=talk(0),
    )(pair_list, pair_count, w_attend, w_value, w_output, w_hidden, norm_gain.reshape(1, -1), w_down)
    own, xj, okeep, jkeep, *early = pl.pallas_call(
        fetch_kernel,
        out_shape=(
            shape((OWN, KEYS, D)), shape((JOBS, KEYS, D)), shape((OWN, KEYS), F32), shape((JOBS, KEYS), F32),
            shape((EARLY, KEYS, D)), shape((EARLY, KEYS, D)), shape((EARLY, KEYS, KEYS), F32),
        ),
        in_specs=[SM, VM, SM, VM] + [VM] * 8,
        out_specs=(VM,) * 7,
        scratch_shapes=[
            V((256, 256), BF),
            V((REACH, MOST, ROWS, D), BF), V((REACH, MOST, ROWS, D), BF), V((REACH, 8, KEYS), F32), V((REACH, 8, KEYS), F32),
            V((SUBS - 1, JOBS, ROWS, D), BF), V((SUBS, JOBS, KEYS), F32), V((SUBS - 1, JOBS, KEYS), F32), V((SUBS, OWN, KEYS), F32),
            DMA((2, REACH)), DMA((2, REACH)), DMA((JOBS + 1, SUBS - 1)), DMA((JOBS + 1, SUBS - 1)), DMA((2, SUBS - 1)), DMA((2, SUBS - 1)),
        ],
        compiler_params=talk(1),
    )(tab, descriptors, counts, visible, w_attend, w_match, *ready)
    common = (tab, own, xj, okeep, jkeep, unassigned_bucket.reshape(1, 1), w_attend, w_match, *ready)
    late = JOBS - FIXED
    rest = pl.pallas_call(
        work_kernel,
        out_shape=(shape((late, KEYS, D)), shape((late, KEYS, D)), shape((late, 8, KEYS), F32), shape((late, 8, KEYS), F32)),
        in_specs=[SM] + [VM] * 13,
        out_specs=(VM,) * 4,
        scratch_shapes=[V((256, 256), BF), V((late, KEYS, KEYS), F32)],
        compiler_params=pltpu.CompilerParams(vmem_limit_bytes=LIMIT),
    )(*common)
    mid = FIXED - EARLY
    return pl.pallas_call(
        give_kernel,
        out_shape=(shape((OWN, ROWS, D)), shape((OWN, ROWS), F32)),
        in_specs=[SM] + [VM] * 20,
        out_specs=(VM, VM),
        scratch_shapes=[
            V((256, 256), BF), V((mid, KEYS, D), BF), V((mid, KEYS, D), BF), V((mid, KEYS, KEYS), F32),
            V((JOBS, SUBS, ROWS, D), BF), V((JOBS, KEYS), F32), V((SUBS, JOBS, KEYS), F32),
            V((REACH, MOST, ROWS, D), BF), V((REACH, 8, KEYS), F32), V((REACH, MOST, ROWS, D), BF), V((REACH, 8, KEYS), F32),
            V((SUBS, OWN, ROWS, D), BF), V((SUBS - 1, OWN, ROWS, D), BF), V((OWN, KEYS), F32), V((SUBS - 1, OWN, KEYS), F32),
            DMA((JOBS + 1, SUBS - 1)), DMA((JOBS + 1, SUBS - 1)), DMA((2, REACH)), DMA((2, REACH)), DMA((2, SUBS - 1)), DMA((2, SUBS - 1)),
        ],
        compiler_params=talk(2),
    )(*common, *early, *rest)


def solution(mesh):
    placed = (P("img", "sub", None), P("img"), P("img", "sub"), P("img", None), P("img")) + (P(),) * 8
    return jax.shard_map(
        local, mesh=mesh, in_specs=placed, out_specs=(P("img", "sub", None), P("img", "sub")), check_vma=False
    )
```

```python
import math

import jax
import jax.numpy as jnp
from jax import lax
from jax.experimental import pallas as pl
from jax.experimental.pallas import tpu as pltpu
from jax.sharding import PartitionSpec as P

BF = jnp.bfloat16
F32 = jnp.float32
I32 = jnp.int32
LOG2E = 1.4426950408889634
FORGET = 30.0 * LOG2E
HEADS = 4
ITERS = 10
KEYS = 256
D = 256
WIN = 3
REACH = 2 * WIN
MOST = 6
OWN = 8
ROWS = 64
SUBS = 4
JOBS = 8
FIXED = 4
PARTS = 4
PART = ROWS // PARTS
HALF = ROWS // 2
MESH = pl.DeviceIdType.MESH
LIMIT = 56 * 2**20


def nn(a, b):
    return lax.dot_general(a, b, (((1,), (0,)), ((), ())), preferred_element_type=F32)


def nt(a, b):
    return lax.dot_general(a, b, (((1,), (1,)), ((), ())), preferred_element_type=F32)


def eye(n):
    up = lax.broadcasted_iota(I32, (n, n), 0)
    return (up == lax.broadcasted_iota(I32, (n, n), 1)).astype(BF)


def to_col(row, ident):
    return nt(ident, jnp.broadcast_to(row, (128, row.shape[1])))


def prepare(wa, wv, wo, wh, gain, wd, waT, wvT, woT, whT, wdT, gcol):
    ident = eye(256)
    waT[...] = nt(ident, wa[...]).astype(BF)
    wvT[...] = nt(ident, wv[...]).astype(BF)
    woT[...] = nt(ident, wo[...]).astype(BF)
    for a in range(0, 512, 256):
        for b in range(0, 512, 256):
            whT[a : a + 256, b : b + 256] = nt(ident, wh[b : b + 256, a : a + 256]).astype(BF)
    for b in range(0, 512, 256):
        wdT[:, b : b + 256] = nt(ident, wd[b : b + 256, :]).astype(BF)
    same = lax.broadcasted_iota(I32, (128, 128), 0) == lax.broadcasted_iota(I32, (128, 128), 1)
    for q in range(0, 512, 128):
        spread = jnp.broadcast_to(gain[:, q : q + 128], (128, 128))
        column = jnp.sum(jnp.where(same, spread, 0.0), axis=1, keepdims=True)
        gcol[q : q + 128, :] = jnp.broadcast_to(column, (128, 128))


def attention(sides, ahead=4, behind=2):
    ones = jnp.ones((16, KEYS), BF)
    steps = [(h, s) for h in range(HEADS) for s in range(len(sides))]

    def similarity(h, s):
        a_other, aT_self, _, bias = sides[s]
        sl = slice(h * 64, h * 64 + 64)
        value = nn(a_other[:, sl], aT_self[sl]) * (LOG2E / 8.0) + bias
        return value, jnp.max(value, axis=0, keepdims=True)

    def finish(r):
        return (r[:64] * (1.0 / r[64:65])).astype(BF)

    waiting = [similarity(*step) for step in steps[:ahead]]
    late = []
    outs = {}
    for i, (h, s) in enumerate(steps):
        if i + ahead < len(steps):
            waiting.append(similarity(*steps[i + ahead]))
        value, top = waiting.pop(0)
        e = jnp.exp2(value - top).astype(BF)
        late.append(((h, s), nn(jnp.concatenate([sides[s][2][h * 64 : h * 64 + 64], ones], axis=0), e)))
        if len(late) > behind:
            step, r = late.pop(0)
            outs[step] = finish(r)
    for step, r in late:
        outs[step] = finish(r)
    return [jnp.concatenate([outs[h, s] for h in range(HEADS)], axis=0) for s in range(len(sides))]


def refine(xs, msgs, w):
    half = math.sqrt(0.5)
    gain = jnp.concatenate([w["gcol"][...]] * 2, axis=1) * half

    def hidden(i):
        sentT = nn(w["woT"][...], msgs[i]).astype(BF)
        return nt(w["whT"][:, :256], xs[i]) + nn(w["whT"][:, 256:], sentT)

    outs = []
    later = hidden(0)
    for i in range(len(xs)):
        hid = later
        if i + 1 < len(xs):
            later = hidden(i + 1)
        mean = jnp.sum(hid, axis=0, keepdims=True) * (1.0 / 512)
        cen = hid - mean
        var = jnp.sum(cen * cen, axis=0, keepdims=True) * (1.0 / 512)
        z = cen * lax.rsqrt(var + 1e-5) * gain
        outs.append(nn(w["wdT"][...], ((half * z) * (1.0 + lax.erf(z))).astype(BF)).astype(BF))
    return outs


def pair_scores(pairs, w):
    ident = w["ident"][...]
    xs, biases = [], []
    for xi, ki, xj, kj in pairs:
        xs += [xi, xj]
        for keep in (ki, kj):
            bias = (to_col(keep, ident) - 1.0) * 1e30
            biases.append(jnp.concatenate([bias, bias], axis=1))
    attend = [nn(x, w["wa"][...]).astype(BF) for x in xs]
    attendT = [nt(w["waT"][...], x).astype(BF) for x in xs]
    valueT = [nt(w["wvT"][...], x).astype(BF) for x in xs]
    msgs = attention([(attend[i ^ 1], attendT[i], valueT[i ^ 1], biases[i ^ 1]) for i in range(len(xs))])
    deltas = [nt(ident, d).astype(BF) for d in refine(xs, msgs, w)]
    match = [
        nn((x.astype(F32) + d.astype(F32)).astype(BF), w["wm"][...]).astype(BF) for x, d in zip(xs, deltas)
    ]
    return [
        (deltas[i], deltas[i + 1], nt(match[i], match[i + 1]) * (LOG2E / 16.0)) for i in range(0, len(xs), 2)
    ]


def marginals(ki, kj, ident):
    m = jnp.sum(ki, axis=1, keepdims=True)
    n = jnp.sum(kj, axis=1, keepdims=True)
    total = m + n
    off = -jnp.log2(jnp.maximum(total, 1.0))
    kic = to_col(ki.astype(BF), ident)
    lr = off - FORGET * (1.0 - kic)
    lc = off - FORGET * (1.0 - kj)
    lrb = jnp.log2(jnp.maximum(n, 1.0)) + off
    lcb = jnp.log2(jnp.maximum(m, 1.0)) + off
    return total, kic, lr, lc, lrb, lcb


def sink_first(c, bucket, lr, lc, lrb, lcb):
    top = jnp.maximum(jnp.max(c, axis=1, keepdims=True), bucket)
    s = jnp.sum(jnp.exp2(c - top), axis=1, keepdims=True) + jnp.exp2(bucket - top)
    f = lr - top - jnp.log2(s)
    fb = lrb - bucket - math.log2(257.0)
    halves = [jnp.sum(jnp.exp2(c[:, at : at + 128] + f), axis=0, keepdims=True) for at in (0, 128)]
    t = jnp.concatenate(halves, axis=1) + jnp.exp2(bucket + fb)
    tb = jnp.sum(jnp.exp2(bucket + f), axis=0, keepdims=True)[:, :1] + jnp.exp2(bucket + fb)
    return f, fb, lc - jnp.log2(t), lcb - jnp.log2(tb)


def sink_next(c, at, bucket, lr, lc, lrb, lcb, state):
    f, fb, g, gb = state
    eb = jnp.exp2(bucket + fb + g)
    ebb = jnp.exp2(bucket + fb + gb)
    dub = lrb - jnp.log2(jnp.sum(eb, axis=1, keepdims=True) + ebb)
    ub = jnp.exp2(dub)
    p0 = jnp.exp2(c[at, :, :128] + g[:, :128] + f)
    p1 = jnp.exp2(c[at, :, 128:] + g[:, 128:] + f)
    b = jnp.exp2((bucket + gb) + f)
    du = lr - jnp.log2(jnp.sum(p0 + p1, axis=1, keepdims=True) + b)
    u = jnp.exp2(du)
    t = [jnp.sum(p * u, axis=0, keepdims=True) for p in (p0, p1)]
    t = eb * ub + jnp.concatenate(t, axis=1)
    tb = ebb * ub + jnp.sum(b * u, axis=0, keepdims=True)[:, :1]
    return f + du, fb + dub, g + lc - jnp.log2(t), gb + lcb - jnp.log2(tb)


def sink_out(c, total, kic, kj, state):
    f, fb, g, gb = state
    p0 = jnp.exp2(c[:, :128] + g[:, :128] + f)
    p1 = jnp.exp2(c[:, 128:] + g[:, 128:] + f)
    mi = (jnp.sum(p0 + p1, axis=1, keepdims=True) * total * kic).astype(BF)
    halves = [jnp.sum(p, axis=0, keepdims=True) for p in (p0, p1)]
    mj = (jnp.concatenate(halves, axis=1) * total * kj).astype(BF)
    first = (lax.broadcasted_iota(I32, (16, 128), 1) == 0).astype(BF)
    return nt(first, mi)[:1], mj.astype(F32)


def row_of(block, index):
    at = lax.broadcasted_iota(I32, block.shape, 0)
    return jnp.sum(jnp.where(at == index, block, 0.0), axis=0, keepdims=True)


def job_of(tab, q, sub):
    code = tab[0, q * SUBS + sub]
    return (code >> 8) & 7, (code >> 12) & 1


def do_scores(jobs, tab, sub, own, xj, okeep, jkeep, w):
    pairs, swaps = [], []
    for q in jobs:
        mine, swap = job_of(tab, q, sub)
        xm, xo = own[mine], xj[q]
        km = row_of(okeep[...], mine)
        ko = row_of(jkeep[...], q)
        ki = jnp.where(swap == 1, ko, km).astype(BF)
        kj = jnp.where(swap == 1, km, ko).astype(BF)
        pairs.append((jnp.where(swap == 1, xo, xm), ki, jnp.where(swap == 1, xm, xo), kj))
        swaps.append(swap)
    return [
        (jnp.where(swap == 1, dj, di), jnp.where(swap == 1, di, dj), scores)
        for swap, (di, dj, scores) in zip(swaps, pair_scores(pairs, w))
    ]


def do_masses(jobs, sc, tab, sub, okeep, jkeep, bucket, ident):
    swaps, margs, states, kjs = [], [], [], []
    for q, (ref, at) in zip(jobs, sc):
        mine, swap = job_of(tab, q, sub)
        km = row_of(okeep[...], mine)
        ko = row_of(jkeep[...], q)
        ki = jnp.where(swap == 1, ko, km)
        kj = jnp.where(swap == 1, km, ko)
        marg = marginals(ki, kj, ident)
        swaps.append(swap)
        kjs.append(kj)
        margs.append(marg)
        states.append(sink_first(ref[at], bucket, *marg[2:]))

    def sweep(_, states):
        return [sink_next(ref, at, bucket, *m[2:], s) for (ref, at), m, s in zip(sc, margs, states)]

    states = lax.fori_loop(0, ITERS - 1, sweep, states)
    outs = []
    for (ref, at), m, s, kj, swap in zip(sc, margs, states, kjs, swaps):
        a, b = sink_out(ref[at], m[0], m[1], kj, s)
        outs.append((jnp.where(swap == 1, b, a), jnp.where(swap == 1, a, b)))
    return outs


def step_of(turn):
    return (turn // 2 + 1) * (1 - 2 * (turn % 2))


def places():
    n = lax.axis_size("img")
    me = lax.axis_index("img")
    sub = lax.axis_index("sub")
    others = [lax.rem(me + step_of(t) + n, n) for t in range(REACH)]
    peers = [lax.rem(sub + d, SUBS) for d in range(1, SUBS)]
    return me, sub, others, peers


def greet(others, peers):
    barrier = pltpu.get_barrier_semaphore()
    for h in others:
        pl.semaphore_signal(barrier, inc=1, device_id={"img": h}, device_id_type=MESH)
    for s in peers:
        pl.semaphore_signal(barrier, inc=1, device_id={"sub": s}, device_id_type=MESH)
    pl.semaphore_wait(barrier, len(others) + len(peers))


def send(src, dst, ssem, rsem, to):
    return pltpu.make_async_remote_copy(
        src_ref=src, dst_ref=dst, send_sem=ssem, recv_sem=rsem, device_id=to, device_id_type=MESH
    )


def own_rows(pairs, live_count, me, img_count):
    first = pairs[:, 0:1]
    second = pairs[:, 1:2]
    slots = pairs.shape[0]
    row_ids = lax.broadcasted_iota(I32, (slots, 1), 0)
    ahead = (second >> 3) - me
    ahead = jnp.where(ahead < 0, ahead + img_count, ahead)
    turn = jnp.where(ahead <= WIN, 2 * (ahead - 1), 2 * (img_count - ahead - 1) + 1)
    live = row_ids < live_count
    key = jnp.where(live, turn, 15)
    code = 1 + (first & 7) * 8 + (second & 7)
    up = lax.broadcasted_iota(I32, (slots, slots), 0)
    across = lax.broadcasted_iota(I32, (slots, slots), 1)
    key_row = jnp.sum(jnp.where(up == across, key, 0), axis=0, keepdims=True)
    rank = jnp.sum(jnp.where((key_row == key) & (across < up), 1, 0), axis=1, keepdims=True)
    lanes = lax.broadcasted_iota(I32, (slots, 128), 1)
    lane = lax.broadcasted_iota(I32, (1, 128), 1)
    rows = []
    for k in (key, key ^ 1):
        at = jnp.where(live, k * 8 + rank, -1)
        codes = jnp.sum(jnp.where(lanes == at, code, 0), axis=0, keepdims=True)
        counts = jnp.sum(jnp.where((lanes == 64 + k) & live, 1, 0), axis=0, keepdims=True)
        row = codes + counts
        rows.append(jnp.where((lane >= 80) & (lane < 88), live_count, row))
    return rows


def plan_rows(own, near, live_count):
    r8 = lax.broadcasted_iota(I32, (8, 128), 0)
    l8 = lax.broadcasted_iota(I32, (8, 128), 1)
    mine = jnp.where(l8 < 64, l8 >> 3, l8 & 7)
    from_near = jnp.sum(jnp.where((mine == r8) & (r8 < REACH), near, 0), axis=0, keepdims=True)
    slots = 64
    lanes = lax.broadcasted_iota(I32, (slots, 128), 1)
    slot = lax.broadcasted_iota(I32, (slots, 1), 0)
    turn = slot >> 3
    u = slot & 7
    own_all = jnp.broadcast_to(own, (slots, 128))
    near_all = jnp.broadcast_to(from_near, (slots, 128))

    def pick(table, lane):
        return jnp.sum(jnp.where(lanes == lane, table, 0), axis=1, keepdims=True)

    n_own = pick(own_all, 64 + turn)
    n_near = pick(near_all, 64 + turn)
    l_near = pick(near_all, 80 + turn)

    def sixth(value):
        return (jnp.maximum(value, 0) * 43) >> 8

    give = jnp.maximum(jnp.minimum(jnp.minimum(sixth(live_count - l_near), n_own), MOST - n_near), 0)
    take = jnp.maximum(jnp.minimum(jnp.minimum(sixth(l_near - live_count), n_near), MOST - n_own), 0)
    kept = n_own - give
    near_kept = n_near - take
    own_code = pick(own_all, turn * 8 + u) - 1
    near_code = pick(near_all, turn * 8 + u) - 1
    taken_code = pick(near_all, turn * 8 + near_kept + u - kept) - 1
    given_code = pick(own_all, turn * 8 + kept + u - near_kept) - 1
    live = (u < kept + take) & (turn < REACH)
    image = jnp.where(u < kept, own_code >> 3, taken_code & 7)
    swap = jnp.where(u < kept, 0, 1)
    asked = (u < near_kept + give) & (turn < REACH)
    sends = jnp.where(u < near_kept, near_code & 7, given_code >> 3)
    eye64 = lax.broadcasted_iota(I32, (slots, slots), 0) == lax.broadcasted_iota(I32, (slots, slots), 1)
    live_row = jnp.sum(jnp.where(eye64, jnp.where(live, 1, 0), 0), axis=0, keepdims=True)
    short = lax.broadcasted_iota(I32, (slots, slots), 1)
    place = jnp.sum(jnp.where(short < slot, live_row, 0), axis=1, keepdims=True)
    count = jnp.sum(live_row, axis=1, keepdims=True)

    def put(lane, value):
        return jnp.sum(jnp.where(lanes == lane, value, 0), axis=0, keepdims=True)

    by_place = put(jnp.where(live, place, -1), 1 + slot + image * 256 + swap * 4096)
    by_slot = put(slot, jnp.where(asked, 1 + sends, 0))
    places_row = put(slot, jnp.where(live, place, 0))
    row = lax.broadcasted_iota(I32, (8, 128), 0)
    out = jnp.where(row == 0, by_place, jnp.where(row == 1, by_slot, jnp.where(row == 2, places_row, count)))
    return out


def own_mask(counts, visible, sub):
    image = lax.broadcasted_iota(I32, (OWN, ROWS), 0)
    found = jnp.zeros((OWN, ROWS), I32)
    for a in range(OWN):
        found = jnp.where(image == a, counts[a], found)
    spot = lax.broadcasted_iota(I32, (OWN, ROWS), 1) + sub * ROWS
    kept = jnp.where((spot < found) & (visible[...] > 0), 1.0, 0.0)
    return my_lanes(jnp.concatenate([kept] * SUBS, axis=1), sub)


def my_lanes(wide, sub):
    lane = lax.broadcasted_iota(I32, wide.shape, 1)
    return jnp.where((lane >= sub * ROWS) & (lane < sub * ROWS + ROWS), wide, 0.0)


def meet_kernel(
    pairs, pair_count, desc, counts, visible, wa, wv, wo, wh, gain, wd,
    tab, waT, wvT, woT, whT, wdT, gcol, upper, okeep, told, near, omask, ssem, rsem, osem, orem,
):
    me, sub, others, peers = places()
    omask[0] = own_mask(counts, visible, sub)
    greet(others, peers)
    ocopies = []
    for d in range(1, SUBS):
        to = {"sub": peers[d - 1]}
        ocopies.append(send(omask.at[0], omask.at[d], osem.at[1, d - 1], orem.at[1, d - 1], to))
        ocopies.append(send(desc.at[:, 0:HALF, :], upper.at[sub], osem.at[0, d - 1], orem.at[0, d - 1], to))
    own, out = own_rows(pairs[...], pair_count[0], me, lax.axis_size("img"))
    told[...] = jnp.broadcast_to(out, (8, 128))
    copies = [send(told, near.at[t ^ 1], ssem.at[t], rsem.at[t ^ 1], {"img": others[t]}) for t in range(REACH)]
    for copy in copies + ocopies:
        copy.start()
    upper[sub] = desc[:, 0:HALF, :]
    prepare(wa, wv, wo, wh, gain, wd, waT, wvT, woT, whT, wdT, gcol)
    for copy in copies:
        copy.wait()
    row = lax.broadcasted_iota(I32, (8, 128), 0)
    table = jnp.zeros((8, 128), I32)
    for t in range(REACH):
        table = jnp.where(row == t, near[t], table)
    tab[...] = plan_rows(own, table, pair_count[0])
    for copy in ocopies:
        copy.wait()
    okeep[...] = omask[0] + omask[1] + omask[2] + omask[3]


def sent_image(tab, t, u):
    return tab[1, t * 8 + u]


def fetch_kernel(
    tab, desc, upper, okeep, own, xj, jkeep, zst, zl0, zl1, zl2, zl3, zms, zml, yst, yl, yms, yml, lower,
    zsem, zrem, ysem, yrem, osem, orem,
):
    me, sub, others, peers = places()
    zland = (zl0, zl1, zl2, zl3)
    wide = my_lanes(okeep[...], sub)
    greet(others, peers)
    order = (4, 5, 2, 3, 0, 1)
    line = lax.broadcasted_iota(I32, (8, KEYS), 0)
    zmcopies = []
    for t in order:
        masks = jnp.zeros((8, KEYS), F32)
        for u in range(MOST):
            masks = jnp.where(line == u, row_of(wide, jnp.maximum(sent_image(tab, t, u) - 1, 0)), masks)
        zms[t] = masks
        zmcopies.append(
            send(zms.at[t], zml.at[t ^ 1], zsem.at[PARTS, t], zrem.at[PARTS, t ^ 1], {"img": others[t]})
        )
        zmcopies[-1].start()
    zcopies = []
    for c in range(PARTS):
        zcopies.append([])
        for t in order:
            for u in range(MOST):
                which = jnp.maximum(sent_image(tab, t, u) - 1, 0)
                zst[c, t, u] = desc[which, c * PART : c * PART + PART, :]
            copy = send(zst.at[c, t], zland[c].at[t ^ 1], zsem.at[c, t], zrem.at[c, t ^ 1], {"img": others[t]})
            copy.start()
            zcopies[c].append(copy)
    ocopies = []
    for d in range(1, SUBS):
        copy = send(desc.at[:, HALF:ROWS, :], lower.at[sub], osem.at[d - 1], orem.at[d - 1], {"sub": peers[d - 1]})
        copy.start()
        ocopies.append(copy)
    lower[sub] = desc[:, HALF:ROWS, :]
    for copy in zmcopies:
        copy.wait()
    zmasks = jnp.concatenate([zml[t] for t in range(REACH)], axis=0)
    slots = []
    for d in range(SUBS):
        worker = sub if d == 0 else peers[d - 1]
        slots.append([jnp.maximum((tab[0, q * SUBS + worker] & 255) - 1, 0) for q in range(JOBS)])
        masks = jnp.zeros((JOBS, KEYS), F32)
        for q in range(JOBS):
            masks = jnp.where(line == q, row_of(zmasks, slots[d][q]), masks)
        yms[d] = masks
    ycopies = []
    for d in range(1, SUBS):
        to = {"sub": peers[d - 1]}
        ycopies.append(send(yms.at[d], yml.at[d - 1], ysem.at[PARTS, d - 1], yrem.at[PARTS, d - 1], to))
        ycopies[-1].start()
    for c in range(PARTS):
        for copy in zcopies[c]:
            copy.wait()
        for d in range(1, SUBS):
            for q in range(JOBS):
                yst[c, d - 1, q] = zland[c][slots[d][q] >> 3, slots[d][q] & 7]
            copy = send(yst.at[c, d - 1], yl.at[c, sub], ysem.at[c, d - 1], yrem.at[c, d - 1], {"sub": peers[d - 1]})
            copy.start()
            ycopies.append(copy)
        for q in range(JOBS):
            yl[c, sub, q] = zland[c][slots[0][q] >> 3, slots[0][q] & 7]
    for copy in ocopies:
        copy.wait()
    for s in range(SUBS):
        own[:, s * ROWS : s * ROWS + HALF, :] = upper[s]
        own[:, s * ROWS + HALF : s * ROWS + ROWS, :] = lower[s]
    for copy in ycopies:
        copy.wait()
    for s in range(SUBS):
        for c in range(PARTS):
            at = s * ROWS + c * PART
            xj[:, at : at + PART, :] = yl[c, s]
    jkeep[...] = yms[0] + yml[0] + yml[1] + yml[2]


def work_kernel(
    tab, own, xj, okeep, jkeep, bucket, wa, wm, waT, wvT, woT, whT, wdT, gcol, dmine, dother, sc, mm, mo, ident, sclate
):
    sub = lax.axis_index("sub")
    ident[...] = eye(256)
    w = dict(wa=wa, wm=wm, waT=waT, wvT=wvT, woT=woT, whT=whT, wdT=wdT, gcol=gcol, ident=ident)
    n = ((tab[3, 0] + (SUBS - 1) - sub) >> 2) - FIXED
    binv = bucket[...] * LOG2E

    def scores(qs, ref, first):
        outs = do_scores(qs, tab, sub, own, xj, okeep, jkeep, w)
        for q, out in zip(qs, outs):
            dmine[q], dother[q], ref[q - first] = out

    def late(ps):
        scores([FIXED + p for p in ps], sclate, FIXED)
        outs = do_masses([FIXED + p for p in ps], [(sclate, p) for p in ps], tab, sub, okeep, jkeep, binv, ident[...])
        for p, (a, b) in zip(ps, outs):
            mm[p] = jnp.broadcast_to(a, (8, KEYS))
            mo[p] = jnp.broadcast_to(b, (8, KEYS))

    @pl.loop(0, FIXED // 2)
    def _(p):
        scores([2 * p, 2 * p + 1], sc, 0)

    @pl.loop(0, n >> 1)
    def _(p):
        late([2 * p, 2 * p + 1])

    @pl.when((n & 1) == 1)
    def _():
        late([n - 1])


def give_kernel(
    tab, okeep, jkeep, bucket, dmine, dother, sc, mm2, mo2,
    upd, mass, ident, yb0, yb1, yb2, yb3, ymst, yml, zst, zms, zret, zmr, parts, got, mparts, mgot,
    ysem, yrem, zsem, zrem, osem, orem,
):
    me, sub, others, peers = places()
    yb = (yb0, yb1, yb2, yb3)
    ident[...] = eye(256)
    binv = bucket[...] * LOG2E
    mline = lax.broadcasted_iota(I32, (JOBS, KEYS), 0)
    order = (4, 5, 2, 3, 0, 1)

    def rows_of(p, c):
        return pl.ds(pl.multiple_of(p * ROWS + c * PART, PART), PART)

    greet(others, peers)
    ycopies = []
    for c in range(PARTS):
        ycopies.append([])
        for d in range(1, SUBS):
            p = peers[d - 1]
            copy = send(
                dother.at[:, rows_of(p, c), :], yb[c].at[sub], ysem.at[c, d - 1], yrem.at[c, d - 1], {"sub": p}
            )
            copy.start()
            ycopies[c].append(copy)
    for c in range(PARTS):
        yb[c][sub] = dother[:, rows_of(sub, c), :]
    n = (tab[3, 0] + (SUBS - 1) - sub) >> 2
    owners = [jnp.where(q < n, job_of(tab, q, sub)[0], -1) for q in range(JOBS)]
    for a in range(OWN):
        for s in range(SUBS):
            value = jnp.zeros((ROWS, D), F32)
            for q in range(JOBS):
                value = value + jnp.where(owners[q] == a, dmine[q, s * ROWS : s * ROWS + ROWS, :].astype(F32), 0.0)
            parts[s, a] = value.astype(BF)
    places_of = [[tab[2, t * 8 + u] for u in range(MOST)] for t in range(REACH)]
    zcopies = [[] for _ in range(PARTS)]

    def pass_on(c):
        for copy in ycopies[c]:
            copy.wait()
        for t in order:
            for u in range(MOST):
                zst[c, t, u] = yb[c][places_of[t][u] & 3, places_of[t][u] >> 2]
            copy = send(zst.at[c, t], zret.at[c, t ^ 1], zsem.at[c, t], zrem.at[c, t ^ 1], {"img": others[t]})
            copy.start()
            zcopies[c].append(copy)

    def some_masses(qs):
        return do_masses(qs, [(sc, q) for q in qs], tab, sub, okeep, jkeep, binv, ident[...])

    pass_on(0)
    masses = some_masses([0, 1])
    pass_on(1)
    pass_on(2)
    ocopies = []
    for d in range(1, SUBS):
        to = {"sub": peers[d - 1]}
        ocopies.append(send(parts.at[peers[d - 1]], got.at[d - 1], osem.at[0, d - 1], orem.at[0, d - 1], to))
        ocopies[-1].start()
    masses += some_masses([2, 3])
    mine = [masses[q][0] if q < FIXED else mm2[q - FIXED, 0:1, :] for q in range(JOBS)]
    away = [masses[q][1] if q < FIXED else mo2[q - FIXED, 0:1, :] for q in range(JOBS)]
    table = jnp.zeros((JOBS, KEYS), F32)
    for q in range(JOBS):
        table = jnp.where(mline == q, away[q], table)
    ymst[...] = table
    yml[sub] = table
    ymcopies = []
    for d in range(1, SUBS):
        to = {"sub": peers[d - 1]}
        ymcopies.append(send(ymst, yml.at[sub], ysem.at[PARTS, d - 1], yrem.at[PARTS, d - 1], to))
        ymcopies[-1].start()
    pass_on(3)
    table = jnp.zeros((OWN, KEYS), F32)
    for a in range(OWN):
        for q in range(JOBS):
            table = table + jnp.where((mline == a) & (owners[q] == a), mine[q], 0.0)
    mparts[...] = table
    for d in range(1, SUBS):
        copy = send(mparts, mgot.at[d - 1], osem.at[1, d - 1], orem.at[1, d - 1], {"sub": peers[d - 1]})
        copy.start()
        ocopies.append(copy)
    for copy in ymcopies:
        copy.wait()
    ymasses = jnp.concatenate([yml[s] for s in range(SUBS)], axis=0)
    zmcopies = []
    for t in order:
        back = jnp.zeros((8, KEYS), F32)
        for u in range(MOST):
            place = places_of[t][u]
            back = jnp.where(mline == u, row_of(ymasses, (place & 3) * JOBS + (place >> 2)), back)
        zms[t] = back
        to = {"img": others[t]}
        zmcopies.append(send(zms.at[t], zmr.at[t ^ 1], zsem.at[PARTS, t], zrem.at[PARTS, t ^ 1], to))
        zmcopies[-1].start()
    wants = [(t, u, sent_image(tab, t, u) - 1) for t in range(REACH) for u in range(MOST)]
    for copy in ocopies[: SUBS - 1]:
        copy.wait()
    for c in (0, 2):
        for copy in zcopies[c] + zcopies[c + 1]:
            copy.wait()
        part = slice(c * PART, c * PART + 2 * PART)
        for a in range(OWN):
            value = parts[sub, a, part].astype(F32)
            for d in range(SUBS - 1):
                value = value + got[d, a, part].astype(F32)
            for t, u, which in wants:
                come = zret[c : c + 2, t, u].reshape(2 * PART, D)
                value = value + jnp.where(which == a, come.astype(F32), 0.0)
            upd[a, part] = value.astype(BF)
    for copy in ocopies[SUBS - 1 :] + zmcopies:
        copy.wait()
    total = mparts[...] + mgot[0] + mgot[1] + mgot[2]
    for a in range(OWN):
        extra = jnp.zeros((1, KEYS), F32)
        for t, u, which in wants:
            extra = extra + jnp.where(which == a, zmr[t, u : u + 1, :], 0.0)
        total = total + jnp.where(mline == a, extra, 0.0)
    out = jnp.zeros((OWN, ROWS), F32)
    for s in range(SUBS):
        out = jnp.where(sub == s, total[:, s * ROWS : s * ROWS + ROWS], out)
    mass[...] = out


VM = pl.BlockSpec(memory_space=pltpu.VMEM)
SM = pl.BlockSpec(memory_space=pltpu.SMEM)
DMA = pltpu.SemaphoreType.DMA


def shape(dims, kind=BF):
    return jax.ShapeDtypeStruct(dims, kind)


def talk(number):
    return pltpu.CompilerParams(collective_id=number, has_side_effects=True, vmem_limit_bytes=LIMIT)


def local(descriptors, counts, visible, pair_list, pair_count, w_attend, w_value, w_output, w_hidden, norm_gain, w_down, w_match, unassigned_bucket):
    V = pltpu.VMEM
    peer = (SUBS - 1,)
    tab, *ready, upper, okeep = pl.pallas_call(
        meet_kernel,
        out_shape=(
            shape((8, 128), I32), *[shape((256, 256))] * 3, shape((512, 512)), shape((256, 512)), shape((512, 128), F32),
            shape((SUBS, OWN, HALF, D)), shape((OWN, KEYS), F32),
        ),
        in_specs=[VM, SM, VM, SM, VM] + [VM] * 6,
        out_specs=(VM,) * 9,
        scratch_shapes=[
            V((8, 128), I32), V((REACH, 8, 128), I32), V((SUBS, OWN, KEYS), F32),
            DMA((REACH,)), DMA((REACH,)), DMA((2, SUBS - 1)), DMA((2, SUBS - 1)),
        ],
        compiler_params=talk(0),
    )(pair_list, pair_count, descriptors, counts, visible, w_attend, w_value, w_output, w_hidden, norm_gain.reshape(1, -1), w_down)
    own, xj, jkeep = pl.pallas_call(
        fetch_kernel,
        out_shape=(shape((OWN, KEYS, D)), shape((JOBS, KEYS, D)), shape((JOBS, KEYS), F32)),
        in_specs=[SM, VM, VM, VM],
        out_specs=(VM,) * 3,
        scratch_shapes=[
            V((PARTS, REACH, MOST, PART, D), BF), *[V((REACH, MOST, PART, D), BF)] * PARTS, V((REACH, 8, KEYS), F32), V((REACH, 8, KEYS), F32),
            V((PARTS, SUBS - 1, JOBS, PART, D), BF), V((PARTS, SUBS, JOBS, PART, D), BF), V((SUBS, JOBS, KEYS), F32), V((SUBS - 1, JOBS, KEYS), F32),
            V((SUBS, OWN, HALF, D), BF),
            DMA((PARTS + 1, REACH)), DMA((PARTS + 1, REACH)), DMA((PARTS + 1, SUBS - 1)), DMA((PARTS + 1, SUBS - 1)), DMA(peer), DMA(peer),
        ],
        compiler_params=talk(1),
    )(tab, descriptors, upper, okeep)
    bucket = unassigned_bucket.reshape(1, 1)
    late = JOBS - FIXED
    done = pl.pallas_call(
        work_kernel,
        out_shape=(
            shape((JOBS, KEYS, D)), shape((JOBS, KEYS, D)), shape((FIXED, KEYS, KEYS), F32),
            shape((late, 8, KEYS), F32), shape((late, 8, KEYS), F32),
        ),
        in_specs=[SM] + [VM] * 13,
        out_specs=(VM,) * 5,
        scratch_shapes=[V((256, 256), BF), V((late, KEYS, KEYS), F32)],
        compiler_params=pltpu.CompilerParams(vmem_limit_bytes=LIMIT),
    )(tab, own, xj, okeep, jkeep, bucket, w_attend, w_match, *ready)
    return pl.pallas_call(
        give_kernel,
        out_shape=(shape((OWN, ROWS, D)), shape((OWN, ROWS), F32)),
        in_specs=[SM] + [VM] * 8,
        out_specs=(VM, VM),
        scratch_shapes=[
            V((256, 256), BF), *[V((SUBS, JOBS, PART, D), BF)] * PARTS, V((JOBS, KEYS), F32), V((SUBS, JOBS, KEYS), F32),
            V((PARTS, REACH, MOST, PART, D), BF), V((REACH, 8, KEYS), F32), V((PARTS, REACH, MOST, PART, D), BF), V((REACH, 8, KEYS), F32),
            V((SUBS, OWN, ROWS, D), BF), V((SUBS - 1, OWN, ROWS, D), BF), V((OWN, KEYS), F32), V((SUBS - 1, OWN, KEYS), F32),
            DMA((PARTS + 1, SUBS - 1)), DMA((PARTS + 1, SUBS - 1)), DMA((PARTS + 1, REACH)), DMA((PARTS + 1, REACH)), DMA((2, SUBS - 1)), DMA((2, SUBS - 1)),
        ],
        compiler_params=talk(2),
    )(tab, okeep, jkeep, bucket, *done)


def solution(mesh):
    placed = (P("img", "sub", None), P("img"), P("img", "sub"), P("img", None), P("img")) + (P(),) * 8
    return jax.shard_map(
        local, mesh=mesh, in_specs=placed, out_specs=(P("img", "sub", None), P("img", "sub")), check_vma=False
    )
```

```python
import math

import jax
import jax.numpy as jnp
from jax import lax
from jax.experimental import pallas as pl
from jax.experimental.pallas import tpu as pltpu
from jax.sharding import PartitionSpec as P

BF = jnp.bfloat16
F32 = jnp.float32
I32 = jnp.int32
LOG2E = 1.4426950408889634
FORGET = 30.0 * LOG2E
HEADS = 4
ITERS = 10
KEYS = 256
D = 256
WIN = 3
REACH = 2 * WIN
MOST = 6
OWN = 8
ROWS = 64
SUBS = 4
JOBS = 8
FIXED = 4
PARTS = 4
PART = ROWS // PARTS
HALF = ROWS // 2
MESH = pl.DeviceIdType.MESH
LIMIT = 24 * 2**20


def nn(a, b):
    return lax.dot_general(a, b, (((1,), (0,)), ((), ())), preferred_element_type=F32)


def nt(a, b):
    return lax.dot_general(a, b, (((1,), (1,)), ((), ())), preferred_element_type=F32)


def eye(n):
    up = lax.broadcasted_iota(I32, (n, n), 0)
    return (up == lax.broadcasted_iota(I32, (n, n), 1)).astype(BF)


def to_col(row, ident):
    return nt(ident, jnp.broadcast_to(row, (128, row.shape[1])))


def prepare(wa, wv, wo, wh, gain, wd, waT, wvT, woT, whT, wdT, gcol):
    ident = eye(256)
    waT[...] = nt(ident, wa[...]).astype(BF)
    wvT[...] = nt(ident, wv[...]).astype(BF)
    woT[...] = nt(ident, wo[...]).astype(BF)
    for a in range(0, 512, 256):
        for b in range(0, 512, 256):
            whT[a : a + 256, b : b + 256] = nt(ident, wh[b : b + 256, a : a + 256]).astype(BF)
    for b in range(0, 512, 256):
        wdT[:, b : b + 256] = nt(ident, wd[b : b + 256, :]).astype(BF)
    same = lax.broadcasted_iota(I32, (128, 128), 0) == lax.broadcasted_iota(I32, (128, 128), 1)
    for q in range(0, 512, 128):
        spread = jnp.broadcast_to(gain[:, q : q + 128], (128, 128))
        column = jnp.sum(jnp.where(same, spread, 0.0), axis=1, keepdims=True)
        gcol[q : q + 128, :] = jnp.broadcast_to(column, (128, 128))


def attention(sides, ahead=4, behind=2):
    ones = jnp.ones((16, KEYS), BF)
    steps = [(h, s) for h in range(HEADS) for s in range(len(sides))]

    def similarity(h, s):
        a_other, aT_self, _, bias = sides[s]
        sl = slice(h * 64, h * 64 + 64)
        value = nn(a_other[:, sl], aT_self[sl]) * (LOG2E / 8.0) + bias
        return value, jnp.max(value, axis=0, keepdims=True)

    def finish(r):
        return (r[:64] * (1.0 / r[64:65])).astype(BF)

    waiting = [similarity(*step) for step in steps[:ahead]]
    late = []
    outs = {}
    for i, (h, s) in enumerate(steps):
        if i + ahead < len(steps):
            waiting.append(similarity(*steps[i + ahead]))
        value, top = waiting.pop(0)
        e = jnp.exp2(value - top).astype(BF)
        late.append(((h, s), nn(jnp.concatenate([sides[s][2][h * 64 : h * 64 + 64], ones], axis=0), e)))
        if len(late) > behind:
            step, r = late.pop(0)
            outs[step] = finish(r)
    for step, r in late:
        outs[step] = finish(r)
    return [jnp.concatenate([outs[h, s] for h in range(HEADS)], axis=0) for s in range(len(sides))]


def refine(xs, msgs, w):
    half = math.sqrt(0.5)
    gain = jnp.concatenate([w["gcol"][...]] * 2, axis=1) * half

    def hidden(i):
        sentT = nn(w["woT"][...], msgs[i]).astype(BF)
        return nt(w["whT"][:, :256], xs[i]) + nn(w["whT"][:, 256:], sentT)

    outs = []
    later = hidden(0)
    for i in range(len(xs)):
        hid = later
        if i + 1 < len(xs):
            later = hidden(i + 1)
        mean = jnp.sum(hid, axis=0, keepdims=True) * (1.0 / 512)
        cen = hid - mean
        var = jnp.sum(cen * cen, axis=0, keepdims=True) * (1.0 / 512)
        z = cen * lax.rsqrt(var + 1e-5) * gain
        outs.append(nn(w["wdT"][...], ((half * z) * (1.0 + lax.erf(z))).astype(BF)).astype(BF))
    return outs


def pair_scores(pairs, w):
    ident = w["ident"][...]
    xs, biases = [], []
    for xi, ki, xj, kj in pairs:
        xs += [xi, xj]
        for keep in (ki, kj):
            bias = (to_col(keep, ident) - 1.0) * 1e30
            biases.append(jnp.concatenate([bias, bias], axis=1))
    attend = [nn(x, w["wa"][...]).astype(BF) for x in xs]
    attendT = [nt(w["waT"][...], x).astype(BF) for x in xs]
    valueT = [nt(w["wvT"][...], x).astype(BF) for x in xs]
    msgs = attention([(attend[i ^ 1], attendT[i], valueT[i ^ 1], biases[i ^ 1]) for i in range(len(xs))])
    deltas = [nt(ident, d).astype(BF) for d in refine(xs, msgs, w)]
    match = [
        nn((x.astype(F32) + d.astype(F32)).astype(BF), w["wm"][...]).astype(BF) for x, d in zip(xs, deltas)
    ]
    return [
        (deltas[i], deltas[i + 1], nt(match[i], match[i + 1]) * (LOG2E / 16.0)) for i in range(0, len(xs), 2)
    ]


def marginals(ki, kj, ident):
    m = jnp.sum(ki, axis=1, keepdims=True)
    n = jnp.sum(kj, axis=1, keepdims=True)
    total = m + n
    off = -jnp.log2(jnp.maximum(total, 1.0))
    kic = to_col(ki.astype(BF), ident)
    lr = off - FORGET * (1.0 - kic)
    lc = off - FORGET * (1.0 - kj)
    lrb = jnp.log2(jnp.maximum(n, 1.0)) + off
    lcb = jnp.log2(jnp.maximum(m, 1.0)) + off
    return total, kic, lr, lc, lrb, lcb


def sink_first(c, bucket, lr, lc, lrb, lcb):
    top = jnp.maximum(jnp.max(c, axis=1, keepdims=True), bucket)
    s = jnp.sum(jnp.exp2(c - top), axis=1, keepdims=True) + jnp.exp2(bucket - top)
    f = lr - top - jnp.log2(s)
    fb = lrb - bucket - math.log2(257.0)
    halves = [jnp.sum(jnp.exp2(c[:, at : at + 128] + f), axis=0, keepdims=True) for at in (0, 128)]
    t = jnp.concatenate(halves, axis=1) + jnp.exp2(bucket + fb)
    tb = jnp.sum(jnp.exp2(bucket + f), axis=0, keepdims=True)[:, :1] + jnp.exp2(bucket + fb)
    return f, fb, lc - jnp.log2(t), lcb - jnp.log2(tb)


def sink_next(c, at, bucket, lr, lc, lrb, lcb, state):
    f, fb, g, gb = state
    eb = jnp.exp2(bucket + fb + g)
    ebb = jnp.exp2(bucket + fb + gb)
    dub = lrb - jnp.log2(jnp.sum(eb, axis=1, keepdims=True) + ebb)
    ub = jnp.exp2(dub)
    p0 = jnp.exp2(c[at, :, :128] + g[:, :128] + f)
    p1 = jnp.exp2(c[at, :, 128:] + g[:, 128:] + f)
    b = jnp.exp2((bucket + gb) + f)
    du = lr - jnp.log2(jnp.sum(p0 + p1, axis=1, keepdims=True) + b)
    u = jnp.exp2(du)
    t = [jnp.sum(p * u, axis=0, keepdims=True) for p in (p0, p1)]
    t = eb * ub + jnp.concatenate(t, axis=1)
    tb = ebb * ub + jnp.sum(b * u, axis=0, keepdims=True)[:, :1]
    return f + du, fb + dub, g + lc - jnp.log2(t), gb + lcb - jnp.log2(tb)


def sink_out(c, total, kic, kj, state):
    f, fb, g, gb = state
    p0 = jnp.exp2(c[:, :128] + g[:, :128] + f)
    p1 = jnp.exp2(c[:, 128:] + g[:, 128:] + f)
    mi = (jnp.sum(p0 + p1, axis=1, keepdims=True) * total * kic).astype(BF)
    halves = [jnp.sum(p, axis=0, keepdims=True) for p in (p0, p1)]
    mj = (jnp.concatenate(halves, axis=1) * total * kj).astype(BF)
    first = (lax.broadcasted_iota(I32, (16, 128), 1) == 0).astype(BF)
    return nt(first, mi)[:1], mj.astype(F32)


def row_of(block, index):
    at = lax.broadcasted_iota(I32, block.shape, 0)
    return jnp.sum(jnp.where(at == index, block, 0.0), axis=0, keepdims=True)


def job_of(tab, q, sub):
    code = tab[0, q * SUBS + sub]
    return (code >> 8) & 7, (code >> 12) & 1


def do_scores(jobs, tab, sub, own, xj, okeep, jkeep, w):
    pairs, swaps = [], []
    for q in jobs:
        mine, swap = job_of(tab, q, sub)
        xm, xo = own[mine], xj[q]
        km = row_of(okeep[...], mine)
        ko = row_of(jkeep[...], q)
        ki = jnp.where(swap == 1, ko, km).astype(BF)
        kj = jnp.where(swap == 1, km, ko).astype(BF)
        pairs.append((jnp.where(swap == 1, xo, xm), ki, jnp.where(swap == 1, xm, xo), kj))
        swaps.append(swap)
    return [
        (jnp.where(swap == 1, dj, di), jnp.where(swap == 1, di, dj), scores)
        for swap, (di, dj, scores) in zip(swaps, pair_scores(pairs, w))
    ]


def do_masses(jobs, sc, tab, sub, okeep, jkeep, bucket, ident):
    swaps, margs, states, kjs = [], [], [], []
    for q, (ref, at) in zip(jobs, sc):
        mine, swap = job_of(tab, q, sub)
        km = row_of(okeep[...], mine)
        ko = row_of(jkeep[...], q)
        ki = jnp.where(swap == 1, ko, km)
        kj = jnp.where(swap == 1, km, ko)
        marg = marginals(ki, kj, ident)
        swaps.append(swap)
        kjs.append(kj)
        margs.append(marg)
        states.append(sink_first(ref[at], bucket, *marg[2:]))

    def sweep(_, states):
        return [sink_next(ref, at, bucket, *m[2:], s) for (ref, at), m, s in zip(sc, margs, states)]

    states = lax.fori_loop(0, ITERS - 1, sweep, states)
    outs = []
    for (ref, at), m, s, kj, swap in zip(sc, margs, states, kjs, swaps):
        a, b = sink_out(ref[at], m[0], m[1], kj, s)
        outs.append((jnp.where(swap == 1, b, a), jnp.where(swap == 1, a, b)))
    return outs


def step_of(turn):
    return (turn // 2 + 1) * (1 - 2 * (turn % 2))


def places():
    n = lax.axis_size("img")
    me = lax.axis_index("img")
    sub = lax.axis_index("sub")
    others = [lax.rem(me + step_of(t) + n, n) for t in range(REACH)]
    peers = [lax.rem(sub + d, SUBS) for d in range(1, SUBS)]
    return me, sub, others, peers


def greet(others, peers):
    barrier = pltpu.get_barrier_semaphore()
    for h in others:
        pl.semaphore_signal(barrier, inc=1, device_id={"img": h}, device_id_type=MESH)
    for s in peers:
        pl.semaphore_signal(barrier, inc=1, device_id={"sub": s}, device_id_type=MESH)
    pl.semaphore_wait(barrier, len(others) + len(peers))


def send(src, dst, ssem, rsem, to):
    return pltpu.make_async_remote_copy(
        src_ref=src, dst_ref=dst, send_sem=ssem, recv_sem=rsem, device_id=to, device_id_type=MESH
    )


def own_rows(pairs, live_count, me, img_count):
    slots = pairs.shape[1]
    up = lax.broadcasted_iota(I32, (slots, slots), 0)
    across = lax.broadcasted_iota(I32, (slots, slots), 1)
    first, second = (
        jnp.sum(jnp.where(up == across, pairs[k : k + 1, :], 0), axis=1, keepdims=True) for k in (0, 1)
    )
    row_ids = lax.broadcasted_iota(I32, (slots, 1), 0)
    ahead = (second >> 3) - me
    ahead = jnp.where(ahead < 0, ahead + img_count, ahead)
    turn = jnp.where(ahead <= WIN, 2 * (ahead - 1), 2 * (img_count - ahead - 1) + 1)
    live = row_ids < live_count
    key = jnp.where(live, turn, 15)
    code = 1 + (first & 7) * 8 + (second & 7)
    key_row = jnp.sum(jnp.where(up == across, key, 0), axis=0, keepdims=True)
    rank = jnp.sum(jnp.where((key_row == key) & (across < up), 1, 0), axis=1, keepdims=True)
    lanes = lax.broadcasted_iota(I32, (slots, 128), 1)
    lane = lax.broadcasted_iota(I32, (1, 128), 1)
    rows = []
    for k in (key, key ^ 1):
        at = jnp.where(live, k * 8 + rank, -1)
        codes = jnp.sum(jnp.where(lanes == at, code, 0), axis=0, keepdims=True)
        counts = jnp.sum(jnp.where((lanes == 64 + k) & live, 1, 0), axis=0, keepdims=True)
        row = codes + counts
        rows.append(jnp.where((lane >= 80) & (lane < 88), live_count, row))
    return rows


def plan_rows(own, near, live_count):
    r8 = lax.broadcasted_iota(I32, (8, 128), 0)
    l8 = lax.broadcasted_iota(I32, (8, 128), 1)
    mine = jnp.where(l8 < 64, l8 >> 3, l8 & 7)
    from_near = jnp.sum(jnp.where((mine == r8) & (r8 < REACH), near, 0), axis=0, keepdims=True)
    slots = 64
    lanes = lax.broadcasted_iota(I32, (slots, 128), 1)
    slot = lax.broadcasted_iota(I32, (slots, 1), 0)
    turn = slot >> 3
    u = slot & 7
    own_all = jnp.broadcast_to(own, (slots, 128))
    near_all = jnp.broadcast_to(from_near, (slots, 128))

    def pick(table, lane):
        return jnp.sum(jnp.where(lanes == lane, table, 0), axis=1, keepdims=True)

    n_own = pick(own_all, 64 + turn)
    n_near = pick(near_all, 64 + turn)
    l_near = pick(near_all, 80 + turn)

    def sixth(value):
        return (jnp.maximum(value, 0) * 43) >> 8

    give = jnp.maximum(jnp.minimum(jnp.minimum(sixth(live_count - l_near), n_own), MOST - n_near), 0)
    take = jnp.maximum(jnp.minimum(jnp.minimum(sixth(l_near - live_count), n_near), MOST - n_own), 0)
    kept = n_own - give
    near_kept = n_near - take
    own_code = pick(own_all, turn * 8 + u) - 1
    near_code = pick(near_all, turn * 8 + u) - 1
    taken_code = pick(near_all, turn * 8 + near_kept + u - kept) - 1
    given_code = pick(own_all, turn * 8 + kept + u - near_kept) - 1
    live = (u < kept + take) & (turn < REACH)
    image = jnp.where(u < kept, own_code >> 3, taken_code & 7)
    swap = jnp.where(u < kept, 0, 1)
    asked = (u < near_kept + give) & (turn < REACH)
    sends = jnp.where(u < near_kept, near_code & 7, given_code >> 3)
    eye64 = lax.broadcasted_iota(I32, (slots, slots), 0) == lax.broadcasted_iota(I32, (slots, slots), 1)
    live_row = jnp.sum(jnp.where(eye64, jnp.where(live, 1, 0), 0), axis=0, keepdims=True)
    short = lax.broadcasted_iota(I32, (slots, slots), 1)
    place = jnp.sum(jnp.where(short < slot, live_row, 0), axis=1, keepdims=True)
    count = jnp.sum(live_row, axis=1, keepdims=True)

    def put(lane, value):
        return jnp.sum(jnp.where(lanes == lane, value, 0), axis=0, keepdims=True)

    by_place = put(jnp.where(live, place, -1), 1 + slot + image * 256 + swap * 4096)
    by_slot = put(slot, jnp.where(asked, 1 + sends, 0))
    places_row = put(slot, jnp.where(live, place, 0))
    row = lax.broadcasted_iota(I32, (8, 128), 0)
    out = jnp.where(row == 0, by_place, jnp.where(row == 1, by_slot, jnp.where(row == 2, places_row, count)))
    return out


def own_mask(counts, visible, sub):
    image = lax.broadcasted_iota(I32, (OWN, ROWS), 0)
    found = jnp.zeros((OWN, ROWS), I32)
    for a in range(OWN):
        found = jnp.where(image == a, counts[a], found)
    spot = lax.broadcasted_iota(I32, (OWN, ROWS), 1) + sub * ROWS
    kept = jnp.where((spot < found) & (visible[...] > 0), 1.0, 0.0)
    return my_lanes(jnp.concatenate([kept] * SUBS, axis=1), sub)


def my_lanes(wide, sub):
    lane = lax.broadcasted_iota(I32, wide.shape, 1)
    return jnp.where((lane >= sub * ROWS) & (lane < sub * ROWS + ROWS), wide, 0.0)


def meet_kernel(
    pairs, pair_count, counts, desc_far, visible_far, wa_far, wv_far, wo_far, wh_far, gain_far, wd_far,
    tab, waT, wvT, woT, whT, wdT, gcol, upper, okeep, told, near, omask, desc, visible, wa, wv, wo, wh, gain, wd,
    ssem, rsem, osem, orem, lsem,
):
    me, sub, others, peers = places()
    far = (desc_far, visible_far, wa_far, wv_far, wo_far, wh_far, gain_far, wd_far)
    loads = [
        pltpu.make_async_copy(src, dst, lsem.at[i])
        for i, (src, dst) in enumerate(zip(far, (desc, visible, wa, wv, wo, wh, gain, wd)))
    ]
    for load in loads:
        load.start()
    own, out = own_rows(pairs[...], pair_count[0], me, lax.axis_size("img"))
    told[...] = jnp.broadcast_to(out, (8, 128))
    for load in loads[:2]:
        load.wait()
    omask[0] = own_mask(counts, visible, sub)
    greet(others, peers)
    ocopies = []
    for d in range(1, SUBS):
        to = {"sub": peers[d - 1]}
        ocopies.append(send(omask.at[0], omask.at[d], osem.at[1, d - 1], orem.at[1, d - 1], to))
        ocopies.append(send(desc.at[:, 0:HALF, :], upper.at[sub], osem.at[0, d - 1], orem.at[0, d - 1], to))
    copies = [send(told, near.at[t ^ 1], ssem.at[t], rsem.at[t ^ 1], {"img": others[t]}) for t in range(REACH)]
    for copy in copies + ocopies:
        copy.start()
    upper[sub] = desc[:, 0:HALF, :]
    for load in loads[2:]:
        load.wait()
    prepare(wa, wv, wo, wh, gain, wd, waT, wvT, woT, whT, wdT, gcol)
    for copy in copies:
        copy.wait()
    row = lax.broadcasted_iota(I32, (8, 128), 0)
    table = jnp.zeros((8, 128), I32)
    for t in range(REACH):
        table = jnp.where(row == t, near[t], table)
    tab[...] = plan_rows(own, table, pair_count[0])
    for copy in ocopies:
        copy.wait()
    okeep[...] = omask[0] + omask[1] + omask[2] + omask[3]


def sent_image(tab, t, u):
    return tab[1, t * 8 + u]


def fetch_kernel(
    tab, desc, upper, okeep, own, xj, jkeep, zst, zl0, zl1, zl2, zl3, zms, zml, yst, yl, yms, yml, lower,
    zsem, zrem, ysem, yrem, osem, orem,
):
    me, sub, others, peers = places()
    zland = (zl0, zl1, zl2, zl3)
    wide = my_lanes(okeep[...], sub)
    greet(others, peers)
    order = (4, 5, 2, 3, 0, 1)
    line = lax.broadcasted_iota(I32, (8, KEYS), 0)
    zmcopies = []
    for t in order:
        masks = jnp.zeros((8, KEYS), F32)
        for u in range(MOST):
            masks = jnp.where(line == u, row_of(wide, jnp.maximum(sent_image(tab, t, u) - 1, 0)), masks)
        zms[t] = masks
        zmcopies.append(
            send(zms.at[t], zml.at[t ^ 1], zsem.at[PARTS, t], zrem.at[PARTS, t ^ 1], {"img": others[t]})
        )
        zmcopies[-1].start()
    zcopies = []
    for c in range(PARTS):
        zcopies.append([])
        for t in order:
            for u in range(MOST):
                which = jnp.maximum(sent_image(tab, t, u) - 1, 0)
                zst[c, t, u] = desc[which, c * PART : c * PART + PART, :]
            copy = send(zst.at[c, t], zland[c].at[t ^ 1], zsem.at[c, t], zrem.at[c, t ^ 1], {"img": others[t]})
            copy.start()
            zcopies[c].append(copy)
    ocopies = []
    for d in range(1, SUBS):
        copy = send(desc.at[:, HALF:ROWS, :], lower.at[sub], osem.at[d - 1], orem.at[d - 1], {"sub": peers[d - 1]})
        copy.start()
        ocopies.append(copy)
    lower[sub] = desc[:, HALF:ROWS, :]
    for copy in zmcopies:
        copy.wait()
    zmasks = jnp.concatenate([zml[t] for t in range(REACH)], axis=0)
    slots = []
    for d in range(SUBS):
        worker = sub if d == 0 else peers[d - 1]
        slots.append([jnp.maximum((tab[0, q * SUBS + worker] & 255) - 1, 0) for q in range(JOBS)])
        masks = jnp.zeros((JOBS, KEYS), F32)
        for q in range(JOBS):
            masks = jnp.where(line == q, row_of(zmasks, slots[d][q]), masks)
        yms[d] = masks
    ycopies = []
    for d in range(1, SUBS):
        to = {"sub": peers[d - 1]}
        ycopies.append(send(yms.at[d], yml.at[d - 1], ysem.at[PARTS, d - 1], yrem.at[PARTS, d - 1], to))
        ycopies[-1].start()
    for c in range(PARTS):
        for copy in zcopies[c]:
            copy.wait()
        for d in range(1, SUBS):
            for q in range(JOBS):
                yst[c, d - 1, q] = zland[c][slots[d][q] >> 3, slots[d][q] & 7]
            copy = send(yst.at[c, d - 1], yl.at[c, sub], ysem.at[c, d - 1], yrem.at[c, d - 1], {"sub": peers[d - 1]})
            copy.start()
            ycopies.append(copy)
        for q in range(JOBS):
            yl[c, sub, q] = zland[c][slots[0][q] >> 3, slots[0][q] & 7]
    for copy in ocopies:
        copy.wait()
    for s in range(SUBS):
        own[:, s * ROWS : s * ROWS + HALF, :] = upper[s]
        own[:, s * ROWS + HALF : s * ROWS + ROWS, :] = lower[s]
    for copy in ycopies:
        copy.wait()
    for s in range(SUBS):
        for c in range(PARTS):
            at = s * ROWS + c * PART
            xj[:, at : at + PART, :] = yl[c, s]
    jkeep[...] = yms[0] + yml[0] + yml[1] + yml[2]


def work_kernel(
    tab, own, xj, okeep, jkeep, bucket, wa, wm, waT, wvT, woT, whT, wdT, gcol, dmine, dother, mm, mo, ident, sc
):
    sub = lax.axis_index("sub")
    ident[...] = eye(256)
    w = dict(wa=wa, wm=wm, waT=waT, wvT=wvT, woT=woT, whT=whT, wdT=wdT, gcol=gcol, ident=ident)
    n = ((tab[3, 0] + (SUBS - 1) - sub) >> 2) - FIXED
    binv = bucket[...] * LOG2E

    def late(ps):
        outs = do_scores([FIXED + p for p in ps], tab, sub, own, xj, okeep, jkeep, w)
        for p, out in zip(ps, outs):
            dmine[p], dother[p], sc[p] = out
        outs = do_masses([FIXED + p for p in ps], [(sc, p) for p in ps], tab, sub, okeep, jkeep, binv, ident[...])
        for p, (a, b) in zip(ps, outs):
            mm[p] = jnp.broadcast_to(a, (8, KEYS))
            mo[p] = jnp.broadcast_to(b, (8, KEYS))

    @pl.loop(0, n >> 1)
    def _(p):
        late([2 * p, 2 * p + 1])

    @pl.when((n & 1) == 1)
    def _():
        late([n - 1])


def give_kernel(
    tab, own, xj, okeep, jkeep, bucket, wa, wm, waT, wvT, woT, whT, wdT, gcol, dmine2, dother2, mm2, mo2,
    zret, zmr, gm, mparts, mgot, ident, dmine, dother, sc, yb0, yb1, yb2, yb3, ymst, yml, zst, zms,
    ysem, yrem, zsem, zrem, osem, orem,
):
    me, sub, others, peers = places()
    yb = (yb0, yb1, yb2, yb3)
    ident[...] = eye(256)
    w = dict(wa=wa, wm=wm, waT=waT, wvT=wvT, woT=woT, whT=whT, wdT=wdT, gcol=gcol, ident=ident)
    binv = bucket[...] * LOG2E
    mline = lax.broadcasted_iota(I32, (JOBS, KEYS), 0)
    order = (4, 5, 2, 3, 0, 1)

    def rows_of(p, c):
        return pl.ds(pl.multiple_of(p * ROWS + c * PART, PART), PART)

    def block_of(p):
        return pl.ds(pl.multiple_of(p * ROWS, ROWS), ROWS)

    greet(others, peers)
    ycopies = [[] for _ in range(PARTS)]
    ocopies = []

    def hand_back(group, theirs, at, to):
        for c in range(PARTS):
            for d in range(1, SUBS):
                p = peers[d - 1]
                copy = send(
                    theirs.at[at, rows_of(p, c), :], yb[c].at[sub, to], ysem.at[group, c, d - 1], yrem.at[group, c, d - 1], {"sub": p}
                )
                copy.start()
                ycopies[c].append(copy)
        for c in range(PARTS):
            yb[c][sub, to] = theirs[at, rows_of(sub, c), :]

    def hand_mine(group, mine, at, to):
        for d in range(1, SUBS):
            p = peers[d - 1]
            copy = send(mine.at[at, block_of(p), :], gm.at[sub, to], osem.at[group, d - 1], orem.at[group, d - 1], {"sub": p})
            copy.start()
            ocopies.append(copy)
        gm[sub, to] = mine[at, block_of(sub), :]

    hand_back(2, dother2, slice(0, JOBS - FIXED), slice(FIXED, JOBS))
    for group in range(2):
        at = slice(2 * group, 2 * group + 2)
        outs = do_scores([2 * group, 2 * group + 1], tab, sub, own, xj, okeep, jkeep, w)
        for q, out in enumerate(outs, 2 * group):
            dmine[q], dother[q], sc[q] = out
        hand_back(group, dother, at, at)
    n = (tab[3, 0] + (SUBS - 1) - sub) >> 2
    owners = [jnp.where(q < n, job_of(tab, q, sub)[0], -1) for q in range(JOBS)]
    places_of = [[tab[2, t * 8 + u] for u in range(MOST)] for t in range(REACH)]
    zcopies = [[] for _ in range(PARTS)]

    def pass_on(c):
        for copy in ycopies[c]:
            copy.wait()
        for t in order:
            for u in range(MOST):
                zst[c, t, u] = yb[c][places_of[t][u] & 3, places_of[t][u] >> 2]
            copy = send(zst.at[c, t], zret.at[c, t ^ 1], zsem.at[c, t], zrem.at[c, t ^ 1], {"img": others[t]})
            copy.start()
            zcopies[c].append(copy)

    def some_masses(qs):
        return do_masses(qs, [(sc, q) for q in qs], tab, sub, okeep, jkeep, binv, ident[...])

    for c in range(PARTS):
        pass_on(c)
    hand_mine(2, dmine2, slice(0, JOBS - FIXED), slice(FIXED, JOBS))
    for group in range(2):
        at = slice(2 * group, 2 * group + 2)
        hand_mine(group, dmine, at, at)
    masses = some_masses([0, 1])
    masses += some_masses([2, 3])
    mine = [masses[q][0] if q < FIXED else mm2[q - FIXED, 0:1, :] for q in range(JOBS)]
    away = [masses[q][1] if q < FIXED else mo2[q - FIXED, 0:1, :] for q in range(JOBS)]
    table = jnp.zeros((JOBS, KEYS), F32)
    for q in range(JOBS):
        table = jnp.where(mline == q, away[q], table)
    ymst[...] = table
    yml[sub] = table
    ymcopies = []
    for d in range(1, SUBS):
        to = {"sub": peers[d - 1]}
        ymcopies.append(send(ymst, yml.at[sub], ysem.at[3, 0, d - 1], yrem.at[3, 0, d - 1], to))
        ymcopies[-1].start()
    table = jnp.zeros((OWN, KEYS), F32)
    for a in range(OWN):
        for q in range(JOBS):
            table = table + jnp.where((mline == a) & (owners[q] == a), mine[q], 0.0)
    mparts[...] = table
    for d in range(1, SUBS):
        copy = send(mparts, mgot.at[d - 1], osem.at[3, d - 1], orem.at[3, d - 1], {"sub": peers[d - 1]})
        copy.start()
        ocopies.append(copy)
    for copy in ymcopies:
        copy.wait()
    ymasses = jnp.concatenate([yml[s] for s in range(SUBS)], axis=0)
    zmcopies = []
    for t in order:
        back = jnp.zeros((8, KEYS), F32)
        for u in range(MOST):
            place = places_of[t][u]
            back = jnp.where(mline == u, row_of(ymasses, (place & 3) * JOBS + (place >> 2)), back)
        zms[t] = back
        to = {"img": others[t]}
        zmcopies.append(send(zms.at[t], zmr.at[t ^ 1], zsem.at[PARTS, t], zrem.at[PARTS, t ^ 1], to))
        zmcopies[-1].start()
    for copy in ocopies + zmcopies:
        copy.wait()
    for c in range(PARTS):
        for copy in zcopies[c]:
            copy.wait()


def sum_kernel(tab, zret, zmr, gm, mparts, mgot, upd, mass, acc, macc):
    sub = lax.axis_index("sub")
    acc[...] = jnp.zeros_like(acc)

    @pl.loop(0, SUBS * JOBS)
    def _(g):
        code = tab[0, g]

        @pl.when(code > 0)
        def _():
            which = (code >> 8) & 7
            acc[which] = acc[which] + gm[g & 3, g >> 2].astype(F32)

    macc[...] = mparts[...] + mgot[0] + mgot[1] + mgot[2]
    line = lax.broadcasted_iota(I32, (8, KEYS), 0)

    @pl.loop(0, REACH)
    def _(t):
        for u in range(MOST):
            which = tab[1, t * 8 + u] - 1

            @pl.when(which >= 0)
            def _():
                for c in range(PARTS):
                    rows = slice(c * PART, c * PART + PART)
                    acc[which, rows] = acc[which, rows] + zret[c, t, u].astype(F32)
                macc[...] = macc[...] + jnp.where(line == which, zmr[t, u : u + 1, :], 0.0)

    upd[...] = acc[...].astype(BF)
    total = macc[...]
    out = jnp.zeros((OWN, ROWS), F32)
    for s in range(SUBS):
        out = jnp.where(sub == s, total[:, s * ROWS : s * ROWS + ROWS], out)
    mass[...] = out


VM = pl.BlockSpec(memory_space=pltpu.VMEM)
SM = pl.BlockSpec(memory_space=pltpu.SMEM)
DMA = pltpu.SemaphoreType.DMA
HB = pl.BlockSpec(memory_space=pltpu.HBM)


def shape(dims, kind=BF):
    return jax.ShapeDtypeStruct(dims, kind)


def talk(number, limit=LIMIT):
    return pltpu.CompilerParams(collective_id=number, has_side_effects=True, vmem_limit_bytes=limit)


COST = pl.CostEstimate(flops=10**10, bytes_accessed=5 * 10**7, transcendentals=10**7)


def local(descriptors, counts, visible, pair_list, pair_count, w_attend, w_value, w_output, w_hidden, norm_gain, w_down, w_match, unassigned_bucket):
    V = pltpu.VMEM
    peer = (SUBS - 1,)
    tab, *ready, upper, okeep = pl.pallas_call(
        meet_kernel,
        out_shape=(
            shape((8, 128), I32), *[shape((256, 256))] * 3, shape((512, 512)), shape((256, 512)), shape((512, 128), F32),
            shape((SUBS, OWN, HALF, D)), shape((OWN, KEYS), F32),
        ),
        in_specs=[VM, SM, SM] + [HB] * 8,
        out_specs=(VM,) * 9,
        scratch_shapes=[
            V((8, 128), I32), V((REACH, 8, 128), I32), V((SUBS, OWN, KEYS), F32),
            V((OWN, ROWS, D), BF), V((OWN, ROWS), I32), *[V((256, 256), BF)] * 3, V((512, 512), BF), V((1, 512), F32), V((512, 256), BF),
            DMA((REACH,)), DMA((REACH,)), DMA((2, SUBS - 1)), DMA((2, SUBS - 1)), DMA((8,)),
        ],
        compiler_params=talk(0, 56 * 2**20),
        cost_estimate=COST,
    )(pair_list.T, pair_count, counts, descriptors, visible, w_attend, w_value, w_output, w_hidden, norm_gain.reshape(1, -1), w_down)
    own, xj, jkeep = pl.pallas_call(
        fetch_kernel,
        out_shape=(shape((OWN, KEYS, D)), shape((JOBS, KEYS, D)), shape((JOBS, KEYS), F32)),
        in_specs=[SM, VM, VM, VM],
        out_specs=(VM,) * 3,
        scratch_shapes=[
            V((PARTS, REACH, MOST, PART, D), BF), *[V((REACH, MOST, PART, D), BF)] * PARTS, V((REACH, 8, KEYS), F32), V((REACH, 8, KEYS), F32),
            V((PARTS, SUBS - 1, JOBS, PART, D), BF), V((PARTS, SUBS, JOBS, PART, D), BF), V((SUBS, JOBS, KEYS), F32), V((SUBS - 1, JOBS, KEYS), F32),
            V((SUBS, OWN, HALF, D), BF),
            DMA((PARTS + 1, REACH)), DMA((PARTS + 1, REACH)), DMA((PARTS + 1, SUBS - 1)), DMA((PARTS + 1, SUBS - 1)), DMA(peer), DMA(peer),
        ],
        compiler_params=talk(1),
        cost_estimate=COST,
    )(tab, descriptors, upper, okeep)
    bucket = unassigned_bucket.reshape(1, 1)
    late = JOBS - FIXED
    common = (tab, own, xj, okeep, jkeep, bucket, w_attend, w_match, *ready)
    rest = pl.pallas_call(
        work_kernel,
        out_shape=(shape((late, KEYS, D)), shape((late, KEYS, D)), shape((late, 8, KEYS), F32), shape((late, 8, KEYS), F32)),
        in_specs=[SM] + [VM] * 13,
        out_specs=(VM,) * 4,
        scratch_shapes=[V((256, 256), BF), V((late, KEYS, KEYS), F32)],
        compiler_params=pltpu.CompilerParams(vmem_limit_bytes=LIMIT),
    )(*common)
    back = pl.pallas_call(
        give_kernel,
        out_shape=(
            shape((PARTS, REACH, MOST, PART, D)), shape((REACH, 8, KEYS), F32), shape((SUBS, JOBS, ROWS, D)),
            shape((OWN, KEYS), F32), shape((SUBS - 1, OWN, KEYS), F32),
        ),
        in_specs=[SM] + [VM] * 17,
        out_specs=(VM,) * 5,
        scratch_shapes=[
            V((256, 256), BF), V((FIXED, KEYS, D), BF), V((FIXED, KEYS, D), BF), V((FIXED, KEYS, KEYS), F32),
            *[V((SUBS, JOBS, PART, D), BF)] * PARTS, V((JOBS, KEYS), F32), V((SUBS, JOBS, KEYS), F32),
            V((PARTS, REACH, MOST, PART, D), BF), V((REACH, 8, KEYS), F32),
            DMA((4, PARTS, SUBS - 1)), DMA((4, PARTS, SUBS - 1)), DMA((PARTS + 1, REACH)), DMA((PARTS + 1, REACH)), DMA((4, SUBS - 1)), DMA((4, SUBS - 1)),
        ],
        compiler_params=talk(2),
        cost_estimate=COST,
    )(*common, *rest)
    return pl.pallas_call(
        sum_kernel,
        out_shape=(shape((OWN, ROWS, D)), shape((OWN, ROWS), F32)),
        in_specs=[SM] + [VM] * 5,
        out_specs=(VM, VM),
        scratch_shapes=[V((OWN, ROWS, D), F32), V((OWN, KEYS), F32)],
        compiler_params=pltpu.CompilerParams(vmem_limit_bytes=LIMIT),
    )(tab, *back)


def solution(mesh):
    placed = (P("img", "sub", None), P("img"), P("img", "sub"), P("img", None), P("img")) + (P(),) * 8
    return jax.shard_map(
        local, mesh=mesh, in_specs=placed, out_specs=(P("img", "sub", None), P("img", "sub")), check_vma=False
    )
```

```python
import math

import jax
import jax.numpy as jnp
from jax import lax
from jax.experimental import pallas as pl
from jax.experimental.pallas import tpu as pltpu
from jax.sharding import PartitionSpec as P

BF = jnp.bfloat16
F32 = jnp.float32
I32 = jnp.int32
LOG2E = 1.4426950408889634
FORGET = 30.0 * LOG2E
HEADS = 4
ITERS = 10
KEYS = 256
D = 256
WIN = 3
REACH = 2 * WIN
MOST = 6
OWN = 8
ROWS = 64
SUBS = 4
JOBS = 8
FIXED = 4
PARTS = 4
PART = ROWS // PARTS
HALF = 16
MESH = pl.DeviceIdType.MESH
LIMIT = 24 * 2**20


def nn(a, b):
    return lax.dot_general(a, b, (((1,), (0,)), ((), ())), preferred_element_type=F32)


def nt(a, b):
    return lax.dot_general(a, b, (((1,), (1,)), ((), ())), preferred_element_type=F32)


def eye(n):
    up = lax.broadcasted_iota(I32, (n, n), 0)
    return (up == lax.broadcasted_iota(I32, (n, n), 1)).astype(BF)


def to_col(row, ident):
    return nt(ident, jnp.broadcast_to(row, (128, row.shape[1])))


def prepare(wa, wv, wo, wh, gain, wd, waT, wvT, woT, whT, wdT, gcol):
    ident = eye(256)
    waT[...] = nt(ident, wa[...]).astype(BF)
    wvT[...] = nt(ident, wv[...]).astype(BF)
    woT[...] = nt(ident, wo[...]).astype(BF)
    for a in range(0, 512, 256):
        for b in range(0, 512, 256):
            whT[a : a + 256, b : b + 256] = nt(ident, wh[b : b + 256, a : a + 256]).astype(BF)
    for b in range(0, 512, 256):
        wdT[:, b : b + 256] = nt(ident, wd[b : b + 256, :]).astype(BF)
    same = lax.broadcasted_iota(I32, (128, 128), 0) == lax.broadcasted_iota(I32, (128, 128), 1)
    for q in range(0, 512, 128):
        spread = jnp.broadcast_to(gain[:, q : q + 128], (128, 128))
        column = jnp.sum(jnp.where(same, spread, 0.0), axis=1, keepdims=True)
        gcol[q : q + 128, :] = jnp.broadcast_to(column, (128, 128))


def attention(sides, ahead=4, behind=2):
    ones = jnp.ones((16, KEYS), BF)
    steps = [(h, s) for h in range(HEADS) for s in range(len(sides))]

    def similarity(h, s):
        a_other, aT_self, _, bias = sides[s]
        sl = slice(h * 64, h * 64 + 64)
        value = nn(a_other[:, sl], aT_self[sl]) * (LOG2E / 8.0) + bias
        return value, jnp.max(value, axis=0, keepdims=True)

    def finish(r):
        return (r[:64] * (1.0 / r[64:65])).astype(BF)

    waiting = [similarity(*step) for step in steps[:ahead]]
    late = []
    outs = {}
    for i, (h, s) in enumerate(steps):
        if i + ahead < len(steps):
            waiting.append(similarity(*steps[i + ahead]))
        value, top = waiting.pop(0)
        e = jnp.exp2(value - top).astype(BF)
        late.append(((h, s), nn(jnp.concatenate([sides[s][2][h * 64 : h * 64 + 64], ones], axis=0), e)))
        if len(late) > behind:
            step, r = late.pop(0)
            outs[step] = finish(r)
    for step, r in late:
        outs[step] = finish(r)
    return [jnp.concatenate([outs[h, s] for h in range(HEADS)], axis=0) for s in range(len(sides))]


def refine(xs, msgs, w):
    half = math.sqrt(0.5)
    gain = jnp.concatenate([w["gcol"][...]] * 2, axis=1) * half

    def hidden(i):
        sentT = nn(w["woT"][...], msgs[i]).astype(BF)
        return nt(w["whT"][:, :256], xs[i]) + nn(w["whT"][:, 256:], sentT)

    outs = []
    later = hidden(0)
    for i in range(len(xs)):
        hid = later
        if i + 1 < len(xs):
            later = hidden(i + 1)
        mean = jnp.sum(hid, axis=0, keepdims=True) * (1.0 / 512)
        cen = hid - mean
        var = jnp.sum(cen * cen, axis=0, keepdims=True) * (1.0 / 512)
        z = cen * lax.rsqrt(var + 1e-5) * gain
        outs.append(nn(w["wdT"][...], ((half * z) * (1.0 + lax.erf(z))).astype(BF)).astype(BF))
    return outs


def pair_scores(pairs, w):
    ident = w["ident"][...]
    xs, biases = [], []
    for xi, ki, xj, kj in pairs:
        xs += [xi, xj]
        for keep in (ki, kj):
            bias = (to_col(keep, ident) - 1.0) * 1e30
            biases.append(jnp.concatenate([bias, bias], axis=1))
    attend = [nn(x, w["wa"][...]).astype(BF) for x in xs]
    attendT = [nt(w["waT"][...], x).astype(BF) for x in xs]
    valueT = [nt(w["wvT"][...], x).astype(BF) for x in xs]
    msgs = attention([(attend[i ^ 1], attendT[i], valueT[i ^ 1], biases[i ^ 1]) for i in range(len(xs))])
    deltas = [nt(ident, d).astype(BF) for d in refine(xs, msgs, w)]
    match = [
        nn((x.astype(F32) + d.astype(F32)).astype(BF), w["wm"][...]).astype(BF) for x, d in zip(xs, deltas)
    ]
    return [
        (deltas[i], deltas[i + 1], nt(match[i], match[i + 1]) * (LOG2E / 16.0)) for i in range(0, len(xs), 2)
    ]


def marginals(ki, kj, ident):
    m = jnp.sum(ki, axis=1, keepdims=True)
    n = jnp.sum(kj, axis=1, keepdims=True)
    total = m + n
    off = -jnp.log2(jnp.maximum(total, 1.0))
    kic = to_col(ki.astype(BF), ident)
    lr = off - FORGET * (1.0 - kic)
    lc = off - FORGET * (1.0 - kj)
    lrb = jnp.log2(jnp.maximum(n, 1.0)) + off
    lcb = jnp.log2(jnp.maximum(m, 1.0)) + off
    return total, kic, lr, lc, lrb, lcb


def sink_first(c, bucket, lr, lc, lrb, lcb):
    top = jnp.maximum(jnp.max(c, axis=1, keepdims=True), bucket)
    s = jnp.sum(jnp.exp2(c - top), axis=1, keepdims=True) + jnp.exp2(bucket - top)
    f = lr - top - jnp.log2(s)
    fb = lrb - bucket - math.log2(257.0)
    halves = [jnp.sum(jnp.exp2(c[:, at : at + 128] + f), axis=0, keepdims=True) for at in (0, 128)]
    t = jnp.concatenate(halves, axis=1) + jnp.exp2(bucket + fb)
    tb = jnp.sum(jnp.exp2(bucket + f), axis=0, keepdims=True)[:, :1] + jnp.exp2(bucket + fb)
    return f, fb, lc - jnp.log2(t), lcb - jnp.log2(tb)


def sink_next(c, at, bucket, lr, lc, lrb, lcb, state):
    f, fb, g, gb = state
    eb = jnp.exp2(bucket + fb + g)
    ebb = jnp.exp2(bucket + fb + gb)
    dub = lrb - jnp.log2(jnp.sum(eb, axis=1, keepdims=True) + ebb)
    ub = jnp.exp2(dub)
    p0 = jnp.exp2(c[at, :, :128] + g[:, :128] + f)
    p1 = jnp.exp2(c[at, :, 128:] + g[:, 128:] + f)
    b = jnp.exp2((bucket + gb) + f)
    du = lr - jnp.log2(jnp.sum(p0 + p1, axis=1, keepdims=True) + b)
    u = jnp.exp2(du)
    t = [jnp.sum(p * u, axis=0, keepdims=True) for p in (p0, p1)]
    t = eb * ub + jnp.concatenate(t, axis=1)
    tb = ebb * ub + jnp.sum(b * u, axis=0, keepdims=True)[:, :1]
    return f + du, fb + dub, g + lc - jnp.log2(t), gb + lcb - jnp.log2(tb)


def sink_out(c, total, kic, kj, state):
    f, fb, g, gb = state
    p0 = jnp.exp2(c[:, :128] + g[:, :128] + f)
    p1 = jnp.exp2(c[:, 128:] + g[:, 128:] + f)
    mi = (jnp.sum(p0 + p1, axis=1, keepdims=True) * total * kic).astype(BF)
    halves = [jnp.sum(p, axis=0, keepdims=True) for p in (p0, p1)]
    mj = (jnp.concatenate(halves, axis=1) * total * kj).astype(BF)
    first = (lax.broadcasted_iota(I32, (16, 128), 1) == 0).astype(BF)
    return nt(first, mi)[:1], mj.astype(F32)


def row_of(block, index):
    at = lax.broadcasted_iota(I32, block.shape, 0)
    return jnp.sum(jnp.where(at == index, block, 0.0), axis=0, keepdims=True)


def job_of(tab, q, sub):
    code = tab[0, q * SUBS + sub]
    return (code >> 8) & 7, (code >> 12) & 1


def do_scores(jobs, tab, sub, own, xj, okeep, jkeep, w):
    pairs, swaps = [], []
    for q in jobs:
        mine, swap = job_of(tab, q, sub)
        xm, xo = own[mine], xj[q]
        km = row_of(okeep[...], mine)
        ko = row_of(jkeep[...], q)
        ki = jnp.where(swap == 1, ko, km).astype(BF)
        kj = jnp.where(swap == 1, km, ko).astype(BF)
        pairs.append((jnp.where(swap == 1, xo, xm), ki, jnp.where(swap == 1, xm, xo), kj))
        swaps.append(swap)
    return [
        (jnp.where(swap == 1, dj, di), jnp.where(swap == 1, di, dj), scores)
        for swap, (di, dj, scores) in zip(swaps, pair_scores(pairs, w))
    ]


def do_masses(jobs, sc, tab, sub, okeep, jkeep, bucket, ident):
    swaps, margs, states, kjs = [], [], [], []
    for q, (ref, at) in zip(jobs, sc):
        mine, swap = job_of(tab, q, sub)
        km = row_of(okeep[...], mine)
        ko = row_of(jkeep[...], q)
        ki = jnp.where(swap == 1, ko, km)
        kj = jnp.where(swap == 1, km, ko)
        marg = marginals(ki, kj, ident)
        swaps.append(swap)
        kjs.append(kj)
        margs.append(marg)
        states.append(sink_first(ref[at], bucket, *marg[2:]))

    def sweep(_, states):
        return [sink_next(ref, at, bucket, *m[2:], s) for (ref, at), m, s in zip(sc, margs, states)]

    states = lax.fori_loop(0, ITERS - 1, sweep, states)
    outs = []
    for (ref, at), m, s, kj, swap in zip(sc, margs, states, kjs, swaps):
        a, b = sink_out(ref[at], m[0], m[1], kj, s)
        outs.append((jnp.where(swap == 1, b, a), jnp.where(swap == 1, a, b)))
    return outs


def step_of(turn):
    return (turn // 2 + 1) * (1 - 2 * (turn % 2))


def places():
    n = lax.axis_size("img")
    me = lax.axis_index("img")
    sub = lax.axis_index("sub")
    others = [lax.rem(me + step_of(t) + n, n) for t in range(REACH)]
    peers = [lax.rem(sub + d, SUBS) for d in range(1, SUBS)]
    return me, sub, others, peers


def greet(others, peers):
    barrier = pltpu.get_barrier_semaphore()
    for h in others:
        pl.semaphore_signal(barrier, inc=1, device_id={"img": h}, device_id_type=MESH)
    for s in peers:
        pl.semaphore_signal(barrier, inc=1, device_id={"sub": s}, device_id_type=MESH)
    pl.semaphore_wait(barrier, len(others) + len(peers))


def send(src, dst, ssem, rsem, to):
    return pltpu.make_async_remote_copy(
        src_ref=src, dst_ref=dst, send_sem=ssem, recv_sem=rsem, device_id=to, device_id_type=MESH
    )


def own_rows(pairs, live_count, me, img_count):
    slots = pairs.shape[1]
    up = lax.broadcasted_iota(I32, (slots, slots), 0)
    across = lax.broadcasted_iota(I32, (slots, slots), 1)
    first, second = (
        jnp.sum(jnp.where(up == across, pairs[k : k + 1, :], 0), axis=1, keepdims=True) for k in (0, 1)
    )
    row_ids = lax.broadcasted_iota(I32, (slots, 1), 0)
    ahead = (second >> 3) - me
    ahead = jnp.where(ahead < 0, ahead + img_count, ahead)
    turn = jnp.where(ahead <= WIN, 2 * (ahead - 1), 2 * (img_count - ahead - 1) + 1)
    live = row_ids < live_count
    key = jnp.where(live, turn, 15)
    code = 1 + (first & 7) * 8 + (second & 7)
    key_row = jnp.sum(jnp.where(up == across, key, 0), axis=0, keepdims=True)
    rank = jnp.sum(jnp.where((key_row == key) & (across < up), 1, 0), axis=1, keepdims=True)
    lanes = lax.broadcasted_iota(I32, (slots, 128), 1)
    lane = lax.broadcasted_iota(I32, (1, 128), 1)
    rows = []
    for k in (key, key ^ 1):
        at = jnp.where(live, k * 8 + rank, -1)
        codes = jnp.sum(jnp.where(lanes == at, code, 0), axis=0, keepdims=True)
        counts = jnp.sum(jnp.where((lanes == 64 + k) & live, 1, 0), axis=0, keepdims=True)
        row = codes + counts
        rows.append(jnp.where((lane >= 80) & (lane < 88), live_count, row))
    return rows


def plan_rows(own, near, live_count):
    r8 = lax.broadcasted_iota(I32, (8, 128), 0)
    l8 = lax.broadcasted_iota(I32, (8, 128), 1)
    mine = jnp.where(l8 < 64, l8 >> 3, l8 & 7)
    from_near = jnp.sum(jnp.where((mine == r8) & (r8 < REACH), near, 0), axis=0, keepdims=True)
    slots = 64
    lanes = lax.broadcasted_iota(I32, (slots, 128), 1)
    slot = lax.broadcasted_iota(I32, (slots, 1), 0)
    turn = slot >> 3
    u = slot & 7
    own_all = jnp.broadcast_to(own, (slots, 128))
    near_all = jnp.broadcast_to(from_near, (slots, 128))

    def pick(table, lane):
        return jnp.sum(jnp.where(lanes == lane, table, 0), axis=1, keepdims=True)

    n_own = pick(own_all, 64 + turn)
    n_near = pick(near_all, 64 + turn)
    l_near = pick(near_all, 80 + turn)

    def sixth(value):
        return (jnp.maximum(value, 0) * 43) >> 8

    give = jnp.maximum(jnp.minimum(jnp.minimum(sixth(live_count - l_near), n_own), MOST - n_near), 0)
    take = jnp.maximum(jnp.minimum(jnp.minimum(sixth(l_near - live_count), n_near), MOST - n_own), 0)
    kept = n_own - give
    near_kept = n_near - take
    own_code = pick(own_all, turn * 8 + u) - 1
    near_code = pick(near_all, turn * 8 + u) - 1
    taken_code = pick(near_all, turn * 8 + near_kept + u - kept) - 1
    given_code = pick(own_all, turn * 8 + kept + u - near_kept) - 1
    live = (u < kept + take) & (turn < REACH)
    image = jnp.where(u < kept, own_code >> 3, taken_code & 7)
    swap = jnp.where(u < kept, 0, 1)
    asked = (u < near_kept + give) & (turn < REACH)
    sends = jnp.where(u < near_kept, near_code & 7, given_code >> 3)
    eye64 = lax.broadcasted_iota(I32, (slots, slots), 0) == lax.broadcasted_iota(I32, (slots, slots), 1)
    live_row = jnp.sum(jnp.where(eye64, jnp.where(live, 1, 0), 0), axis=0, keepdims=True)
    short = lax.broadcasted_iota(I32, (slots, slots), 1)
    place = jnp.sum(jnp.where(short < slot, live_row, 0), axis=1, keepdims=True)
    count = jnp.sum(live_row, axis=1, keepdims=True)

    def put(lane, value):
        return jnp.sum(jnp.where(lanes == lane, value, 0), axis=0, keepdims=True)

    by_place = put(jnp.where(live, place, -1), 1 + slot + image * 256 + swap * 4096)
    by_slot = put(slot, jnp.where(asked, 1 + sends, 0))
    places_row = put(slot, jnp.where(live, place, 0))
    row = lax.broadcasted_iota(I32, (8, 128), 0)
    out = jnp.where(row == 0, by_place, jnp.where(row == 1, by_slot, jnp.where(row == 2, places_row, count)))
    return out


def own_mask(counts, visible, sub):
    image = lax.broadcasted_iota(I32, (OWN, ROWS), 0)
    found = jnp.zeros((OWN, ROWS), I32)
    for a in range(OWN):
        found = jnp.where(image == a, counts[a], found)
    spot = lax.broadcasted_iota(I32, (OWN, ROWS), 1) + sub * ROWS
    kept = jnp.where((spot < found) & (visible[...] > 0), 1.0, 0.0)
    return my_lanes(jnp.concatenate([kept] * SUBS, axis=1), sub)


def my_lanes(wide, sub):
    lane = lax.broadcasted_iota(I32, wide.shape, 1)
    return jnp.where((lane >= sub * ROWS) & (lane < sub * ROWS + ROWS), wide, 0.0)


def meet_kernel(
    pairs, pair_count, counts, desc_far, visible_far, wa_far, wv_far, wo_far, wh_far, gain_far, wd_far,
    tab, waT, wvT, woT, whT, wdT, gcol, upper, okeep, told, near, omask, desc, visible, wa, wv, wo, wh, gain, wd,
    ssem, rsem, osem, orem, lsem,
):
    me, sub, others, peers = places()
    far = (desc_far, visible_far, wa_far, wv_far, wo_far, wh_far, gain_far, wd_far)
    loads = [
        pltpu.make_async_copy(src, dst, lsem.at[i])
        for i, (src, dst) in enumerate(zip(far, (desc, visible, wa, wv, wo, wh, gain, wd)))
    ]
    for load in loads:
        load.start()
    own, out = own_rows(pairs[...], pair_count[0], me, lax.axis_size("img"))
    told[...] = jnp.broadcast_to(out, (8, 128))
    for load in loads[:2]:
        load.wait()
    omask[0] = own_mask(counts, visible, sub)
    greet(others, peers)
    ocopies = []
    for d in range(1, SUBS):
        to = {"sub": peers[d - 1]}
        ocopies.append(send(omask.at[0], omask.at[d], osem.at[1, d - 1], orem.at[1, d - 1], to))
        ocopies.append(send(desc.at[:, 0:HALF, :], upper.at[sub], osem.at[0, d - 1], orem.at[0, d - 1], to))
    copies = [send(told, near.at[t ^ 1], ssem.at[t], rsem.at[t ^ 1], {"img": others[t]}) for t in range(REACH)]
    for copy in copies + ocopies:
        copy.start()
    upper[sub] = desc[:, 0:HALF, :]
    for load in loads[2:]:
        load.wait()
    prepare(wa, wv, wo, wh, gain, wd, waT, wvT, woT, whT, wdT, gcol)
    for copy in copies:
        copy.wait()
    row = lax.broadcasted_iota(I32, (8, 128), 0)
    table = jnp.zeros((8, 128), I32)
    for t in range(REACH):
        table = jnp.where(row == t, near[t], table)
    tab[...] = plan_rows(own, table, pair_count[0])
    for copy in ocopies:
        copy.wait()
    okeep[...] = omask[0] + omask[1] + omask[2] + omask[3]


def sent_image(tab, t, u):
    return tab[1, t * 8 + u]


def fetch_kernel(
    tab, desc, upper, okeep, own, xj, jkeep, zst, zl0, zl1, zl2, zl3, zms, zml, yst, yl, yms, yml, lower,
    zsem, zrem, ysem, yrem, osem, orem,
):
    me, sub, others, peers = places()
    zland = (zl0, zl1, zl2, zl3)
    wide = my_lanes(okeep[...], sub)
    greet(others, peers)
    order = (4, 5, 2, 3, 0, 1)
    line = lax.broadcasted_iota(I32, (8, KEYS), 0)
    zmcopies = []
    for t in order:
        masks = jnp.zeros((8, KEYS), F32)
        for u in range(MOST):
            masks = jnp.where(line == u, row_of(wide, jnp.maximum(sent_image(tab, t, u) - 1, 0)), masks)
        zms[t] = masks
        zmcopies.append(
            send(zms.at[t], zml.at[t ^ 1], zsem.at[PARTS, t], zrem.at[PARTS, t ^ 1], {"img": others[t]})
        )
        zmcopies[-1].start()
    zcopies = []
    for c in range(PARTS):
        zcopies.append([])
        for t in order:
            for u in range(MOST):
                which = jnp.maximum(sent_image(tab, t, u) - 1, 0)
                zst[c, t, u] = desc[which, c * PART : c * PART + PART, :]
            copy = send(zst.at[c, t], zland[c].at[t ^ 1], zsem.at[c, t], zrem.at[c, t ^ 1], {"img": others[t]})
            copy.start()
            zcopies[c].append(copy)
    ocopies = []
    for d in range(1, SUBS):
        copy = send(desc.at[:, HALF:ROWS, :], lower.at[sub], osem.at[d - 1], orem.at[d - 1], {"sub": peers[d - 1]})
        copy.start()
        ocopies.append(copy)
    lower[sub] = desc[:, HALF:ROWS, :]
    for copy in zmcopies:
        copy.wait()
    zmasks = jnp.concatenate([zml[t] for t in range(REACH)], axis=0)
    slots = []
    for d in range(SUBS):
        worker = sub if d == 0 else peers[d - 1]
        slots.append([jnp.maximum((tab[0, q * SUBS + worker] & 255) - 1, 0) for q in range(JOBS)])
        masks = jnp.zeros((JOBS, KEYS), F32)
        for q in range(JOBS):
            masks = jnp.where(line == q, row_of(zmasks, slots[d][q]), masks)
        yms[d] = masks
    ycopies = []
    for d in range(1, SUBS):
        to = {"sub": peers[d - 1]}
        ycopies.append(send(yms.at[d], yml.at[d - 1], ysem.at[PARTS, d - 1], yrem.at[PARTS, d - 1], to))
        ycopies[-1].start()
    for c in range(PARTS):
        for copy in zcopies[c]:
            copy.wait()
        for d in range(1, SUBS):
            for q in range(JOBS):
                yst[c, d - 1, q] = zland[c][slots[d][q] >> 3, slots[d][q] & 7]
            copy = send(yst.at[c, d - 1], yl.at[c, sub], ysem.at[c, d - 1], yrem.at[c, d - 1], {"sub": peers[d - 1]})
            copy.start()
            ycopies.append(copy)
        for q in range(JOBS):
            yl[c, sub, q] = zland[c][slots[0][q] >> 3, slots[0][q] & 7]
    for copy in ocopies:
        copy.wait()
    for s in range(SUBS):
        own[:, s * ROWS : s * ROWS + HALF, :] = upper[s]
        own[:, s * ROWS + HALF : s * ROWS + ROWS, :] = lower[s]
    for copy in ycopies:
        copy.wait()
    for s in range(SUBS):
        for c in range(PARTS):
            at = s * ROWS + c * PART
            xj[:, at : at + PART, :] = yl[c, s]
    jkeep[...] = yms[0] + yml[0] + yml[1] + yml[2]


def work_kernel(
    tab, own, xj, okeep, jkeep, bucket, wa, wm, waT, wvT, woT, whT, wdT, gcol, dmine, dother, mm, mo, ident, sc
):
    sub = lax.axis_index("sub")
    ident[...] = eye(256)
    w = dict(wa=wa, wm=wm, waT=waT, wvT=wvT, woT=woT, whT=whT, wdT=wdT, gcol=gcol, ident=ident)
    n = ((tab[3, 0] + (SUBS - 1) - sub) >> 2) - FIXED
    binv = bucket[...] * LOG2E

    def late(ps):
        outs = do_scores([FIXED + p for p in ps], tab, sub, own, xj, okeep, jkeep, w)
        for p, out in zip(ps, outs):
            dmine[p], dother[p], sc[p] = out
        outs = do_masses([FIXED + p for p in ps], [(sc, p) for p in ps], tab, sub, okeep, jkeep, binv, ident[...])
        for p, (a, b) in zip(ps, outs):
            mm[p] = jnp.broadcast_to(a, (8, KEYS))
            mo[p] = jnp.broadcast_to(b, (8, KEYS))

    @pl.loop(0, n >> 1)
    def _(p):
        late([2 * p, 2 * p + 1])

    @pl.when((n & 1) == 1)
    def _():
        late([n - 1])


def give_kernel(
    tab, own, xj, okeep, jkeep, bucket, wa, wm, waT, wvT, woT, whT, wdT, gcol, dmine2, dother2, mm2, mo2,
    zret, zmr, gm, mparts, mgot, ident, dmine, dother, sc, yb0, yb1, yb2, yb3, ymst, yml, zst, zms,
    ysem, yrem, zsem, zrem, osem, orem,
):
    me, sub, others, peers = places()
    yb = (yb0, yb1, yb2, yb3)
    ident[...] = eye(256)
    w = dict(wa=wa, wm=wm, waT=waT, wvT=wvT, woT=woT, whT=whT, wdT=wdT, gcol=gcol, ident=ident)
    binv = bucket[...] * LOG2E
    mline = lax.broadcasted_iota(I32, (JOBS, KEYS), 0)
    order = (4, 5, 2, 3, 0, 1)

    def rows_of(p, c):
        return pl.ds(pl.multiple_of(p * ROWS + c * PART, PART), PART)

    def block_of(p):
        return pl.ds(pl.multiple_of(p * ROWS, ROWS), ROWS)

    greet(others, peers)
    ycopies = [[] for _ in range(PARTS)]
    ocopies = []

    def hand_back(group, theirs, at, to):
        for c in range(PARTS):
            for d in range(1, SUBS):
                p = peers[d - 1]
                copy = send(
                    theirs.at[at, rows_of(p, c), :], yb[c].at[sub, to], ysem.at[group, c, d - 1], yrem.at[group, c, d - 1], {"sub": p}
                )
                copy.start()
                ycopies[c].append(copy)
        for c in range(PARTS):
            yb[c][sub, to] = theirs[at, rows_of(sub, c), :]

    def hand_mine(group, mine, at, to):
        for d in range(1, SUBS):
            p = peers[d - 1]
            copy = send(mine.at[at, block_of(p), :], gm.at[sub, to], osem.at[group, d - 1], orem.at[group, d - 1], {"sub": p})
            copy.start()
            ocopies.append(copy)
        gm[sub, to] = mine[at, block_of(sub), :]

    hand_back(2, dother2, slice(0, JOBS - FIXED), slice(FIXED, JOBS))
    for group in range(2):
        at = slice(2 * group, 2 * group + 2)
        outs = do_scores([2 * group, 2 * group + 1], tab, sub, own, xj, okeep, jkeep, w)
        for q, out in enumerate(outs, 2 * group):
            dmine[q], dother[q], sc[q] = out
        hand_back(group, dother, at, at)
    n = (tab[3, 0] + (SUBS - 1) - sub) >> 2
    owners = [jnp.where(q < n, job_of(tab, q, sub)[0], -1) for q in range(JOBS)]
    places_of = [[tab[2, t * 8 + u] for u in range(MOST)] for t in range(REACH)]
    zcopies = [[] for _ in range(PARTS)]

    def pass_on(c):
        for copy in ycopies[c]:
            copy.wait()
        for t in order:
            for u in range(MOST):
                zst[c, t, u] = yb[c][places_of[t][u] & 3, places_of[t][u] >> 2]
            copy = send(zst.at[c, t], zret.at[c, t ^ 1], zsem.at[c, t], zrem.at[c, t ^ 1], {"img": others[t]})
            copy.start()
            zcopies[c].append(copy)

    def some_masses(qs):
        return do_masses(qs, [(sc, q) for q in qs], tab, sub, okeep, jkeep, binv, ident[...])

    for c in range(PARTS):
        pass_on(c)
    hand_mine(2, dmine2, slice(0, JOBS - FIXED), slice(FIXED, JOBS))
    for group in range(2):
        at = slice(2 * group, 2 * group + 2)
        hand_mine(group, dmine, at, at)
    masses = some_masses([0, 1])
    masses += some_masses([2, 3])
    mine = [masses[q][0] if q < FIXED else mm2[q - FIXED, 0:1, :] for q in range(JOBS)]
    away = [masses[q][1] if q < FIXED else mo2[q - FIXED, 0:1, :] for q in range(JOBS)]
    table = jnp.zeros((JOBS, KEYS), F32)
    for q in range(JOBS):
        table = jnp.where(mline == q, away[q], table)
    ymst[...] = table
    yml[sub] = table
    ymcopies = []
    for d in range(1, SUBS):
        to = {"sub": peers[d - 1]}
        ymcopies.append(send(ymst, yml.at[sub], ysem.at[3, 0, d - 1], yrem.at[3, 0, d - 1], to))
        ymcopies[-1].start()
    table = jnp.zeros((OWN, KEYS), F32)
    for a in range(OWN):
        for q in range(JOBS):
            table = table + jnp.where((mline == a) & (owners[q] == a), mine[q], 0.0)
    mparts[...] = table
    for d in range(1, SUBS):
        copy = send(mparts, mgot.at[d - 1], osem.at[3, d - 1], orem.at[3, d - 1], {"sub": peers[d - 1]})
        copy.start()
        ocopies.append(copy)
    for copy in ymcopies:
        copy.wait()
    ymasses = jnp.concatenate([yml[s] for s in range(SUBS)], axis=0)
    zmcopies = []
    for t in order:
        back = jnp.zeros((8, KEYS), F32)
        for u in range(MOST):
            place = places_of[t][u]
            back = jnp.where(mline == u, row_of(ymasses, (place & 3) * JOBS + (place >> 2)), back)
        zms[t] = back
        to = {"img": others[t]}
        zmcopies.append(send(zms.at[t], zmr.at[t ^ 1], zsem.at[PARTS, t], zrem.at[PARTS, t ^ 1], to))
        zmcopies[-1].start()
    for copy in ocopies + zmcopies:
        copy.wait()
    for c in range(PARTS):
        for copy in zcopies[c]:
            copy.wait()


def sum_kernel(tab, zret, zmr, gm, mparts, mgot, upd, mass, acc, macc):
    sub = lax.axis_index("sub")
    acc[...] = jnp.zeros_like(acc)

    @pl.loop(0, SUBS * JOBS)
    def _(g):
        code = tab[0, g]

        @pl.when(code > 0)
        def _():
            which = (code >> 8) & 7
            acc[which] = acc[which] + gm[g & 3, g >> 2].astype(F32)

    macc[...] = mparts[...] + mgot[0] + mgot[1] + mgot[2]
    line = lax.broadcasted_iota(I32, (8, KEYS), 0)

    @pl.loop(0, REACH)
    def _(t):
        for u in range(MOST):
            which = tab[1, t * 8 + u] - 1

            @pl.when(which >= 0)
            def _():
                for c in range(PARTS):
                    rows = slice(c * PART, c * PART + PART)
                    acc[which, rows] = acc[which, rows] + zret[c, t, u].astype(F32)
                macc[...] = macc[...] + jnp.where(line == which, zmr[t, u : u + 1, :], 0.0)

    upd[...] = acc[...].astype(BF)
    total = macc[...]
    out = jnp.zeros((OWN, ROWS), F32)
    for s in range(SUBS):
        out = jnp.where(sub == s, total[:, s * ROWS : s * ROWS + ROWS], out)
    mass[...] = out


VM = pl.BlockSpec(memory_space=pltpu.VMEM)
SM = pl.BlockSpec(memory_space=pltpu.SMEM)
DMA = pltpu.SemaphoreType.DMA
HB = pl.BlockSpec(memory_space=pltpu.HBM)


def shape(dims, kind=BF):
    return jax.ShapeDtypeStruct(dims, kind)


def talk(number, limit=LIMIT):
    return pltpu.CompilerParams(collective_id=number, has_side_effects=True, vmem_limit_bytes=limit)


COST = pl.CostEstimate(flops=10**10, bytes_accessed=5 * 10**7, transcendentals=10**7)


def local(descriptors, counts, visible, pair_list, pair_count, w_attend, w_value, w_output, w_hidden, norm_gain, w_down, w_match, unassigned_bucket):
    V = pltpu.VMEM
    peer = (SUBS - 1,)
    tab, *ready, upper, okeep = pl.pallas_call(
        meet_kernel,
        out_shape=(
            shape((8, 128), I32), *[shape((256, 256))] * 3, shape((512, 512)), shape((256, 512)), shape((512, 128), F32),
            shape((SUBS, OWN, HALF, D)), shape((OWN, KEYS), F32),
        ),
        in_specs=[VM, SM, SM] + [HB] * 8,
        out_specs=(VM,) * 9,
        scratch_shapes=[
            V((8, 128), I32), V((REACH, 8, 128), I32), V((SUBS, OWN, KEYS), F32),
            V((OWN, ROWS, D), BF), V((OWN, ROWS), I32), *[V((256, 256), BF)] * 3, V((512, 512), BF), V((1, 512), F32), V((512, 256), BF),
            DMA((REACH,)), DMA((REACH,)), DMA((2, SUBS - 1)), DMA((2, SUBS - 1)), DMA((8,)),
        ],
        compiler_params=talk(0, 56 * 2**20),
        cost_estimate=COST,
    )(pair_list.T, pair_count, counts, descriptors, visible, w_attend, w_value, w_output, w_hidden, norm_gain.reshape(1, -1), w_down)
    own, xj, jkeep = pl.pallas_call(
        fetch_kernel,
        out_shape=(shape((OWN, KEYS, D)), shape((JOBS, KEYS, D)), shape((JOBS, KEYS), F32)),
        in_specs=[SM, VM, VM, VM],
        out_specs=(VM,) * 3,
        scratch_shapes=[
            V((PARTS, REACH, MOST, PART, D), BF), *[V((REACH, MOST, PART, D), BF)] * PARTS, V((REACH, 8, KEYS), F32), V((REACH, 8, KEYS), F32),
            V((PARTS, SUBS - 1, JOBS, PART, D), BF), V((PARTS, SUBS, JOBS, PART, D), BF), V((SUBS, JOBS, KEYS), F32), V((SUBS - 1, JOBS, KEYS), F32),
            V((SUBS, OWN, ROWS - HALF, D), BF),
            DMA((PARTS + 1, REACH)), DMA((PARTS + 1, REACH)), DMA((PARTS + 1, SUBS - 1)), DMA((PARTS + 1, SUBS - 1)), DMA(peer), DMA(peer),
        ],
        compiler_params=talk(1),
        cost_estimate=COST,
    )(tab, descriptors, upper, okeep)
    bucket = unassigned_bucket.reshape(1, 1)
    late = JOBS - FIXED
    common = (tab, own, xj, okeep, jkeep, bucket, w_attend, w_match, *ready)
    rest = pl.pallas_call(
        work_kernel,
        out_shape=(shape((late, KEYS, D)), shape((late, KEYS, D)), shape((late, 8, KEYS), F32), shape((late, 8, KEYS), F32)),
        in_specs=[SM] + [VM] * 13,
        out_specs=(VM,) * 4,
        scratch_shapes=[V((256, 256), BF), V((late, KEYS, KEYS), F32)],
        compiler_params=pltpu.CompilerParams(vmem_limit_bytes=LIMIT),
    )(*common)
    back = pl.pallas_call(
        give_kernel,
        out_shape=(
            shape((PARTS, REACH, MOST, PART, D)), shape((REACH, 8, KEYS), F32), shape((SUBS, JOBS, ROWS, D)),
            shape((OWN, KEYS), F32), shape((SUBS - 1, OWN, KEYS), F32),
        ),
        in_specs=[SM] + [VM] * 17,
        out_specs=(VM,) * 5,
        scratch_shapes=[
            V((256, 256), BF), V((FIXED, KEYS, D), BF), V((FIXED, KEYS, D), BF), V((FIXED, KEYS, KEYS), F32),
            *[V((SUBS, JOBS, PART, D), BF)] * PARTS, V((JOBS, KEYS), F32), V((SUBS, JOBS, KEYS), F32),
            V((PARTS, REACH, MOST, PART, D), BF), V((REACH, 8, KEYS), F32),
            DMA((4, PARTS, SUBS - 1)), DMA((4, PARTS, SUBS - 1)), DMA((PARTS + 1, REACH)), DMA((PARTS + 1, REACH)), DMA((4, SUBS - 1)), DMA((4, SUBS - 1)),
        ],
        compiler_params=talk(2),
        cost_estimate=COST,
    )(*common, *rest)
    return pl.pallas_call(
        sum_kernel,
        out_shape=(shape((OWN, ROWS, D)), shape((OWN, ROWS), F32)),
        in_specs=[SM] + [VM] * 5,
        out_specs=(VM, VM),
        scratch_shapes=[V((OWN, ROWS, D), F32), V((OWN, KEYS), F32)],
        compiler_params=pltpu.CompilerParams(vmem_limit_bytes=LIMIT),
    )(tab, *back)


def solution(mesh):
    placed = (P("img", "sub", None), P("img"), P("img", "sub"), P("img", None), P("img")) + (P(),) * 8
    return jax.shard_map(
        local, mesh=mesh, in_specs=placed, out_specs=(P("img", "sub", None), P("img", "sub")), check_vma=False
    )
```

```python
import math

import jax
import jax.numpy as jnp
from jax import lax
from jax.experimental import pallas as pl
from jax.experimental.pallas import tpu as pltpu
from jax.sharding import PartitionSpec as P

BF = jnp.bfloat16
F32 = jnp.float32
I32 = jnp.int32
LOG2E = 1.4426950408889634
FORGET = 30.0 * LOG2E
HEADS = 4
ITERS = 10
KEYS = 256
D = 256
WIN = 3
REACH = 2 * WIN
MOST = 6
OWN = 8
ROWS = 64
SUBS = 4
JOBS = 8
FIXED = 4
PARTS = 4
PART = ROWS // PARTS
MESH = pl.DeviceIdType.MESH
LIMIT = 24 * 2**20


def nn(a, b):
    return lax.dot_general(a, b, (((1,), (0,)), ((), ())), preferred_element_type=F32)


def nt(a, b):
    return lax.dot_general(a, b, (((1,), (1,)), ((), ())), preferred_element_type=F32)


def eye(n):
    up = lax.broadcasted_iota(I32, (n, n), 0)
    return (up == lax.broadcasted_iota(I32, (n, n), 1)).astype(BF)


def to_col(row, ident):
    return nt(ident, jnp.broadcast_to(row, (128, row.shape[1])))


def prepare(wa, wv, wo, wh, gain, wd, waT, wvT, woT, whT, wdT, gcol):
    ident = eye(256)
    waT[...] = nt(ident, wa[...]).astype(BF)
    wvT[...] = nt(ident, wv[...]).astype(BF)
    woT[...] = nt(ident, wo[...]).astype(BF)
    for a in range(0, 512, 256):
        for b in range(0, 512, 256):
            whT[a : a + 256, b : b + 256] = nt(ident, wh[b : b + 256, a : a + 256]).astype(BF)
    for b in range(0, 512, 256):
        wdT[:, b : b + 256] = nt(ident, wd[b : b + 256, :]).astype(BF)
    same = lax.broadcasted_iota(I32, (128, 128), 0) == lax.broadcasted_iota(I32, (128, 128), 1)
    for q in range(0, 512, 128):
        spread = jnp.broadcast_to(gain[:, q : q + 128], (128, 128))
        column = jnp.sum(jnp.where(same, spread, 0.0), axis=1, keepdims=True)
        gcol[q : q + 128, :] = jnp.broadcast_to(column, (128, 128))


def attention(sides, ahead=4, behind=2):
    ones = jnp.ones((16, KEYS), BF)
    steps = [(h, s) for h in range(HEADS) for s in range(len(sides))]

    def similarity(h, s):
        a_other, aT_self, _, bias = sides[s]
        sl = slice(h * 64, h * 64 + 64)
        value = nn(a_other[:, sl], aT_self[sl]) * (LOG2E / 8.0) + bias
        return value, jnp.max(value, axis=0, keepdims=True)

    def finish(r):
        return (r[:64] * (1.0 / r[64:65])).astype(BF)

    waiting = [similarity(*step) for step in steps[:ahead]]
    late = []
    outs = {}
    for i, (h, s) in enumerate(steps):
        if i + ahead < len(steps):
            waiting.append(similarity(*steps[i + ahead]))
        value, top = waiting.pop(0)
        e = jnp.exp2(value - top).astype(BF)
        late.append(((h, s), nn(jnp.concatenate([sides[s][2][h * 64 : h * 64 + 64], ones], axis=0), e)))
        if len(late) > behind:
            step, r = late.pop(0)
            outs[step] = finish(r)
    for step, r in late:
        outs[step] = finish(r)
    return [jnp.concatenate([outs[h, s] for h in range(HEADS)], axis=0) for s in range(len(sides))]


def refine(xs, msgs, w):
    half = math.sqrt(0.5)
    gain = jnp.concatenate([w["gcol"][...]] * 2, axis=1) * half

    def hidden(i):
        sentT = nn(w["woT"][...], msgs[i]).astype(BF)
        return nt(w["whT"][:, :256], xs[i]) + nn(w["whT"][:, 256:], sentT)

    outs = []
    later = hidden(0)
    for i in range(len(xs)):
        hid = later
        if i + 1 < len(xs):
            later = hidden(i + 1)
        mean = jnp.sum(hid, axis=0, keepdims=True) * (1.0 / 512)
        cen = hid - mean
        var = jnp.sum(cen * cen, axis=0, keepdims=True) * (1.0 / 512)
        z = cen * lax.rsqrt(var + 1e-5) * gain
        outs.append(nn(w["wdT"][...], ((half * z) * (1.0 + lax.erf(z))).astype(BF)).astype(BF))
    return outs


def pair_scores(pairs, w):
    ident = w["ident"][...]
    xs, biases = [], []
    for xi, ki, xj, kj in pairs:
        xs += [xi, xj]
        for keep in (ki, kj):
            bias = (to_col(keep, ident) - 1.0) * 1e30
            biases.append(jnp.concatenate([bias, bias], axis=1))
    attend = [nn(x, w["wa"][...]).astype(BF) for x in xs]
    attendT = [nt(w["waT"][...], x).astype(BF) for x in xs]
    valueT = [nt(w["wvT"][...], x).astype(BF) for x in xs]
    msgs = attention([(attend[i ^ 1], attendT[i], valueT[i ^ 1], biases[i ^ 1]) for i in range(len(xs))])
    deltas = [nt(ident, d).astype(BF) for d in refine(xs, msgs, w)]
    match = [
        nn((x.astype(F32) + d.astype(F32)).astype(BF), w["wm"][...]).astype(BF) for x, d in zip(xs, deltas)
    ]
    return [
        (deltas[i], deltas[i + 1], nt(match[i], match[i + 1]) * (LOG2E / 16.0)) for i in range(0, len(xs), 2)
    ]


def marginals(ki, kj, ident):
    m = jnp.sum(ki, axis=1, keepdims=True)
    n = jnp.sum(kj, axis=1, keepdims=True)
    total = m + n
    off = -jnp.log2(jnp.maximum(total, 1.0))
    kic = to_col(ki.astype(BF), ident)
    lr = off - FORGET * (1.0 - kic)
    lc = off - FORGET * (1.0 - kj)
    lrb = jnp.log2(jnp.maximum(n, 1.0)) + off
    lcb = jnp.log2(jnp.maximum(m, 1.0)) + off
    return total, kic, lr, lc, lrb, lcb


def sink_first(c, bucket, lr, lc, lrb, lcb):
    top = jnp.maximum(jnp.max(c, axis=1, keepdims=True), bucket)
    s = jnp.sum(jnp.exp2(c - top), axis=1, keepdims=True) + jnp.exp2(bucket - top)
    f = lr - top - jnp.log2(s)
    fb = lrb - bucket - math.log2(257.0)
    halves = [jnp.sum(jnp.exp2(c[:, at : at + 128] + f), axis=0, keepdims=True) for at in (0, 128)]
    t = jnp.concatenate(halves, axis=1) + jnp.exp2(bucket + fb)
    tb = jnp.sum(jnp.exp2(bucket + f), axis=0, keepdims=True)[:, :1] + jnp.exp2(bucket + fb)
    return f, fb, lc - jnp.log2(t), lcb - jnp.log2(tb)


def sink_next(c, at, bucket, lr, lc, lrb, lcb, state):
    f, fb, g, gb = state
    eb = jnp.exp2(bucket + fb + g)
    ebb = jnp.exp2(bucket + fb + gb)
    dub = lrb - jnp.log2(jnp.sum(eb, axis=1, keepdims=True) + ebb)
    ub = jnp.exp2(dub)
    p0 = jnp.exp2(c[at, :, :128] + g[:, :128] + f)
    p1 = jnp.exp2(c[at, :, 128:] + g[:, 128:] + f)
    b = jnp.exp2((bucket + gb) + f)
    du = lr - jnp.log2(jnp.sum(p0 + p1, axis=1, keepdims=True) + b)
    u = jnp.exp2(du)
    t = [jnp.sum(p * u, axis=0, keepdims=True) for p in (p0, p1)]
    t = eb * ub + jnp.concatenate(t, axis=1)
    tb = ebb * ub + jnp.sum(b * u, axis=0, keepdims=True)[:, :1]
    return f + du, fb + dub, g + lc - jnp.log2(t), gb + lcb - jnp.log2(tb)


def sink_out(c, total, kic, kj, state):
    f, fb, g, gb = state
    p0 = jnp.exp2(c[:, :128] + g[:, :128] + f)
    p1 = jnp.exp2(c[:, 128:] + g[:, 128:] + f)
    mi = (jnp.sum(p0 + p1, axis=1, keepdims=True) * total * kic).astype(BF)
    halves = [jnp.sum(p, axis=0, keepdims=True) for p in (p0, p1)]
    mj = (jnp.concatenate(halves, axis=1) * total * kj).astype(BF)
    first = (lax.broadcasted_iota(I32, (16, 128), 1) == 0).astype(BF)
    return nt(first, mi)[:1], mj.astype(F32)


def row_of(block, index):
    at = lax.broadcasted_iota(I32, block.shape, 0)
    return jnp.sum(jnp.where(at == index, block, 0.0), axis=0, keepdims=True)


def job_of(tab, q, sub):
    code = tab[0, q * SUBS + sub]
    return (code >> 8) & 7, (code >> 12) & 1


def do_scores(jobs, tab, sub, own, xj, okeep, jkeep, w):
    pairs, swaps = [], []
    for q in jobs:
        mine, swap = job_of(tab, q, sub)
        xm, xo = own[mine], xj[q]
        km = row_of(okeep[...], mine)
        ko = row_of(jkeep[...], q)
        ki = jnp.where(swap == 1, ko, km).astype(BF)
        kj = jnp.where(swap == 1, km, ko).astype(BF)
        pairs.append((jnp.where(swap == 1, xo, xm), ki, jnp.where(swap == 1, xm, xo), kj))
        swaps.append(swap)
    return [
        (jnp.where(swap == 1, dj, di), jnp.where(swap == 1, di, dj), scores)
        for swap, (di, dj, scores) in zip(swaps, pair_scores(pairs, w))
    ]


def do_masses(jobs, sc, tab, sub, okeep, jkeep, bucket, ident):
    swaps, margs, states, kjs = [], [], [], []
    for q, (ref, at) in zip(jobs, sc):
        mine, swap = job_of(tab, q, sub)
        km = row_of(okeep[...], mine)
        ko = row_of(jkeep[...], q)
        ki = jnp.where(swap == 1, ko, km)
        kj = jnp.where(swap == 1, km, ko)
        marg = marginals(ki, kj, ident)
        swaps.append(swap)
        kjs.append(kj)
        margs.append(marg)
        states.append(sink_first(ref[at], bucket, *marg[2:]))

    def sweep(_, states):
        return [sink_next(ref, at, bucket, *m[2:], s) for (ref, at), m, s in zip(sc, margs, states)]

    states = lax.fori_loop(0, ITERS - 1, sweep, states)
    outs = []
    for (ref, at), m, s, kj, swap in zip(sc, margs, states, kjs, swaps):
        a, b = sink_out(ref[at], m[0], m[1], kj, s)
        outs.append((jnp.where(swap == 1, b, a), jnp.where(swap == 1, a, b)))
    return outs


def step_of(turn):
    return (turn // 2 + 1) * (1 - 2 * (turn % 2))


def places():
    n = lax.axis_size("img")
    me = lax.axis_index("img")
    sub = lax.axis_index("sub")
    others = [lax.rem(me + step_of(t) + n, n) for t in range(REACH)]
    peers = [lax.rem(sub + d, SUBS) for d in range(1, SUBS)]
    return me, sub, others, peers


def greet(others, peers):
    barrier = pltpu.get_barrier_semaphore()
    for h in others:
        pl.semaphore_signal(barrier, inc=1, device_id={"img": h}, device_id_type=MESH)
    for s in peers:
        pl.semaphore_signal(barrier, inc=1, device_id={"sub": s}, device_id_type=MESH)
    pl.semaphore_wait(barrier, len(others) + len(peers))


def send(src, dst, ssem, rsem, to):
    return pltpu.make_async_remote_copy(
        src_ref=src, dst_ref=dst, send_sem=ssem, recv_sem=rsem, device_id=to, device_id_type=MESH
    )


def own_rows(pairs, live_count, me, img_count):
    slots = pairs.shape[1]
    up = lax.broadcasted_iota(I32, (slots, slots), 0)
    across = lax.broadcasted_iota(I32, (slots, slots), 1)
    first, second = (
        jnp.sum(jnp.where(up == across, pairs[k : k + 1, :], 0), axis=1, keepdims=True) for k in (0, 1)
    )
    row_ids = lax.broadcasted_iota(I32, (slots, 1), 0)
    ahead = (second >> 3) - me
    ahead = jnp.where(ahead < 0, ahead + img_count, ahead)
    turn = jnp.where(ahead <= WIN, 2 * (ahead - 1), 2 * (img_count - ahead - 1) + 1)
    live = row_ids < live_count
    key = jnp.where(live, turn, 15)
    code = 1 + (first & 7) * 8 + (second & 7)
    key_row = jnp.sum(jnp.where(up == across, key, 0), axis=0, keepdims=True)
    rank = jnp.sum(jnp.where((key_row == key) & (across < up), 1, 0), axis=1, keepdims=True)
    lanes = lax.broadcasted_iota(I32, (slots, 128), 1)
    lane = lax.broadcasted_iota(I32, (1, 128), 1)
    rows = []
    for k in (key, key ^ 1):
        at = jnp.where(live, k * 8 + rank, -1)
        codes = jnp.sum(jnp.where(lanes == at, code, 0), axis=0, keepdims=True)
        counts = jnp.sum(jnp.where((lanes == 64 + k) & live, 1, 0), axis=0, keepdims=True)
        row = codes + counts
        rows.append(jnp.where((lane >= 80) & (lane < 88), live_count, row))
    return rows


def plan_rows(own, near, live_count):
    r8 = lax.broadcasted_iota(I32, (8, 128), 0)
    l8 = lax.broadcasted_iota(I32, (8, 128), 1)
    mine = jnp.where(l8 < 64, l8 >> 3, l8 & 7)
    from_near = jnp.sum(jnp.where((mine == r8) & (r8 < REACH), near, 0), axis=0, keepdims=True)
    slots = 64
    lanes = lax.broadcasted_iota(I32, (slots, 128), 1)
    slot = lax.broadcasted_iota(I32, (slots, 1), 0)
    turn = slot >> 3
    u = slot & 7
    own_all = jnp.broadcast_to(own, (slots, 128))
    near_all = jnp.broadcast_to(from_near, (slots, 128))

    def pick(table, lane):
        return jnp.sum(jnp.where(lanes == lane, table, 0), axis=1, keepdims=True)

    n_own = pick(own_all, 64 + turn)
    n_near = pick(near_all, 64 + turn)
    l_near = pick(near_all, 80 + turn)

    def sixth(value):
        return (jnp.maximum(value, 0) * 43) >> 8

    give = jnp.maximum(jnp.minimum(jnp.minimum(sixth(live_count - l_near), n_own), MOST - n_near), 0)
    take = jnp.maximum(jnp.minimum(jnp.minimum(sixth(l_near - live_count), n_near), MOST - n_own), 0)
    kept = n_own - give
    near_kept = n_near - take
    own_code = pick(own_all, turn * 8 + u) - 1
    near_code = pick(near_all, turn * 8 + u) - 1
    taken_code = pick(near_all, turn * 8 + near_kept + u - kept) - 1
    given_code = pick(own_all, turn * 8 + kept + u - near_kept) - 1
    live = (u < kept + take) & (turn < REACH)
    image = jnp.where(u < kept, own_code >> 3, taken_code & 7)
    swap = jnp.where(u < kept, 0, 1)
    asked = (u < near_kept + give) & (turn < REACH)
    sends = jnp.where(u < near_kept, near_code & 7, given_code >> 3)
    eye64 = lax.broadcasted_iota(I32, (slots, slots), 0) == lax.broadcasted_iota(I32, (slots, slots), 1)
    live_row = jnp.sum(jnp.where(eye64, jnp.where(live, 1, 0), 0), axis=0, keepdims=True)
    short = lax.broadcasted_iota(I32, (slots, slots), 1)
    place = jnp.sum(jnp.where(short < slot, live_row, 0), axis=1, keepdims=True)
    count = jnp.sum(live_row, axis=1, keepdims=True)

    def put(lane, value):
        return jnp.sum(jnp.where(lanes == lane, value, 0), axis=0, keepdims=True)

    by_place = put(jnp.where(live, place, -1), 1 + slot + image * 256 + swap * 4096)
    by_slot = put(slot, jnp.where(asked, 1 + sends, 0))
    places_row = put(slot, jnp.where(live, place, 0))
    row = lax.broadcasted_iota(I32, (8, 128), 0)
    out = jnp.where(row == 0, by_place, jnp.where(row == 1, by_slot, jnp.where(row == 2, places_row, count)))
    return out


def own_mask(counts, visible, sub):
    image = lax.broadcasted_iota(I32, (OWN, ROWS), 0)
    found = jnp.zeros((OWN, ROWS), I32)
    for a in range(OWN):
        found = jnp.where(image == a, counts[a], found)
    spot = lax.broadcasted_iota(I32, (OWN, ROWS), 1) + sub * ROWS
    kept = jnp.where((spot < found) & (visible[...] > 0), 1.0, 0.0)
    return my_lanes(jnp.concatenate([kept] * SUBS, axis=1), sub)


def my_lanes(wide, sub):
    lane = lax.broadcasted_iota(I32, wide.shape, 1)
    return jnp.where((lane >= sub * ROWS) & (lane < sub * ROWS + ROWS), wide, 0.0)


def meet_kernel(
    pairs, pair_count, counts, visible_far, wa_far, wv_far, wo_far, wh_far, gain_far, wd_far,
    tab, waT, wvT, woT, whT, wdT, gcol, okeep, told, near, omask, visible, wa, wv, wo, wh, gain, wd,
    ssem, rsem, osem, orem, lsem,
):
    me, sub, others, peers = places()
    far = (visible_far, wa_far, wv_far, wo_far, wh_far, gain_far, wd_far)
    loads = [
        pltpu.make_async_copy(src, dst, lsem.at[i])
        for i, (src, dst) in enumerate(zip(far, (visible, wa, wv, wo, wh, gain, wd)))
    ]
    for load in loads:
        load.start()
    own, out = own_rows(pairs[...], pair_count[0], me, lax.axis_size("img"))
    told[...] = jnp.broadcast_to(out, (8, 128))
    for load in loads[:1]:
        load.wait()
    omask[0] = own_mask(counts, visible, sub)
    greet(others, peers)
    ocopies = []
    for d in range(1, SUBS):
        to = {"sub": peers[d - 1]}
        ocopies.append(send(omask.at[0], omask.at[d], osem.at[1, d - 1], orem.at[1, d - 1], to))
    copies = [send(told, near.at[t ^ 1], ssem.at[t], rsem.at[t ^ 1], {"img": others[t]}) for t in range(REACH)]
    for copy in copies + ocopies:
        copy.start()
    for load in loads[1:]:
        load.wait()
    prepare(wa, wv, wo, wh, gain, wd, waT, wvT, woT, whT, wdT, gcol)
    for copy in copies:
        copy.wait()
    row = lax.broadcasted_iota(I32, (8, 128), 0)
    table = jnp.zeros((8, 128), I32)
    for t in range(REACH):
        table = jnp.where(row == t, near[t], table)
    tab[...] = plan_rows(own, table, pair_count[0])
    for copy in ocopies:
        copy.wait()
    okeep[...] = omask[0] + omask[1] + omask[2] + omask[3]


def sent_image(tab, t, u):
    return tab[1, t * 8 + u]


def fetch_kernel(
    tab, desc, okeep, own, xj, jkeep, zst, zl0, zl1, zl2, zl3, zms, zml, yst, yl, yms, yml, lower,
    zsem, zrem, ysem, yrem, osem, orem,
):
    me, sub, others, peers = places()
    zland = (zl0, zl1, zl2, zl3)
    wide = my_lanes(okeep[...], sub)
    greet(others, peers)
    order = (4, 5, 2, 3, 0, 1)
    line = lax.broadcasted_iota(I32, (8, KEYS), 0)
    zmcopies = []
    for t in order:
        masks = jnp.zeros((8, KEYS), F32)
        for u in range(MOST):
            masks = jnp.where(line == u, row_of(wide, jnp.maximum(sent_image(tab, t, u) - 1, 0)), masks)
        zms[t] = masks
        zmcopies.append(
            send(zms.at[t], zml.at[t ^ 1], zsem.at[PARTS, t], zrem.at[PARTS, t ^ 1], {"img": others[t]})
        )
        zmcopies[-1].start()
    zcopies = []
    for c in range(PARTS):
        zcopies.append([])
        for t in order:
            for u in range(MOST):
                which = jnp.maximum(sent_image(tab, t, u) - 1, 0)
                zst[c, t, u] = desc[which, c * PART : c * PART + PART, :]
            copy = send(zst.at[c, t], zland[c].at[t ^ 1], zsem.at[c, t], zrem.at[c, t ^ 1], {"img": others[t]})
            copy.start()
            zcopies[c].append(copy)
    ocopies = []
    for d in range(1, SUBS):
        copy = send(desc, lower.at[sub], osem.at[d - 1], orem.at[d - 1], {"sub": peers[d - 1]})
        copy.start()
        ocopies.append(copy)
    lower[sub] = desc[...]
    for copy in zmcopies:
        copy.wait()
    zmasks = jnp.concatenate([zml[t] for t in range(REACH)], axis=0)
    slots = []
    for d in range(SUBS):
        worker = sub if d == 0 else peers[d - 1]
        slots.append([jnp.maximum((tab[0, q * SUBS + worker] & 255) - 1, 0) for q in range(JOBS)])
        masks = jnp.zeros((JOBS, KEYS), F32)
        for q in range(JOBS):
            masks = jnp.where(line == q, row_of(zmasks, slots[d][q]), masks)
        yms[d] = masks
    ycopies = []
    for d in range(1, SUBS):
        to = {"sub": peers[d - 1]}
        ycopies.append(send(yms.at[d], yml.at[d - 1], ysem.at[PARTS, d - 1], yrem.at[PARTS, d - 1], to))
        ycopies[-1].start()
    for c in range(PARTS):
        for copy in zcopies[c]:
            copy.wait()
        for d in range(1, SUBS):
            for q in range(JOBS):
                yst[c, d - 1, q] = zland[c][slots[d][q] >> 3, slots[d][q] & 7]
            copy = send(yst.at[c, d - 1], yl.at[c, sub], ysem.at[c, d - 1], yrem.at[c, d - 1], {"sub": peers[d - 1]})
            copy.start()
            ycopies.append(copy)
        for q in range(JOBS):
            yl[c, sub, q] = zland[c][slots[0][q] >> 3, slots[0][q] & 7]
    for copy in ocopies:
        copy.wait()
    for s in range(SUBS):
        own[:, s * ROWS : s * ROWS + ROWS, :] = lower[s]
    for copy in ycopies:
        copy.wait()
    for s in range(SUBS):
        for c in range(PARTS):
            at = s * ROWS + c * PART
            xj[:, at : at + PART, :] = yl[c, s]
    jkeep[...] = yms[0] + yml[0] + yml[1] + yml[2]


def work_kernel(
    tab, own, xj, okeep, jkeep, bucket, wa, wm, waT, wvT, woT, whT, wdT, gcol, dmine, dother, mm, mo, ident, sc
):
    sub = lax.axis_index("sub")
    ident[...] = eye(256)
    w = dict(wa=wa, wm=wm, waT=waT, wvT=wvT, woT=woT, whT=whT, wdT=wdT, gcol=gcol, ident=ident)
    n = ((tab[3, 0] + (SUBS - 1) - sub) >> 2) - FIXED
    binv = bucket[...] * LOG2E

    def late(ps):
        outs = do_scores([FIXED + p for p in ps], tab, sub, own, xj, okeep, jkeep, w)
        for p, out in zip(ps, outs):
            dmine[p], dother[p], sc[p] = out
        outs = do_masses([FIXED + p for p in ps], [(sc, p) for p in ps], tab, sub, okeep, jkeep, binv, ident[...])
        for p, (a, b) in zip(ps, outs):
            mm[p] = jnp.broadcast_to(a, (8, KEYS))
            mo[p] = jnp.broadcast_to(b, (8, KEYS))

    @pl.loop(0, n >> 1)
    def _(p):
        late([2 * p, 2 * p + 1])

    @pl.when((n & 1) == 1)
    def _():
        late([n - 1])


def give_kernel(
    tab, own, xj, okeep, jkeep, bucket, wa, wm, waT, wvT, woT, whT, wdT, gcol, dmine2, dother2, mm2, mo2,
    zret, zmr, gm, mparts, mgot, ident, dmine, dother, sc, yb0, yb1, yb2, yb3, ymst, yml, zst, zms,
    ysem, yrem, zsem, zrem, osem, orem,
):
    me, sub, others, peers = places()
    yb = (yb0, yb1, yb2, yb3)
    ident[...] = eye(256)
    w = dict(wa=wa, wm=wm, waT=waT, wvT=wvT, woT=woT, whT=whT, wdT=wdT, gcol=gcol, ident=ident)
    binv = bucket[...] * LOG2E
    mline = lax.broadcasted_iota(I32, (JOBS, KEYS), 0)
    order = (4, 5, 2, 3, 0, 1)

    def rows_of(p, c):
        return pl.ds(pl.multiple_of(p * ROWS + c * PART, PART), PART)

    def block_of(p):
        return pl.ds(pl.multiple_of(p * ROWS, ROWS), ROWS)

    greet(others, peers)
    ycopies = [[] for _ in range(PARTS)]
    ocopies = []

    def hand_back(group, theirs, at, to):
        for c in range(PARTS):
            for d in range(1, SUBS):
                p = peers[d - 1]
                copy = send(
                    theirs.at[at, rows_of(p, c), :], yb[c].at[sub, to], ysem.at[group, c, d - 1], yrem.at[group, c, d - 1], {"sub": p}
                )
                copy.start()
                ycopies[c].append(copy)
        for c in range(PARTS):
            yb[c][sub, to] = theirs[at, rows_of(sub, c), :]

    def hand_mine(group, mine, at, to):
        for d in range(1, SUBS):
            p = peers[d - 1]
            copy = send(mine.at[at, block_of(p), :], gm.at[sub, to], osem.at[group, d - 1], orem.at[group, d - 1], {"sub": p})
            copy.start()
            ocopies.append(copy)
        gm[sub, to] = mine[at, block_of(sub), :]

    hand_back(2, dother2, slice(0, JOBS - FIXED), slice(FIXED, JOBS))
    for group in range(2):
        at = slice(2 * group, 2 * group + 2)
        outs = do_scores([2 * group, 2 * group + 1], tab, sub, own, xj, okeep, jkeep, w)
        for q, out in enumerate(outs, 2 * group):
            dmine[q], dother[q], sc[q] = out
        hand_back(group, dother, at, at)
    n = (tab[3, 0] + (SUBS - 1) - sub) >> 2
    owners = [jnp.where(q < n, job_of(tab, q, sub)[0], -1) for q in range(JOBS)]
    places_of = [[tab[2, t * 8 + u] for u in range(MOST)] for t in range(REACH)]
    zcopies = [[] for _ in range(PARTS)]

    def pass_on(c):
        for copy in ycopies[c]:
            copy.wait()
        for t in order:
            for u in range(MOST):
                zst[c, t, u] = yb[c][places_of[t][u] & 3, places_of[t][u] >> 2]
            copy = send(zst.at[c, t], zret.at[c, t ^ 1], zsem.at[c, t], zrem.at[c, t ^ 1], {"img": others[t]})
            copy.start()
            zcopies[c].append(copy)

    def some_masses(qs):
        return do_masses(qs, [(sc, q) for q in qs], tab, sub, okeep, jkeep, binv, ident[...])

    for c in range(PARTS):
        pass_on(c)
    hand_mine(2, dmine2, slice(0, JOBS - FIXED), slice(FIXED, JOBS))
    for group in range(2):
        at = slice(2 * group, 2 * group + 2)
        hand_mine(group, dmine, at, at)
    masses = some_masses([0, 1])
    masses += some_masses([2, 3])
    mine = [masses[q][0] if q < FIXED else mm2[q - FIXED, 0:1, :] for q in range(JOBS)]
    away = [masses[q][1] if q < FIXED else mo2[q - FIXED, 0:1, :] for q in range(JOBS)]
    table = jnp.zeros((JOBS, KEYS), F32)
    for q in range(JOBS):
        table = jnp.where(mline == q, away[q], table)
    ymst[...] = table
    yml[sub] = table
    ymcopies = []
    for d in range(1, SUBS):
        to = {"sub": peers[d - 1]}
        ymcopies.append(send(ymst, yml.at[sub], ysem.at[3, 0, d - 1], yrem.at[3, 0, d - 1], to))
        ymcopies[-1].start()
    table = jnp.zeros((OWN, KEYS), F32)
    for a in range(OWN):
        for q in range(JOBS):
            table = table + jnp.where((mline == a) & (owners[q] == a), mine[q], 0.0)
    mparts[...] = table
    for d in range(1, SUBS):
        copy = send(mparts, mgot.at[d - 1], osem.at[3, d - 1], orem.at[3, d - 1], {"sub": peers[d - 1]})
        copy.start()
        ocopies.append(copy)
    for copy in ymcopies:
        copy.wait()
    ymasses = jnp.concatenate([yml[s] for s in range(SUBS)], axis=0)
    zmcopies = []
    for t in order:
        back = jnp.zeros((8, KEYS), F32)
        for u in range(MOST):
            place = places_of[t][u]
            back = jnp.where(mline == u, row_of(ymasses, (place & 3) * JOBS + (place >> 2)), back)
        zms[t] = back
        to = {"img": others[t]}
        zmcopies.append(send(zms.at[t], zmr.at[t ^ 1], zsem.at[PARTS, t], zrem.at[PARTS, t ^ 1], to))
        zmcopies[-1].start()
    for copy in ocopies + zmcopies:
        copy.wait()
    for c in range(PARTS):
        for copy in zcopies[c]:
            copy.wait()


def sum_kernel(tab, zret, zmr, gm, mparts, mgot, upd, mass, acc, macc):
    sub = lax.axis_index("sub")
    acc[...] = jnp.zeros_like(acc)

    @pl.loop(0, SUBS * JOBS)
    def _(g):
        code = tab[0, g]

        @pl.when(code > 0)
        def _():
            which = (code >> 8) & 7
            acc[which] = acc[which] + gm[g & 3, g >> 2].astype(F32)

    macc[...] = mparts[...] + mgot[0] + mgot[1] + mgot[2]
    line = lax.broadcasted_iota(I32, (8, KEYS), 0)

    @pl.loop(0, REACH)
    def _(t):
        for u in range(MOST):
            which = tab[1, t * 8 + u] - 1

            @pl.when(which >= 0)
            def _():
                for c in range(PARTS):
                    rows = slice(c * PART, c * PART + PART)
                    acc[which, rows] = acc[which, rows] + zret[c, t, u].astype(F32)
                macc[...] = macc[...] + jnp.where(line == which, zmr[t, u : u + 1, :], 0.0)

    upd[...] = acc[...].astype(BF)
    total = macc[...]
    out = jnp.zeros((OWN, ROWS), F32)
    for s in range(SUBS):
        out = jnp.where(sub == s, total[:, s * ROWS : s * ROWS + ROWS], out)
    mass[...] = out


VM = pl.BlockSpec(memory_space=pltpu.VMEM)
SM = pl.BlockSpec(memory_space=pltpu.SMEM)
DMA = pltpu.SemaphoreType.DMA
HB = pl.BlockSpec(memory_space=pltpu.HBM)


def shape(dims, kind=BF):
    return jax.ShapeDtypeStruct(dims, kind)


def talk(number, limit=LIMIT):
    return pltpu.CompilerParams(collective_id=number, has_side_effects=True, vmem_limit_bytes=limit)


COST = pl.CostEstimate(flops=10**10, bytes_accessed=5 * 10**7, transcendentals=10**7)


def local(descriptors, counts, visible, pair_list, pair_count, w_attend, w_value, w_output, w_hidden, norm_gain, w_down, w_match, unassigned_bucket):
    V = pltpu.VMEM
    peer = (SUBS - 1,)
    tab, *ready, okeep = pl.pallas_call(
        meet_kernel,
        out_shape=(
            shape((8, 128), I32), *[shape((256, 256))] * 3, shape((512, 512)), shape((256, 512)), shape((512, 128), F32),
            shape((OWN, KEYS), F32),
        ),
        in_specs=[VM, SM, SM] + [HB] * 7,
        out_specs=(VM,) * 8,
        scratch_shapes=[
            V((8, 128), I32), V((REACH, 8, 128), I32), V((SUBS, OWN, KEYS), F32),
            V((OWN, ROWS), I32), *[V((256, 256), BF)] * 3, V((512, 512), BF), V((1, 512), F32), V((512, 256), BF),
            DMA((REACH,)), DMA((REACH,)), DMA((2, SUBS - 1)), DMA((2, SUBS - 1)), DMA((7,)),
        ],
        compiler_params=talk(0, 56 * 2**20),
        cost_estimate=COST,
    )(pair_list.T, pair_count, counts, visible, w_attend, w_value, w_output, w_hidden, norm_gain.reshape(1, -1), w_down)
    own, xj, jkeep = pl.pallas_call(
        fetch_kernel,
        out_shape=(shape((OWN, KEYS, D)), shape((JOBS, KEYS, D)), shape((JOBS, KEYS), F32)),
        in_specs=[SM, VM, VM],
        out_specs=(VM,) * 3,
        scratch_shapes=[
            V((PARTS, REACH, MOST, PART, D), BF), *[V((REACH, MOST, PART, D), BF)] * PARTS, V((REACH, 8, KEYS), F32), V((REACH, 8, KEYS), F32),
            V((PARTS, SUBS - 1, JOBS, PART, D), BF), V((PARTS, SUBS, JOBS, PART, D), BF), V((SUBS, JOBS, KEYS), F32), V((SUBS - 1, JOBS, KEYS), F32),
            V((SUBS, OWN, ROWS, D), BF),
            DMA((PARTS + 1, REACH)), DMA((PARTS + 1, REACH)), DMA((PARTS + 1, SUBS - 1)), DMA((PARTS + 1, SUBS - 1)), DMA(peer), DMA(peer),
        ],
        compiler_params=talk(1),
        cost_estimate=COST,
    )(tab, descriptors, okeep)
    bucket = unassigned_bucket.reshape(1, 1)
    late = JOBS - FIXED
    common = (tab, own, xj, okeep, jkeep, bucket, w_attend, w_match, *ready)
    rest = pl.pallas_call(
        work_kernel,
        out_shape=(shape((late, KEYS, D)), shape((late, KEYS, D)), shape((late, 8, KEYS), F32), shape((late, 8, KEYS), F32)),
        in_specs=[SM] + [VM] * 13,
        out_specs=(VM,) * 4,
        scratch_shapes=[V((256, 256), BF), V((late, KEYS, KEYS), F32)],
        compiler_params=pltpu.CompilerParams(vmem_limit_bytes=LIMIT),
    )(*common)
    back = pl.pallas_call(
        give_kernel,
        out_shape=(
            shape((PARTS, REACH, MOST, PART, D)), shape((REACH, 8, KEYS), F32), shape((SUBS, JOBS, ROWS, D)),
            shape((OWN, KEYS), F32), shape((SUBS - 1, OWN, KEYS), F32),
        ),
        in_specs=[SM] + [VM] * 17,
        out_specs=(VM,) * 5,
        scratch_shapes=[
            V((256, 256), BF), V((FIXED, KEYS, D), BF), V((FIXED, KEYS, D), BF), V((FIXED, KEYS, KEYS), F32),
            *[V((SUBS, JOBS, PART, D), BF)] * PARTS, V((JOBS, KEYS), F32), V((SUBS, JOBS, KEYS), F32),
            V((PARTS, REACH, MOST, PART, D), BF), V((REACH, 8, KEYS), F32),
            DMA((4, PARTS, SUBS - 1)), DMA((4, PARTS, SUBS - 1)), DMA((PARTS + 1, REACH)), DMA((PARTS + 1, REACH)), DMA((4, SUBS - 1)), DMA((4, SUBS - 1)),
        ],
        compiler_params=talk(2),
        cost_estimate=COST,
    )(*common, *rest)
    return pl.pallas_call(
        sum_kernel,
        out_shape=(shape((OWN, ROWS, D)), shape((OWN, ROWS), F32)),
        in_specs=[SM] + [VM] * 5,
        out_specs=(VM, VM),
        scratch_shapes=[V((OWN, ROWS, D), F32), V((OWN, KEYS), F32)],
        compiler_params=pltpu.CompilerParams(vmem_limit_bytes=LIMIT),
    )(tab, *back)


def solution(mesh):
    placed = (P("img", "sub", None), P("img"), P("img", "sub"), P("img", None), P("img")) + (P(),) * 8
    return jax.shard_map(
        local, mesh=mesh, in_specs=placed, out_specs=(P("img", "sub", None), P("img", "sub")), check_vma=False
    )
```
